32 devices in a mesh: dp: 8 (over y, x, core), band: 4 (over z).
Axes of the slice: x: 2, y: 2, z: 4, core: 2. Of those that a mesh axis runs over, the one named last changes fastest.
Arguments:
- images: float32 [12, 16, 16, 2048], P(None, 'band', None, 'dp'), may hold values from -0.5 to 0.46875
- noise: float32 [12, 16, 16, 2048], P(None, 'band', None, 'dp'), may hold values from 0 to 0.03125
- labels: int32 [2048], P('dp'), may hold values from 0 to 9, as said below
- conv_in: float32 [9, 512, 6], replicated, may hold values from -0.875 to 0.875
- mixer: float32 [512, 512], replicated, may hold values from -0.25 to 0.25
- conv_out: float32 [9, 12, 512], replicated, may hold values from -0.09375 to 0.09375
- prior_conv: float32 [9, 48, 24], replicated, may hold values from -0.21875 to 0.21875
- hidden_bias: float32 [2, 512], replicated, may hold values from -1 to 1
- step_gains: float32 [3, 12], replicated, may hold values from -0.5 to 0.8
- lu_parts: float32 [12, 12], replicated, may hold values from -0.9 to 0.9
- class_table: float32 [10, 96], replicated, may hold values from -1.2 to 1.2
- first_conv_in: float32 [9, 512, 6], replicated, may hold values from -7.357695e-06 to 7.357695e-06
- first_mixer: float32 [512, 512], replicated, may hold values from -7.357695e-06 to 7.357695e-06
- first_conv_out: float32 [9, 12, 512], replicated, may hold values from -7.357695e-06 to 7.357695e-06
- first_prior: float32 [9, 48, 24], replicated, may hold values from -7.357695e-06 to 7.357695e-06
- first_hidden_bias: float32 [2, 512], replicated, may hold values from -2.1738644e-05 to 2.1738644e-05
- first_gains: float32 [3, 12], replicated, may hold values from -2.1738644e-05 to 2.1738644e-05
- first_lu: float32 [12, 12], replicated, may hold values from -2.1738644e-05 to 2.1738644e-05
- first_table: float32 [10, 96], replicated, may hold values from -2.1738644e-05 to 2.1738644e-05
- second_conv_in: float32 [9, 512, 6], replicated, may hold values from 1.3981321e-13 to 2.2370114e-12
- second_mixer: float32 [512, 512], replicated, may hold values from 1.3981321e-13 to 2.2370114e-12
- second_conv_out: float32 [9, 12, 512], replicated, may hold values from 1.3981321e-13 to 2.2370114e-12
- second_prior: float32 [9, 48, 24], replicated, may hold values from 1.3981321e-13 to 2.2370114e-12
- second_hidden_bias: float32 [2, 512], replicated, may hold values from 1.2583189e-12 to 2.0133102e-11
- second_gains: float32 [3, 12], replicated, may hold values from 1.2583189e-12 to 2.0133102e-11
- second_lu: float32 [12, 12], replicated, may hold values from 1.2583189e-12 to 2.0133102e-11
- second_table: float32 [10, 96], replicated, may hold values from 1.2583189e-12 to 2.0133102e-11
Outputs:
- loss: float32 [], replicated
- grad_norm: float32 [], replicated
- new_conv_in: float32 [9, 512, 6], replicated
- new_mixer: float32 [512, 512], replicated
- new_conv_out: float32 [9, 12, 512], replicated
- new_prior: float32 [9, 48, 24], replicated
- new_hidden_bias: float32 [2, 512], replicated
- new_gains: float32 [3, 12], replicated
- new_lu: float32 [12, 12], replicated
- new_table: float32 [10, 96], replicated
- new_first_conv_in: float32 [9, 512, 6], replicated
- new_first_mixer: float32 [512, 512], replicated
- new_first_conv_out: float32 [9, 12, 512], replicated
- new_first_prior: float32 [9, 48, 24], replicated
- new_first_hidden_bias: float32 [2, 512], replicated
- new_first_gains: float32 [3, 12], replicated
- new_first_lu: float32 [12, 12], replicated
- new_first_table: float32 [10, 96], replicated
- new_second_conv_in: float32 [9, 512, 6], replicated
- new_second_mixer: float32 [512, 512], replicated
- new_second_conv_out: float32 [9, 12, 512], replicated
- new_second_prior: float32 [9, 48, 24], replicated
- new_second_hidden_bias: float32 [2, 512], replicated
- new_second_gains: float32 [3, 12], replicated
- new_second_lu: float32 [12, 12], replicated
- new_second_table: float32 [10, 96], replicated
The draws below stay inside these ranges and needn't reach their ends.
Inputs may be any that keep to these rules, and one draw needn't show every extreme that they name: `labels`: one class, drawn from the seed, has no image at all; the first image has class 0 and the last class 10 - 1.
All inputs are finite; a program needn't handle non-finite values.
Results may differ from the reference program's by a relative error of at most 0.003.
Values may be sent and summed in bfloat16 or wider, within the bound.
No kernel may reach another device: no remote copies, remote signals or barrier semaphores. Data moves between devices by JAX's collectives and lax.ppermute only.
A program may use at most 320 MiB of HBM per device.

```python
import math
import jax
import jax.numpy as jnp
from jax import lax

HID = 512
STEP = 10
CLASSES = 10
IMAGES = 2048


def draw_labels(key, part):
    key = jax.random.fold_in(key, 7)
    order_key, empty_key, pick_key = jax.random.split(key, 3)
    order = jax.random.permutation(order_key, CLASSES)
    ranks = jnp.zeros((CLASSES,), jnp.int32).at[order].set(jnp.arange(CLASSES, dtype=jnp.int32))
    weights = 2520 // (ranks + 1)
    empty = jax.random.randint(empty_key, (), 1, CLASSES - 1, dtype=jnp.int32)
    weights = jnp.where(jnp.arange(CLASSES, dtype=jnp.int32) == empty, 0, weights)
    bounds = jnp.cumsum(weights)
    picks = jax.random.randint(pick_key, (IMAGES,), 0, 1, dtype=jnp.int32) + jax.random.randint(pick_key, (IMAGES,), 0, 2 ** 30, dtype=jnp.int32) % bounds[-1]
    labels = jnp.sum((picks[:, None] >= bounds[None, :]).astype(jnp.int32), axis=1)
    labels = labels.at[0].set(0)
    labels = labels.at[IMAGES - 1].set(CLASSES - 1)
    return labels.astype(jnp.int32)


def block_scale(stream_key, extent, pieces, smallest, top_value):
    def one(dim, blocks):
        steps = jax.random.uniform(jax.random.fold_in(jax.random.fold_in(stream_key, 6), dim), (blocks,), jnp.float32, smallest / len(pieces), top_value / len(pieces))
        return jnp.repeat(jnp.exp(steps), extent[dim] // blocks).reshape((-1,) + (1,) * (len(extent) - dim - 1))

    loudness = one(*pieces[0])
    for cut in pieces[1:]:
        loudness = loudness * one(*cut)
    return loudness


def gaussian(rng, shape, deviation, bound, held_as=jnp.bfloat16):
    result = deviation * jax.random.normal(rng, shape, jnp.float32)
    return jnp.clip(result, min=-bound, max=bound).astype(held_as)


def setup_inputs(seed: int = 0) -> dict:
    seeds = jax.random.split(jax.random.key(seed), 28)
    return {
        "images": jnp.clip(-0.5 + 0.96875 * jax.random.uniform(seeds[0], (12, 16, 16, IMAGES), jnp.float32) ** block_scale(seeds[0], (12, 16, 16, IMAGES), ((1, 4), (3, 8)), -0.2, 0.2), -0.5, 0.46875),
        "noise": jnp.clip(0.03125 * jax.random.uniform(seeds[1], (12, 16, 16, IMAGES), jnp.float32) ** block_scale(seeds[1], (12, 16, 16, IMAGES), ((1, 4), (3, 8)), -0.2, 0.2), 0.0, 0.03125),
        "labels": draw_labels(jax.random.fold_in(seeds[27], 71), 0),
        "conv_in": gaussian(seeds[3], (9, HID, 6), 54 ** -0.5, 0.875, jnp.float32),
        "mixer": gaussian(seeds[4], (HID, HID), HID ** -0.5, 0.25, jnp.float32),
        "conv_out": gaussian(seeds[5], (9, 12, HID), (9 * HID) ** -0.5, 0.09375, jnp.float32),
        "prior_conv": gaussian(seeds[6], (9, 48, 24), 864 ** -0.5, 0.21875, jnp.float32),
        "hidden_bias": gaussian(seeds[7], (2, HID), 0.2, 1.0, jnp.float32),
        "step_gains": jnp.clip(jax.random.uniform(seeds[8], (3, 12), jnp.float32, -0.5, 0.8), -0.5, 0.8),
        "lu_parts": gaussian(seeds[9], (12, 12), 0.15, 0.9, jnp.float32),
        "class_table": gaussian(seeds[10], (CLASSES, 96), 0.3, 1.2, jnp.float32),
        "first_conv_in": gaussian(seeds[11], (9, HID, 6), (0.0011 * (164 * HID + HID * HID + 11508) ** -0.5), 7.357694812526461e-06, jnp.float32),
        "first_mixer": gaussian(seeds[12], (HID, HID), (0.0011 * (164 * HID + HID * HID + 11508) ** -0.5), 7.357694812526461e-06, jnp.float32),
        "first_conv_out": gaussian(seeds[13], (9, 12, HID), (0.0011 * (164 * HID + HID * HID + 11508) ** -0.5), 7.357694812526461e-06, jnp.float32),
        "first_prior": gaussian(seeds[14], (9, 48, 24), (0.0011 * (164 * HID + HID * HID + 11508) ** -0.5), 7.357694812526461e-06, jnp.float32),
        "first_hidden_bias": gaussian(seeds[15], (2, HID), (0.0033 * (164 * HID + HID * HID + 11508) ** -0.5), 2.173864413634874e-05, jnp.float32),
        "first_gains": gaussian(seeds[16], (3, 12), (0.0033 * (164 * HID + HID * HID + 11508) ** -0.5), 2.173864413634874e-05, jnp.float32),
        "first_lu": gaussian(seeds[17], (12, 12), (0.0033 * (164 * HID + HID * HID + 11508) ** -0.5), 2.173864413634874e-05, jnp.float32),
        "first_table": gaussian(seeds[18], (CLASSES, 96), (0.0033 * (164 * HID + HID * HID + 11508) ** -0.5), 2.173864413634874e-05, jnp.float32),
        "second_conv_in": jnp.clip(jnp.exp(jax.random.uniform(seeds[19], (9, HID, 6), jnp.float32, math.log(1.398132098377053e-13), math.log(2.2370113574032846e-12))), 1.398132098377053e-13, 2.2370113574032846e-12),
        "second_mixer": jnp.clip(jnp.exp(jax.random.uniform(seeds[20], (HID, HID), jnp.float32, math.log(1.398132098377053e-13), math.log(2.2370113574032846e-12))), 1.398132098377053e-13, 2.2370113574032846e-12),
        "second_conv_out": jnp.clip(jnp.exp(jax.random.uniform(seeds[21], (9, 12, HID), jnp.float32, math.log(1.398132098377053e-13), math.log(2.2370113574032846e-12))), 1.398132098377053e-13, 2.2370113574032846e-12),
        "second_prior": jnp.clip(jnp.exp(jax.random.uniform(seeds[22], (9, 48, 24), jnp.float32, math.log(1.398132098377053e-13), math.log(2.2370113574032846e-12))), 1.398132098377053e-13, 2.2370113574032846e-12),
        "second_hidden_bias": jnp.clip(jnp.exp(jax.random.uniform(seeds[23], (2, HID), jnp.float32, math.log(1.2583188614342933e-12), math.log(2.0133101782948692e-11))), 1.2583188614342933e-12, 2.0133101782948692e-11),
        "second_gains": jnp.clip(jnp.exp(jax.random.uniform(seeds[24], (3, 12), jnp.float32, math.log(1.2583188614342933e-12), math.log(2.0133101782948692e-11))), 1.2583188614342933e-12, 2.0133101782948692e-11),
        "second_lu": jnp.clip(jnp.exp(jax.random.uniform(seeds[25], (12, 12), jnp.float32, math.log(1.2583188614342933e-12), math.log(2.0133101782948692e-11))), 1.2583188614342933e-12, 2.0133101782948692e-11),
        "second_table": jnp.clip(jnp.exp(jax.random.uniform(seeds[26], (CLASSES, 96), jnp.float32, math.log(1.2583188614342933e-12), math.log(2.0133101782948692e-11))), 1.2583188614342933e-12, 2.0133101782948692e-11),
    }


HIGH = lax.Precision.HIGHEST
LOG_TWO = math.log(2.0)
CLIP_NORM = 0.01
RATE = 0.05
BETA_ONE = 0.9
BETA_TWO = 0.999
EPSILON = 1e-08
DECAY = 0.01
BITS = 5.0

@jax.custom_vjp
def low(v):
    return lax.optimization_barrier(v.astype(jnp.bfloat16)).astype(jnp.float32)

@jax.custom_vjp
def low_back(v):
    return v

def low_keep(v):
    return (low(v), None)

def low_pass(kept, grad):
    return (grad,)

def back_keep(v):
    return (v, None)

def back_low(kept, grad):
    return (low(grad),)
low.defvjp(low_keep, low_pass)
low_back.defvjp(back_keep, back_low)

def conv(value, weight):
    kernel = weight.reshape(3, 3, weight.shape[1], weight.shape[2])
    return lax.conv_general_dilated(value, kernel, (1, 1), 'SAME', dimension_numbers=('CHWN', 'HWOI', 'CHWN'), precision=HIGH)

def lu_matrix(parts):
    eye = jnp.eye(parts.shape[0], dtype=parts.dtype)
    lower = jnp.tril(parts, -1) + eye
    upper = jnp.triu(parts, 1) + jnp.diag(jnp.exp(jnp.diagonal(parts)))
    return jnp.dot(lower, upper, precision=HIGH)[::-1]

def gauss(value, mean, logs):
    return -0.5 * (math.log(2.0 * math.pi) + 2.0 * logs + (value - mean) ** 2 * jnp.exp(-2.0 * logs))

def squeeze(field):
    chans, rows, cols, count = field.shape
    split = field.reshape(chans, rows // 2, 2, cols // 2, 2, count)
    return split.transpose(0, 2, 4, 1, 3, 5).reshape(chans * 4, rows // 2, cols // 2, count)

def column(vector):
    return vector[:, None, None, None]

def flow_loss(params, field, coef, onehot):
    conv_in, mixer, conv_out, prior_conv, hidden_bias, step_gains, lu_parts, class_table = params
    shifted = (field + column(step_gains[0])) * column(jnp.exp(step_gains[1]))
    mixed = jnp.einsum('oc,chwb->ohwb', lu_matrix(lu_parts), shifted, precision=HIGH)
    active, passive = (mixed[:6], mixed[6:])
    pre_one = low_back(conv(low(active), low(conv_in)) + column(hidden_bias[0]))
    act_one = low(jax.nn.silu(pre_one))
    pre_two = low_back(jnp.einsum('oi,ihwb->ohwb', low(mixer), act_one, precision=HIGH) + column(hidden_bias[1]))
    act_two = low(jax.nn.silu(pre_two))
    network = low_back(conv(act_two, low(conv_out)) + column(step_gains[2]))
    raw = network[6:] + 2.0
    moved = (passive + network[:6]) * jax.nn.sigmoid(raw)
    squeezed = squeeze(jnp.concatenate([active, moved], axis=0))
    first, second = (squeezed[:24], squeezed[24:])
    cls = jnp.dot(onehot, class_table, precision=HIGH)
    stats = conv(first, prior_conv) + cls[:, :48].T[:, None, None, :]
    top = cls[:, 48:].T[:, None, None, :]
    logp = gauss(second, stats[:24], stats[24:]) + gauss(first, top[:24], top[24:])
    logp = lax.optimization_barrier(jnp.sum(logp, axis=(0, 1, 2)))
    area = field.shape[1] * field.shape[2]
    logdet = area * (jnp.sum(step_gains[1]) + jnp.sum(jnp.diagonal(lu_parts)))
    logdet = logdet + lax.optimization_barrier(jnp.sum(jax.nn.log_sigmoid(raw), axis=(0, 1, 2)))
    return jnp.sum(coef * -(logdet + logp))

def adamw(weight, first, second, grad):
    first_new = BETA_ONE * first + (1.0 - BETA_ONE) * grad
    second_new = BETA_TWO * second + (1.0 - BETA_TWO) * grad * grad
    first_hat = first_new / (1.0 - BETA_ONE ** STEP)
    second_hat = second_new / (1.0 - BETA_TWO ** STEP)
    return (weight - RATE * (first_hat / (jnp.sqrt(second_hat) + EPSILON) + DECAY * weight), first_new, second_new)

def reference(images, noise, labels, conv_in, mixer, conv_out, prior_conv, hidden_bias, step_gains, lu_parts, class_table, first_conv_in, first_mixer, first_conv_out, first_prior, first_hidden_bias, first_gains, first_lu, first_table, second_conv_in, second_mixer, second_conv_out, second_prior, second_hidden_bias, second_gains, second_lu, second_table):
    field = images + noise
    classes = class_table.shape[0]
    onehot = (labels[:, None] == jnp.arange(classes, dtype=jnp.int32)[None, :]).astype(images.dtype)
    counts = lax.optimization_barrier(jnp.sum(onehot, axis=0))
    present = jnp.maximum(counts, 1.0)
    dims = field.shape[0] * field.shape[1] * field.shape[2]
    coef = lax.optimization_barrier(jnp.sum(onehot / (classes * present * dims * LOG_TWO)[None, :], axis=1))
    total = field.shape[3]
    block = math.gcd(total, 128)
    number = total // block
    blocks = field.reshape(field.shape[:3] + (number, block)).transpose(3, 0, 1, 2, 4)
    params = (conv_in, mixer, conv_out, prior_conv, hidden_bias, step_gains, lu_parts, class_table)

    def accumulate(carry, item):
        piece, piece_coef, piece_hot = item
        value, back = jax.vjp(lambda p: flow_loss(p, piece, piece_coef, piece_hot), params)
        grads = back(jnp.ones_like(value))[0]
        return ((carry[0] + value, jax.tree.map(jnp.add, carry[1], grads)), None)
    start = (jnp.zeros((), images.dtype), jax.tree.map(jnp.zeros_like, params))
    (loss_sum, grads), _ = lax.scan(accumulate, start, (blocks, coef.reshape(number, block), onehot.reshape(number, block, classes)))
    loss = loss_sum + jnp.sum(BITS * counts / present) / classes
    squares = sum((jnp.sum(grad * grad) for grad in grads))
    grad_norm = jnp.sqrt(squares)
    factor = jnp.minimum(1.0, CLIP_NORM / (grad_norm + 1e-06))
    firsts = (first_conv_in, first_mixer, first_conv_out, first_prior, first_hidden_bias, first_gains, first_lu, first_table)
    seconds = (second_conv_in, second_mixer, second_conv_out, second_prior, second_hidden_bias, second_gains, second_lu, second_table)
    results = [adamw(w, m, v, factor * g) for w, m, v, g in zip(params, firsts, seconds, grads)]
    return (loss, grad_norm) + tuple((r[0] for r in results)) + tuple((r[1] for r in results)) + tuple((r[2] for r in results))
```

```python
import functools
import math

import jax
import jax.numpy as jnp
from jax import lax
from jax.experimental import pallas as pl
from jax.experimental.pallas import tpu as pltpu
from jax.sharding import PartitionSpec as P

STEP = 10
HIGH = lax.Precision.HIGHEST
LOG_TWO = math.log(2.0)
LOG_TWO_PI = math.log(2.0 * math.pi)
CLIP_NORM = 0.01
RATE = 0.05
BETA_ONE = 0.9
BETA_TWO = 0.999
EPSILON = 1e-08
DECAY = 0.01
BITS = 5.0
F32 = jnp.float32
BF16 = jnp.bfloat16
MIB = 1024 * 1024
NN = (((1,), (0,)), ((), ()))
NT = (((1,), (1,)), ((), ()))
TN = (((0,), (0,)), ((), ()))

ROW_MIX = 0
ROW_OUT = 512
ROW_IN = ROW_OUT + 144
ROW_PRIOR = ROW_IN + 96
ROW_SMALL = ROW_PRIOR + 72
ROWS = ROW_SMALL + 24


def dot(left, right, dims=NN, precision=None):
    return lax.dot_general(left, right, dims, precision=precision, preferred_element_type=F32)


def iota(shape, dim):
    return lax.broadcasted_iota(jnp.int32, shape, dim)


def as_f32(mask):
    return jnp.where(mask, 1.0, 0.0).astype(F32)


def prior_out_map():
    row, col = iota((48, 64), 0), iota((48, 64), 1)
    kind, d, c = col >> 5, (col >> 3) & 3, col & 7
    return as_f32((c < 6) & (row == kind * 24 + 4 * c + d))


def prior_in_map():
    row, col = iota((288, 216), 0), iota((288, 216), 1)
    tap, d, c = row >> 5, (row >> 3) & 3, row & 7
    return as_f32((c < 6) & (col == tap * 24 + 4 * c + d))


def channel_map():
    row, col = iota((16, 128), 0), iota((16, 128), 1)
    return as_f32(((row < 6) & (col == 11 - row)) | ((row >= 8) & (row < 14) & (col == 13 - row)))


def half_map():
    row, col = iota((16, 128), 0), iota((16, 128), 1)
    return as_f32(((row < 6) & (col == row)) | ((row >= 8) & (row < 14) & (col == row - 2)))


def lu_factors(lu):
    row, col = iota((128, 128), 0), iota((128, 128), 1)
    eye = (row == col) & (row < 12)
    lower = jnp.where(row > col, lu, 0.0) + as_f32(eye)
    upper = jnp.where(row < col, lu, 0.0) + jnp.where(eye, jnp.exp(lu), 0.0)
    return lower, upper, eye


def spread_weight(lu, gains):
    lower, upper, _ = lu_factors(lu)
    weight = dot(channel_map(), dot(lower, upper, NN, HIGH), NN, HIGH)
    scaled = weight * jnp.exp(gains[1:2])
    shift = jnp.sum(scaled * gains[0:1], axis=1, keepdims=True)
    return jnp.where(iota((16, 128), 1) == 12, shift, scaled)


def weights_kernel(cin, mix, cout, prior, bias, gains, lu, table,
                   win, wt, mixh, mixth, bias2, wout, woutt, weff, wpt, wp, tablep,
                   big, square, strip):
    hidden = mix.shape[0]
    wt[...] = jnp.zeros_like(wt)
    for dy in range(3):
        for dx in range(3):
            wt[pl.ds(dy * 32 + dx * 8, 6), :] = (
                0.5 * cin[dy * 3 + dx]
            ).astype(BF16).astype(F32)
    half = 0.5 * bias[0:1, :]
    first = half.astype(BF16).astype(F32)
    rest = half - first
    second = rest.astype(BF16).astype(F32)
    wt[46:47, :] = first
    wt[38:39, :] = second
    wt[54:55, :] = rest - second
    win[...] = wt[...].T.astype(BF16)
    mixh[...] = (0.5 * mix[...]).astype(BF16)
    mixth[...] = (0.5 * mix[...]).T.astype(BF16)
    bias2[...] = jnp.broadcast_to(0.5 * bias[1:2, :], (128, hidden)).T
    big[...] = jnp.zeros_like(big)
    for tap in range(9):
        big[pl.ds(tap * 16, 6), :] = cout[tap, 0:6, :]
        big[pl.ds(tap * 16 + 8, 6), :] = cout[tap, 6:12, :]
    wout[...] = big[0:144, :].astype(BF16)
    woutt[...] = (0.5 * big[0:256, :]).T.astype(BF16)
    square[...] = jnp.zeros_like(square)
    square[0:12, 0:12] = lu[...]
    strip[...] = jnp.zeros_like(strip)
    strip[0:3, 0:12] = gains[...]
    weff[...] = spread_weight(square[...], strip[0:8, :])
    out_map = prior_out_map()
    flat = dot(prior_in_map(), dot(prior[...].reshape(216, 48), out_map, NN, HIGH), NN, HIGH)
    flat_hi = flat.astype(BF16)
    flat_lo = (flat - flat_hi.astype(F32)).astype(BF16)
    wpt[...] = jnp.zeros_like(wpt)
    wpt[:, 0:64] = flat_hi
    wpt[:, 64:128] = flat_lo
    wpt[:, 128:192] = flat_hi
    big[...] = jnp.zeros_like(big)
    big[0:288, 0:64] = flat_hi.astype(F32)
    big[0:288, 64:128] = flat_lo.astype(F32)
    wp[...] = big[0:384, 0:128].T.astype(BF16)
    tablep[...] = jnp.zeros_like(tablep)
    tablep[0:10, 0:64] = dot(table[:, 0:48], out_map, NN, HIGH)
    tablep[0:10, 64:128] = dot(table[:, 48:96], out_map, NN, HIGH)


def hidden_unit(u):
    wide = 1.0 + jnp.tanh(u)
    act = u * wide
    return act.astype(BF16), (wide + act * (2.0 - wide)).astype(BF16)


def forward_kernel(cols, sub, images, noise, top, bottom, flags, weff, win, mixh, bias2, wout,
                   act1, sg1, act2, sg2, xa2, xt, xaf, xbf, nn, edge_top, edge_bottom,
                   xs, taps, acc):
    step = pl.program_id(0)
    rows, width, count = images.shape[1:]
    groups = width // cols

    @pl.when(step == 0)
    def _():
        xs[:, 0:2] = top[...]
        xs[:, 2 : rows + 2] = images[...] + noise[...]
        xs[:, rows + 2 : rows + 4] = bottom[...]
        xaf[...] = jnp.zeros_like(xaf)
        xt[...] = jnp.zeros_like(xt)
        acc[...] = jnp.zeros_like(acc)
        row8 = iota((8, count), 0)
        ones = jnp.where((iota((16, count), 0) & 7) == 6, 1.0, 0.0)
        col_a = [jnp.broadcast_to(weff[0:8, c : c + 1], (8, count)) for c in range(13)]
        col_b = [jnp.broadcast_to(weff[8:16, c : c + 1], (8, count)) for c in range(13)]

        def per_row(er, carry):
            own = (er >= 2) & (er < rows + 2)
            valid = jnp.where(er < 2, flags[0], jnp.where(er >= rows + 2, flags[1], 1.0))
            inner = jnp.clip(er - 2, 0, rows - 1)
            for c in range(width):
                a, b = col_a[12], col_b[12]
                t0 = jnp.zeros((8, count), F32)
                t1 = jnp.where(row8 == 4, valid, 0.0)
                for ch in range(12):
                    x = jnp.broadcast_to(xs[ch, er, c : c + 1, :], (8, count))
                    a = a + col_a[ch] * x
                    b = b + col_b[ch] * x
                    if ch < 8:
                        t0 = jnp.where(row8 == ch, x, t0)
                    else:
                        t1 = jnp.where(row8 == ch - 8, x, t1)
                xaf[er, c + 2] = a * valid
                xt[er, c + 1] = jnp.concatenate([t0, t1], axis=0).astype(BF16)

                @pl.when(own)
                def _():
                    xbf[inner, c] = b

            for c in range(width + 2):
                pair = jnp.concatenate([xaf[er, c + 1], xaf[er, c + 2]], axis=0)
                xa2[er, c] = (pair + ones).astype(BF16)
            return carry

        lax.fori_loop(0, rows + 4, per_row, 0)

    row = step // groups
    start = (step % groups) * cols
    for i in range(cols):
        lanes = pl.ds(i * count, count)
        for dy in range(3):
            for j in range(2):
                taps[pl.ds((dy * 2 + j) * 16, 16), lanes] = xa2[row + 1 + dy, start + i + 2 * j]
        taps[96:112, lanes] = xt[row + 2, start + i + 1]
        taps[112:128, lanes] = xt[row + 2, start + i + 1]
    size = sub * count
    for s in range(cols // sub):
        lanes = pl.ds(s * size, size)
        one, slope1 = hidden_unit(dot(win[...], taps[:, lanes]))
        act1[0, :, lanes] = one
        sg1[0, :, lanes] = slope1
        bias = jnp.concatenate([bias2[...]] * (size // 128), axis=1)
        two, slope2 = hidden_unit(dot(mixh[...], one) + bias)
        act2[0, :, lanes] = two
        sg2[0, :, lanes] = slope2
        out = dot(wout[...], two)
        for i in range(sub):
            for dy in range(3):
                for dx in range(3):
                    r = row + 2 - dy
                    c = start + s * sub + i + 2 - dx
                    tap = dy * 3 + dx
                    acc[r, c] += out[tap * 16 : tap * 16 + 16, i * count : (i + 1) * count]

    @pl.when(step == rows * groups - 1)
    def _():
        nn[...] = acc[1 : rows + 1, 1 : width + 1]
        edge_top[...] = acc[0, 1 : width + 1].astype(BF16)
        edge_bottom[...] = acc[rows + 1, 1 : width + 1].astype(BF16)


def coupling_kernel(nn, edge_top, edge_bottom, xaf, xbf, xt, labels, counts, wp, wpt, tablep, weff_gains,
                    dn, dprior, small, taps_hi, taps_lo, stats, dstats, dtaps, dxa, dxb, total,
                    loss_acc, gain_acc, table_acc):
    rows, width, _, count = nn.shape
    half = width // 2
    classes = 10
    hot = as_f32(iota((16, count), 0) == jnp.broadcast_to(labels[...], (16, count)))
    present = jnp.maximum(counts[...], 1.0)
    dims = 12.0 * width * width
    scale16 = 1.0 / (classes * present * (dims * LOG_TWO))
    coef = jnp.sum(hot * scale16[:, 0:1], axis=0, keepdims=True)
    coef = jnp.broadcast_to(coef, (8, count))
    cls = dot(tablep[...], hot, TN, HIGH)
    dxa[...] = jnp.zeros_like(dxa)
    loss_acc[...] = jnp.zeros_like(loss_acc)
    gain_acc[...] = jnp.zeros_like(gain_acc)
    table_acc[...] = jnp.zeros_like(table_acc)
    dprior[...] = jnp.zeros_like(dprior)
    dstats[...] = jnp.zeros_like(dstats)
    keep = iota((8, count), 0) < 6
    net_bias = weff_gains[...]
    bias_a = jnp.broadcast_to(net_bias[0:8, 0:1], (8, count))
    bias_b = jnp.broadcast_to(net_bias[8:16, 0:1], (8, count))

    def per_row(r2, carry):
        for w in range(half):
            lanes = pl.ds(w * count, count)
            for ty in range(3):
                for tx in range(3):
                    for dy in range(2):
                        er, ec = 2 * r2 + 2 * ty + dy, 2 * w + 2 * tx
                        pair = jnp.concatenate([xaf[er, ec], xaf[er, ec + 1]], axis=0)
                        high = pair.astype(BF16)
                        at = pl.ds((ty * 3 + tx) * 32 + dy * 16, 16)
                        taps_hi[at, lanes] = high
                        taps_lo[at, lanes] = (pair - high.astype(F32)).astype(BF16)
        main = dot(wp[:, 0:288], taps_hi[...])
        stats[...] = main[0:64] + main[64:128] + dot(wp[0:64, 0:288], taps_lo[...])
        for w in range(half):
            lanes = pl.ds(w * count, count)
            for dy in range(2):
                for dx in range(2):
                    d = 2 * dy + dx
                    r, c = 2 * r2 + dy, 2 * w + dx
                    tile = nn[r, c]
                    shift = tile[0:8] + bias_a
                    raw = tile[8:16] + bias_b
                    sig = jax.nn.sigmoid(raw)
                    log_sig = jnp.minimum(raw, 0.0) - jnp.log(1.0 + jnp.exp(-jnp.abs(raw)))
                    base = xbf[r, c] + shift
                    second = base * sig
                    mean = stats[pl.ds(8 * d, 8), lanes] + cls[8 * d : 8 * d + 8]
                    logs = stats[pl.ds(32 + 8 * d, 8), lanes] + cls[32 + 8 * d : 40 + 8 * d]
                    diff = second - mean
                    weighted = diff * jnp.exp(-2.0 * logs)
                    quad = diff * weighted
                    first = xaf[r + 2, c + 2]
                    mean1 = cls[64 + 8 * d : 72 + 8 * d]
                    logs1 = cls[96 + 8 * d : 104 + 8 * d]
                    diff1 = first - mean1
                    weighted1 = diff1 * jnp.exp(-2.0 * logs1)
                    quad1 = diff1 * weighted1
                    value = log_sig - 0.5 * (
                        2.0 * LOG_TWO_PI + 2.0 * (logs + logs1) + quad + quad1
                    )
                    loss_acc[...] += jnp.where(keep, value, 0.0)
                    dv = coef * weighted
                    ds_ = coef - coef * quad
                    dv1 = coef * weighted1
                    table_acc[pl.ds(8 * d, 8), :] -= dv
                    table_acc[pl.ds(32 + 8 * d, 8), :] += ds_
                    table_acc[pl.ds(64 + 8 * d, 8), :] -= dv1
                    table_acc[pl.ds(96 + 8 * d, 8), :] += coef - coef * quad1
                    dstats[pl.ds(8 * d, 8), lanes] = -dv
                    dstats[pl.ds(32 + 8 * d, 8), lanes] = ds_
                    dxa[r + 2, c + 2] += dv1
                    passed = dv * sig
                    dxb[r, c] = passed
                    draw = (passed * base - coef) * (1.0 - sig)
                    net = jnp.concatenate([passed, draw], axis=0).astype(BF16)
                    dn[r, c] = net
                    gain_acc[...] += net.astype(F32)
        grads = dstats[0:64, :]
        high = grads.astype(BF16)
        low = (grads - high.astype(F32)).astype(BF16)
        dprior[:, 0:64] += (
            dot(taps_hi[...], high, NT) + dot(taps_hi[...], low, NT) + dot(taps_lo[...], high, NT)
        )
        stack = jnp.concatenate([high, high, low], axis=0)
        dtaps[...] = dot(wpt[:, 0:192], stack)
        for w in range(half):
            lanes = pl.ds(w * count, count)
            for ty in range(3):
                for tx in range(3):
                    for dy in range(2):
                        for dx in range(2):
                            k = (ty * 3 + tx) * 32 + dy * 16 + dx * 8
                            dxa[2 * r2 + 2 * ty + dy, 2 * w + 2 * tx + dx] += dtaps[pl.ds(k, 8), lanes]
        return carry

    lax.fori_loop(0, rows // 2, per_row, 0)

    total[...] = jnp.zeros_like(total)
    for er in range(rows + 4):
        field = xt[er, 1 : width + 1].reshape(width * 16, count)
        part_a = dxa[er, 2 : width + 2].reshape(width * 8, count)
        if 2 <= er < rows + 2:
            part_b = dxb[er - 2].reshape(width * 8, count)
            part = jnp.concatenate([part_a, part_b], axis=0)
        else:
            part = part_a
        size = part.shape[0]
        high = part.astype(BF16)
        low = (part - high.astype(F32)).astype(BF16)
        total[0:size, :] += dot(high, field, NT) + dot(low, field, NT)
    row, col = iota((256, 256), 0), iota((256, 256), 1)
    masked = jnp.where(((row & 127) >> 3) == (col >> 4), total[...], 0.0)
    gather = as_f32((iota((16, 256), 0) == ((iota((16, 256), 1) & 7) + 8 * (iota((16, 256), 1) >> 7))))
    fold = as_f32((iota((256, 128), 0) & 15) == iota((256, 128), 1))
    small[...] = jnp.zeros_like(small)
    small[8:24, 128:256] = dot(dot(gather, masked, NN, HIGH), fold, NN, HIGH)
    small[8:24, 0:128] = dot(hot, table_acc[...], NT, HIGH)
    lone = jnp.ones((8, count), F32)
    gain_row = dot(dot(lone, gain_acc[...], NT, HIGH), half_map(), NN, HIGH)
    small[8:16, 256:384] = gain_row
    value = jnp.sum(jnp.sum(loss_acc[...], axis=0, keepdims=True) * coef[0:1], axis=1, keepdims=True)
    small[16:24, 256:384] = jnp.broadcast_to(-value, (8, 128))


def backward_kernel(cols, sub, act1, sg1, act2, sg2, dn, dn_top, dn_bottom, xa2, xt, mixth, woutt, wt,
                    dprior, small, packed, dnp, taps, gtaps, bias_acc, wfield):
    step = pl.program_id(0)
    rows, width, _, count = dn.shape
    groups = width // cols

    @pl.when(step == 0)
    def _():
        packed[...] = jnp.zeros_like(packed)
        bias_acc[...] = jnp.zeros_like(bias_acc)
        wfield[...] = jnp.zeros_like(wfield)
        dnp[...] = jnp.zeros_like(dnp)
        dnp[0, 1 : width + 1] = dn_top[...]
        dnp[1 : rows + 1, 1 : width + 1] = dn[...]
        dnp[rows + 1, 1 : width + 1] = dn_bottom[...]
        taps[240:256, :] = jnp.zeros_like(taps[240:256, :])
        gtaps[144:256, :] = jnp.zeros_like(gtaps[144:256, :])

    row = step // groups
    start = (step % groups) * cols
    for i in range(cols):
        lanes = pl.ds(i * count, count)
        for dy in range(3):
            for j in range(2):
                taps[pl.ds((dy * 2 + j) * 16, 16), lanes] = xa2[row + 1 + dy, start + i + 2 * j]
            for dx in range(3):
                tap = dy * 3 + dx
                taps[pl.ds(96 + tap * 16, 16), lanes] = xt[row + 1 + dy, start + i + dx]
                gtaps[pl.ds(tap * 16, 16), lanes] = dnp[row + 2 - dy, start + i + 2 - dx]
    size = sub * count
    for s in range(cols // sub):
        lanes = pl.ds(s * size, size)
        grad2 = (dot(woutt[...], gtaps[:, lanes]) * sg2[0, :, lanes].astype(F32)).astype(BF16)
        grad1 = (dot(mixth[...], grad2) * sg1[0, :, lanes].astype(F32)).astype(BF16)
        wide = grad2.astype(F32)
        bias = wide[:, 0:128]
        for k in range(1, size // 128):
            bias = bias + wide[:, k * 128 : (k + 1) * 128]
        bias_acc[...] += bias
        packed[ROW_OUT:ROW_IN, :] += dot(gtaps[0:144, lanes], act2[0, :, lanes], NT)
        packed[ROW_MIX:ROW_OUT, :] += dot(grad2, act1[0, :, lanes], NT)
        gathered = dot(taps[0:240, lanes], grad1, NT)
        packed[ROW_IN:ROW_PRIOR, :] += gathered[0:96]
        wfield[...] += gathered[96:240]

    @pl.when(step == rows * groups - 1)
    def _():
        for k in range(4):
            packed[ROW_PRIOR:ROW_SMALL, 128 * k : 128 * k + 128] = dprior[72 * k : 72 * k + 72, :]
        packed[ROW_SMALL:ROWS, :] = small[...]
        lone = jnp.ones((8, 128), F32)
        packed[ROW_SMALL : ROW_SMALL + 8, :] = dot(lone, bias_acc[...], NT, HIGH)
        cross = dot(wt[0:96, :], wfield[...], NT, HIGH)
        row, col = iota((96, 144), 0), iota((96, 144), 1)
        slot = (row >> 3) & 3
        same = (slot < 3) & ((row >> 5) * 3 + slot == col >> 4) & ((row & 7) < 6)
        gather = as_f32(iota((8, 96), 0) == (iota((8, 96), 1) & 7))
        fold = as_f32((iota((144, 128), 0) & 15) == iota((144, 128), 1))
        field_terms = dot(dot(gather, jnp.where(same, cross, 0.0), NN, HIGH), fold, NN, HIGH)
        packed[ROW_SMALL + 8 : ROW_SMALL + 16, 128:256] += 2.0 * field_terms


def adamw(weight, first, second, grad, out, out_first, out_second, at=Ellipsis):
    first_new = BETA_ONE * first[at] + (1.0 - BETA_ONE) * grad
    second_new = BETA_TWO * second[at] + (1.0 - BETA_TWO) * grad * grad
    first_hat = first_new / (1.0 - BETA_ONE**STEP)
    second_hat = second_new / (1.0 - BETA_TWO**STEP)
    out[at] = weight[at] - RATE * (
        first_hat / (jnp.sqrt(second_hat) + EPSILON) + DECAY * weight[at]
    )
    out_first[at] = first_new
    out_second[at] = second_new


def update_kernel(area, dims, *refs):
    grads, counts = refs[:2]
    params, firsts, seconds = refs[2:10], refs[10:18], refs[18:26]
    loss, norm = refs[26:28]
    news, new_firsts, new_seconds = refs[28:36], refs[36:44], refs[44:52]
    square, strip, gin, gout, flat = refs[52:]
    bias, gains_ref, lu_ref = params[4:7]
    hidden = grads.shape[1]
    square[...] = jnp.zeros_like(square)
    square[0:12, 0:12] = lu_ref[...]
    strip[...] = jnp.zeros_like(strip)
    strip[0:3, 0:12] = gains_ref[...]
    gains = strip[...]
    lower, upper, eye = lu_factors(square[...])
    weight = spread_weight(square[...], gains)
    field = grads[ROW_SMALL + 8 : ROWS, 128:256]
    lane = iota((16, 128), 1)
    level = jnp.sum(jnp.where(lane == 12, field, 0.0), axis=1, keepdims=True)
    real = iota((16, 128), 0) & 7
    moved = jnp.where((lane < 12) & (real < 6), field + level * gains[0:1], 0.0)
    level = jnp.where(real < 6, level, 0.0)
    present = counts[...] / jnp.maximum(counts[...], 1.0)
    share = jnp.sum(present[:, 0:1], axis=0, keepdims=True)
    coef = share * (1.0 / (10.0 * dims * LOG_TWO)) * area
    weight = jnp.where(lane < 12, weight, 0.0)
    d_shift = jnp.sum(weight * level, axis=0, keepdims=True)
    d_scale = jnp.sum(weight * moved, axis=0, keepdims=True) - coef
    d_product = dot(channel_map(), moved * jnp.exp(gains[1:2]), TN, HIGH)
    d_lower = dot(d_product, upper, NT, HIGH)
    d_upper = dot(lower, d_product, TN, HIGH)
    row, col = iota((128, 128), 0), iota((128, 128), 1)
    d_lu = jnp.where(row > col, d_lower, 0.0) + jnp.where(row < col, d_upper, 0.0)
    d_lu = d_lu + jnp.where(eye, d_upper * jnp.exp(square[...]) - coef, 0.0)
    d_lu = jnp.where((row < 12) & (col < 12), d_lu, 0.0)
    diag = jnp.sum(jnp.sum(jnp.where(eye, square[...], 0.0), axis=0, keepdims=True), axis=1, keepdims=True)
    logs = jnp.sum(jnp.where(lane[0:1] < 12, gains[1:2], 0.0), axis=1, keepdims=True)
    d_bias_out = grads[ROW_SMALL + 8 : ROW_SMALL + 9, 256:384]
    row8 = iota((8, 128), 0)
    d_gains = jnp.where(row8 == 0, d_shift, jnp.where(row8 == 1, d_scale, jnp.where(row8 == 2, d_bias_out, 0.0)))
    d_gains = jnp.where(iota((8, 128), 1) < 12, d_gains, 0.0)
    for tap in range(9):
        dy, dx = tap // 3, tap % 3
        gin[tap] = grads[ROW_IN + dy * 32 + dx * 8 : ROW_IN + dy * 32 + dx * 8 + 6, :]
        at = ROW_OUT + tap * 16
        gout[tap, 0:6, :] = grads[at : at + 6, :]
        gout[tap, 6:12, :] = grads[at + 8 : at + 14, :]
    for k in range(4):
        flat[72 * k : 72 * k + 72, :] = grads[ROW_PRIOR:ROW_SMALL, 128 * k : 128 * k + 128]
    out_map = prior_out_map()
    d_prior = dot(dot(prior_in_map(), flat[...], TN, HIGH)[:, 0:64], out_map, NT, HIGH)
    d_table = grads[ROW_SMALL + 8 : ROWS, 0:128]
    d_table = [dot(d_table[:, 0:64], out_map, NT, HIGH), dot(d_table[:, 64:128], out_map, NT, HIGH)]
    d_table = [part[0:10] for part in d_table]
    d_bias = [grads[ROW_IN + 46 : ROW_IN + 47, :], grads[ROW_SMALL : ROW_SMALL + 1, :]]
    d_mix = grads[0:ROW_OUT, :]

    def squares(value):
        value = value * value
        if value.ndim == 3:
            value = jnp.sum(value, axis=0)
        return jnp.sum(jnp.sum(value, axis=0, keepdims=True), axis=1, keepdims=True)

    squared = squares(d_mix) + squares(gin[...]) + squares(gout[...]) + squares(d_prior)
    squared = squared + squares(d_bias[0]) + squares(d_bias[1]) + squares(d_gains) + squares(d_lu)
    squared = squared + squares(d_table[0]) + squares(d_table[1])
    total_norm = jnp.sqrt(squared)
    factor = jnp.minimum(1.0, CLIP_NORM / (total_norm + 1e-06))
    norm[...] = total_norm
    loss[...] = (
        grads[ROW_SMALL + 16 : ROW_SMALL + 17, 256:257] - coef * (logs + diag) + BITS * share / 10.0
    )

    def put(k, grad, at=Ellipsis):
        adamw(params[k], firsts[k], seconds[k], grad, news[k], new_firsts[k], new_seconds[k], at)

    put(0, factor * gin[...])
    put(1, factor * d_mix)
    put(2, factor * gout[...])
    put(3, (factor * d_prior).reshape(9, 24, 48))
    put(4, factor * d_bias[0], (slice(0, 1), slice(None)))
    put(4, factor * d_bias[1], (slice(1, 2), slice(None)))
    put(5, (factor * d_gains)[0:3, 0:12])
    put(6, (factor * d_lu)[0:12, 0:12])
    put(7, factor * d_table[0], (slice(None), slice(0, 48)))
    put(7, factor * d_table[1], (slice(None), slice(48, 96)))


def shape(dims, dtype=F32):
    return jax.ShapeDtypeStruct(dims, dtype)


def params_of(limit):
    return pltpu.CompilerParams(vmem_limit_bytes=limit * MIB)


def exchange_rows(up, down):
    count = lax.axis_size("band")
    before = lax.ppermute(down, "band", [(i, i + 1) for i in range(count - 1)])
    after = lax.ppermute(up, "band", [(i + 1, i) for i in range(count - 1)])
    return before, after


def body(images, noise, labels, *rest):
    params, firsts, seconds = (list(rest[8 * k : 8 * k + 8]) for k in range(3))
    for group in (params, firsts, seconds):
        group[0] = group[0].transpose(0, 2, 1)
        group[3] = group[3].transpose(0, 2, 1)
    chans, rows, width, count = images.shape
    hidden = params[1].shape[0]
    band = lax.axis_index("band")
    bands = lax.axis_size("band")
    whole = pl.BlockSpec(memory_space=pltpu.VMEM)

    top, bottom = exchange_rows(
        images[:, :2] + noise[:, :2], images[:, rows - 2 :] + noise[:, rows - 2 :]
    )
    flags = jnp.stack([band > 0, band < bands - 1]).astype(F32)
    hits = (labels[None, :] == jnp.arange(16, dtype=jnp.int32)[:, None]).astype(F32)
    counts = lax.psum(jnp.sum(hits, axis=1), "dp")
    counts = jnp.broadcast_to(counts[:, None], (16, 128))

    win, wt, mixh, mixth, bias2, wout, woutt, weff, wpt, wp, tablep = pl.pallas_call(
        weights_kernel,
        out_shape=(
            shape((hidden, 128), BF16),
            shape((128, hidden)),
            shape((hidden, hidden), BF16),
            shape((hidden, hidden), BF16),
            shape((hidden, 128)),
            shape((144, hidden), BF16),
            shape((hidden, 256), BF16),
            shape((16, 128)),
            shape((288, 256), BF16),
            shape((128, 384), BF16),
            shape((16, 128)),
        ),
        in_specs=[whole] * 8,
        out_specs=(whole,) * 11,
        scratch_shapes=[
            pltpu.VMEM((512, hidden), F32),
            pltpu.VMEM((128, 128), F32),
            pltpu.VMEM((8, 128), F32),
        ],
        compiler_params=params_of(40),
        name="weights",
    )(*params)

    cols, sub = 4, 2
    groups = width // cols
    steps = rows * groups
    size = cols * count
    full = lambda dims: pl.BlockSpec(dims, lambda i: (0,) * len(dims))
    chunk = pl.BlockSpec((1, hidden, size), lambda i: (i, 0, 0))
    ext = (rows + 4, width + 2, 16, count)
    exta = (rows + 4, width + 4, 8, count)
    act1, sg1, act2, sg2, xa2, xt, xaf, xbf, nn, edge_top, edge_bottom = pl.pallas_call(
        functools.partial(forward_kernel, cols, sub),
        grid=(steps,),
        out_shape=(shape((steps, hidden, size), BF16),) * 4
        + (
            shape(ext, BF16),
            shape(ext, BF16),
            shape(exta),
            shape((rows, width, 8, count)),
            shape((rows, width, 16, count)),
            shape((width, 16, count), BF16),
            shape((width, 16, count), BF16),
        ),
        in_specs=[full(images.shape)] * 2
        + [full(top.shape)] * 2
        + [pl.BlockSpec(memory_space=pltpu.SMEM)]
        + [full(a.shape) for a in (weff, win, mixh, bias2, wout)],
        out_specs=(chunk,) * 4
        + (
            full(ext),
            full(ext),
            full(exta),
            full((rows, width, 8, count)),
            full((rows, width, 16, count)),
            full((width, 16, count)),
            full((width, 16, count)),
        ),
        scratch_shapes=[
            pltpu.VMEM((chans, rows + 4, width, count), F32),
            pltpu.VMEM((128, size), BF16),
            pltpu.VMEM((rows + 2, width + 2, 16, count), F32),
        ],
        compiler_params=params_of(56),
        name="forward",
    )(images, noise, top, bottom, flags, weff, win, mixh, bias2, wout)

    got_top, got_bottom = exchange_rows(edge_top, edge_bottom)
    nn = nn.at[0].add(got_top.astype(F32))
    nn = nn.at[rows - 1].add(got_bottom.astype(F32))
    gain3 = params[5][2]
    zero = jnp.zeros((2,), F32)
    net_bias = jnp.concatenate([gain3[:6], zero, gain3[6:] + 2.0, zero])[:, None]
    pixels = (width // 2) * count
    dn, dprior, small = pl.pallas_call(
        coupling_kernel,
        out_shape=(
            shape((rows, width, 16, count), BF16),
            shape((288, 128)),
            shape((24, 512)),
        ),
        in_specs=[whole] * 12,
        out_specs=(whole,) * 3,
        scratch_shapes=[
            pltpu.VMEM((288, pixels), BF16),
            pltpu.VMEM((288, pixels), BF16),
            pltpu.VMEM((64, pixels), F32),
            pltpu.VMEM((64, pixels), F32),
            pltpu.VMEM((288, pixels), F32),
            pltpu.VMEM(exta, F32),
            pltpu.VMEM((rows, width, 8, count), F32),
            pltpu.VMEM((256, 256), F32),
            pltpu.VMEM((8, count), F32),
            pltpu.VMEM((16, count), F32),
            pltpu.VMEM((128, count), F32),
        ],
        compiler_params=params_of(48),
        name="coupling",
    )(nn, edge_top, edge_bottom, xaf, xbf, xt, labels[None, :], counts, wp, wpt, tablep, net_bias)

    dn_top, dn_bottom = exchange_rows(dn[0], dn[rows - 1])
    packed = pl.pallas_call(
        functools.partial(backward_kernel, cols, sub),
        grid=(steps,),
        out_shape=shape((ROWS, hidden)),
        in_specs=[chunk] * 4
        + [full(a.shape) for a in (dn, dn_top, dn_bottom, xa2, xt, mixth, woutt, wt, dprior, small)],
        out_specs=full((ROWS, hidden)),
        scratch_shapes=[
            pltpu.VMEM((rows + 2, width + 2, 16, count), BF16),
            pltpu.VMEM((256, size), BF16),
            pltpu.VMEM((256, size), BF16),
            pltpu.VMEM((hidden, 128), F32),
            pltpu.VMEM((144, hidden), F32),
        ],
        compiler_params=params_of(56),
        name="backward",
    )(act1, sg1, act2, sg2, dn, dn_top, dn_bottom, xa2, xt, mixth, woutt, wt, dprior, small)

    both = ("dp", "band")
    devices = lax.axis_size(both)
    lanes = ROWS * hidden // 128
    per = -(-lanes // devices)
    flat = jnp.pad(packed.reshape(lanes, 128), ((0, per * devices - lanes), (0, 0)))
    parts = lax.all_to_all(flat.reshape(devices, per, 128), both, 0, 0, tiled=True)
    mine = jnp.sum(parts, axis=0)
    spread = jnp.broadcast_to(mine[None], (devices, per, 128))
    grads = lax.all_to_all(spread, both, 0, 0, tiled=True)
    grads = grads.reshape(devices * per, 128)[:lanes].reshape(ROWS, hidden)

    area = float(width * width)
    results = pl.pallas_call(
        functools.partial(update_kernel, area, 12.0 * width * width),
        out_shape=(shape((1, 1)), shape((1, 1))) + tuple(shape(p.shape) for p in params) * 3,
        in_specs=[whole] * 26,
        out_specs=(whole,) * 26,
        scratch_shapes=[
            pltpu.VMEM((128, 128), F32),
            pltpu.VMEM((8, 128), F32),
            pltpu.VMEM((9, 6, hidden), F32),
            pltpu.VMEM((9, 12, hidden), F32),
            pltpu.VMEM((288, 128), F32),
        ],
        compiler_params=params_of(48),
        name="update",
    )(grads, counts, *params, *firsts, *seconds)
    outs = [results[0][0, 0], results[1][0, 0]]
    for k in range(3):
        group = list(results[2 + 8 * k : 10 + 8 * k])
        group[0] = group[0].transpose(0, 2, 1)
        group[3] = group[3].transpose(0, 2, 1)
        outs += group
    return tuple(outs)


def solution(mesh):
    field = P(None, "band", None, "dp")
    return jax.shard_map(
        body,
        mesh=mesh,
        in_specs=(field, field, P("dp")) + (P(),) * 24,
        out_specs=(P(),) * 26,
        check_vma=False,
    )
```

```python
import functools
import math

import jax
import jax.numpy as jnp
from jax import lax
from jax.experimental import pallas as pl
from jax.experimental.pallas import tpu as pltpu
from jax.sharding import PartitionSpec as P

STEP = 10
HIGH = lax.Precision.HIGHEST
LOG_TWO = math.log(2.0)
LOG_TWO_PI = math.log(2.0 * math.pi)
CLIP_NORM = 0.01
RATE = 0.05
BETA_ONE = 0.9
BETA_TWO = 0.999
EPSILON = 1e-08
DECAY = 0.01
BITS = 5.0
F32 = jnp.float32
BF16 = jnp.bfloat16
MIB = 1024 * 1024
NN = (((1,), (0,)), ((), ()))
NT = (((1,), (1,)), ((), ()))
TN = (((0,), (0,)), ((), ()))

ROW_MIX = 0
ROW_OUT = 512
ROW_IN = ROW_OUT + 108
ROW_BIAS = ROW_IN + 54
ROW_PRIOR = ROW_BIAS + 6
ROW_SMALL = ROW_PRIOR + 72
ROWS = ROW_SMALL + 16


def dot(left, right, dims=NN, precision=None):
    return lax.dot_general(left, right, dims, precision=precision, preferred_element_type=F32)


def iota(shape, dim):
    return lax.broadcasted_iota(jnp.int32, shape, dim)


def as_f32(mask):
    return jnp.where(mask, 1.0, 0.0).astype(F32)


def prior_out_map():
    row, col = iota((48, 64), 0), iota((48, 64), 1)
    kind, d, c = col >> 5, (col >> 3) & 3, col & 7
    return as_f32((c < 6) & (row == kind * 24 + 4 * c + d))


def prior_in_map():
    row, col = iota((288, 216), 0), iota((288, 216), 1)
    tap, d, c = row >> 5, (row >> 3) & 3, row & 7
    return as_f32((c < 6) & (col == tap * 24 + 4 * c + d))


def channel_map():
    row, col = iota((16, 128), 0), iota((16, 128), 1)
    return as_f32(((row < 6) & (col == 11 - row)) | ((row >= 8) & (row < 14) & (col == 13 - row)))


def half_map():
    row, col = iota((16, 128), 0), iota((16, 128), 1)
    return as_f32(((row < 6) & (col == row)) | ((row >= 8) & (row < 14) & (col == row - 2)))


def lu_factors(lu):
    row, col = iota((128, 128), 0), iota((128, 128), 1)
    eye = (row == col) & (row < 12)
    lower = jnp.where(row > col, lu, 0.0) + as_f32(eye)
    upper = jnp.where(row < col, lu, 0.0) + jnp.where(eye, jnp.exp(lu), 0.0)
    return lower, upper, eye


def spread_weight(lu, gains):
    lower, upper, _ = lu_factors(lu)
    weight = dot(channel_map(), dot(lower, upper, NN, HIGH), NN, HIGH)
    scaled = weight * jnp.exp(gains[1:2])
    shift = jnp.sum(scaled * gains[0:1], axis=1, keepdims=True)
    return jnp.where(iota((16, 128), 1) == 12, shift, scaled)


def weights_kernel(cin, mix, cout, prior, bias, gains, lu, table,
                   win, wt, mixh, mixth, bias2, wout, woutt, weff, wpt, wp, tablep,
                   big, square, strip):
    hidden = mix.shape[0]
    wt[...] = jnp.zeros_like(wt)
    for dy in range(3):
        for dx in range(3):
            wt[pl.ds(dy * 32 + dx * 8, 6), :] = (
                0.5 * cin[dy * 3 + dx]
            ).astype(BF16).astype(F32)
    half = 0.5 * bias[0:1, :]
    first = half.astype(BF16).astype(F32)
    rest = half - first
    second = rest.astype(BF16).astype(F32)
    wt[46:47, :] = first
    wt[38:39, :] = second
    wt[54:55, :] = rest - second
    win[...] = wt[...].T.astype(BF16)
    mixh[...] = (0.5 * mix[...]).astype(BF16)
    mixth[...] = (0.5 * mix[...]).T.astype(BF16)
    bias2[...] = jnp.broadcast_to(0.5 * bias[1:2, :], (128, hidden)).T
    big[...] = jnp.zeros_like(big)
    for tap in range(9):
        big[pl.ds(tap * 16, 6), :] = cout[tap, 0:6, :]
        big[pl.ds(tap * 16 + 8, 6), :] = cout[tap, 6:12, :]
    wout[...] = big[0:144, :].astype(BF16)
    woutt[...] = (0.5 * big[0:256, :]).T.astype(BF16)
    square[...] = jnp.zeros_like(square)
    square[0:12, 0:12] = lu[...]
    strip[...] = jnp.zeros_like(strip)
    strip[0:3, 0:12] = gains[...]
    weff[...] = spread_weight(square[...], strip[0:8, :])
    out_map = prior_out_map()
    flat = dot(prior_in_map(), dot(prior[...].reshape(216, 48), out_map, NN, HIGH), NN, HIGH)
    flat_hi = flat.astype(BF16)
    flat_lo = (flat - flat_hi.astype(F32)).astype(BF16)
    wpt[...] = jnp.zeros_like(wpt)
    wpt[:, 0:64] = flat_hi
    wpt[:, 64:128] = flat_lo
    wpt[:, 128:192] = flat_hi
    big[...] = jnp.zeros_like(big)
    big[0:288, 0:64] = flat_hi.astype(F32)
    big[0:288, 64:128] = flat_lo.astype(F32)
    wp[...] = big[0:384, 0:128].T.astype(BF16)
    tablep[...] = jnp.zeros_like(tablep)
    tablep[0:10, 0:64] = dot(table[:, 0:48], out_map, NN, HIGH)
    tablep[0:10, 64:128] = dot(table[:, 48:96], out_map, NN, HIGH)


def hidden_unit(u):
    wide = 1.0 + jnp.tanh(u)
    act = u * wide
    return act.astype(BF16), (wide + act * (2.0 - wide)).astype(BF16)


def forward_kernel(cols, sub, images, noise, top, bottom, flags, weff, win, mixh, bias2, wout,
                   act1, sg1, act2, sg2, xa2, xt, xaf, xbf, nn, edge_top, edge_bottom,
                   xs, taps, acc):
    step = pl.program_id(0)
    rows, width, count = images.shape[1:]
    groups = width // cols

    @pl.when(step == 0)
    def _():
        xs[:, 0:2] = top[...]
        xs[:, 2 : rows + 2] = images[...] + noise[...]
        xs[:, rows + 2 : rows + 4] = bottom[...]
        xaf[...] = jnp.zeros_like(xaf)
        xt[...] = jnp.zeros_like(xt)
        acc[...] = jnp.zeros_like(acc)
        row8 = iota((8, count), 0)
        ones = jnp.where((iota((16, count), 0) & 7) == 6, 1.0, 0.0)
        col_a = [jnp.broadcast_to(weff[0:8, c : c + 1], (8, count)) for c in range(13)]
        col_b = [jnp.broadcast_to(weff[8:16, c : c + 1], (8, count)) for c in range(13)]

        def per_row(er, carry):
            own = (er >= 2) & (er < rows + 2)
            valid = jnp.where(er < 2, flags[0], jnp.where(er >= rows + 2, flags[1], 1.0))
            inner = jnp.clip(er - 2, 0, rows - 1)
            for c in range(width):
                a, b = col_a[12], col_b[12]
                t0 = jnp.zeros((8, count), F32)
                t1 = jnp.where(row8 == 4, valid, 0.0)
                for ch in range(12):
                    x = jnp.broadcast_to(xs[ch, er, c : c + 1, :], (8, count))
                    a = a + col_a[ch] * x
                    b = b + col_b[ch] * x
                    if ch < 8:
                        t0 = jnp.where(row8 == ch, x, t0)
                    else:
                        t1 = jnp.where(row8 == ch - 8, x, t1)
                xaf[er, c + 2] = a * valid
                xt[er, c + 1] = jnp.concatenate([t0, t1], axis=0).astype(BF16)

                @pl.when(own)
                def _():
                    xbf[inner, c] = b

            for c in range(width + 2):
                pair = jnp.concatenate([xaf[er, c + 1], xaf[er, c + 2]], axis=0)
                xa2[er, c] = (pair + ones).astype(BF16)
            return carry

        lax.fori_loop(0, rows + 4, per_row, 0)

    row = step // groups
    start = (step % groups) * cols
    for i in range(cols):
        lanes = pl.ds(i * count, count)
        for dy in range(3):
            for j in range(2):
                taps[pl.ds((dy * 2 + j) * 16, 16), lanes] = xa2[row + 1 + dy, start + i + 2 * j]
        taps[96:112, lanes] = xt[row + 2, start + i + 1]
        taps[112:128, lanes] = xt[row + 2, start + i + 1]
    size = sub * count
    for s in range(cols // sub):
        lanes = pl.ds(s * size, size)
        one, slope1 = hidden_unit(dot(win[...], taps[:, lanes]))
        act1[0, :, lanes] = one
        sg1[0, :, lanes] = slope1
        bias = jnp.concatenate([bias2[...]] * (size // 128), axis=1)
        two, slope2 = hidden_unit(dot(mixh[...], one) + bias)
        act2[0, :, lanes] = two
        sg2[0, :, lanes] = slope2
        out = dot(wout[...], two)
        for i in range(sub):
            for dy in range(3):
                for dx in range(3):
                    r = row + 2 - dy
                    c = start + s * sub + i + 2 - dx
                    tap = dy * 3 + dx
                    acc[r, c] += out[tap * 16 : tap * 16 + 16, i * count : (i + 1) * count]

    @pl.when(step == rows * groups - 1)
    def _():
        nn[...] = acc[1 : rows + 1, 1 : width + 1]
        edge_top[...] = acc[0, 1 : width + 1].astype(BF16)
        edge_bottom[...] = acc[rows + 1, 1 : width + 1].astype(BF16)


def coupling_kernel(nn, edge_top, edge_bottom, xaf, xbf, xt, labels, counts, wp, wpt, tablep, net_bias_ref,
                    dn, dprior, small, taps_hi, taps_lo, stats, dstats, dtaps, dxa, dxb, total,
                    loss_acc, gain_acc, table_acc):
    rows, width, _, count = nn.shape
    half = width // 2
    classes = 10
    hot = as_f32(iota((16, count), 0) == jnp.broadcast_to(labels[...], (16, count)))
    present = jnp.maximum(counts[...], 1.0)
    dims = 12.0 * width * width
    scale16 = 1.0 / (classes * present * (dims * LOG_TWO))
    coef = jnp.sum(hot * scale16[:, 0:1], axis=0, keepdims=True)
    coef = jnp.broadcast_to(coef, (8, count))
    cls = dot(tablep[...], hot, TN, HIGH)
    dxa[...] = jnp.zeros_like(dxa)
    loss_acc[...] = jnp.zeros_like(loss_acc)
    gain_acc[...] = jnp.zeros_like(gain_acc)
    table_acc[...] = jnp.zeros_like(table_acc)
    dprior[...] = jnp.zeros_like(dprior)
    dstats[...] = jnp.zeros_like(dstats)
    keep = iota((8, count), 0) < 6
    net_bias = net_bias_ref[...]
    bias_a = jnp.broadcast_to(net_bias[0:8, 0:1], (8, count))
    bias_b = jnp.broadcast_to(net_bias[8:16, 0:1], (8, count))

    def per_row(r2, carry):
        for w in range(half):
            lanes = pl.ds(w * count, count)
            for ty in range(3):
                for tx in range(3):
                    for dy in range(2):
                        er, ec = 2 * r2 + 2 * ty + dy, 2 * w + 2 * tx
                        pair = jnp.concatenate([xaf[er, ec], xaf[er, ec + 1]], axis=0)
                        high = pair.astype(BF16)
                        at = pl.ds((ty * 3 + tx) * 32 + dy * 16, 16)
                        taps_hi[at, lanes] = high
                        taps_lo[at, lanes] = (pair - high.astype(F32)).astype(BF16)
        main = dot(wp[:, 0:288], taps_hi[...])
        stats[...] = main[0:64] + main[64:128] + dot(wp[0:64, 0:288], taps_lo[...])
        for w in range(half):
            lanes = pl.ds(w * count, count)
            for dy in range(2):
                for dx in range(2):
                    d = 2 * dy + dx
                    r, c = 2 * r2 + dy, 2 * w + dx
                    tile = nn[r, c]
                    tile = tile + jnp.where(r == 0, edge_top[c].astype(F32), 0.0)
                    tile = tile + jnp.where(r == rows - 1, edge_bottom[c].astype(F32), 0.0)
                    shift = tile[0:8] + bias_a
                    raw = tile[8:16] + bias_b
                    sig = jax.nn.sigmoid(raw)
                    log_sig = jnp.minimum(raw, 0.0) - jnp.log(1.0 + jnp.exp(-jnp.abs(raw)))
                    base = xbf[r, c] + shift
                    second = base * sig
                    mean = stats[pl.ds(8 * d, 8), lanes] + cls[8 * d : 8 * d + 8]
                    logs = stats[pl.ds(32 + 8 * d, 8), lanes] + cls[32 + 8 * d : 40 + 8 * d]
                    diff = second - mean
                    weighted = diff * jnp.exp(-2.0 * logs)
                    quad = diff * weighted
                    first = xaf[r + 2, c + 2]
                    mean1 = cls[64 + 8 * d : 72 + 8 * d]
                    logs1 = cls[96 + 8 * d : 104 + 8 * d]
                    diff1 = first - mean1
                    weighted1 = diff1 * jnp.exp(-2.0 * logs1)
                    quad1 = diff1 * weighted1
                    value = log_sig - 0.5 * (
                        2.0 * LOG_TWO_PI + 2.0 * (logs + logs1) + quad + quad1
                    )
                    loss_acc[...] += jnp.where(keep, value, 0.0)
                    dv = coef * weighted
                    ds_ = coef - coef * quad
                    dv1 = coef * weighted1
                    table_acc[pl.ds(8 * d, 8), :] -= dv
                    table_acc[pl.ds(32 + 8 * d, 8), :] += ds_
                    table_acc[pl.ds(64 + 8 * d, 8), :] -= dv1
                    table_acc[pl.ds(96 + 8 * d, 8), :] += coef - coef * quad1
                    dstats[pl.ds(8 * d, 8), lanes] = -dv
                    dstats[pl.ds(32 + 8 * d, 8), lanes] = ds_
                    dxa[r + 2, c + 2] += dv1
                    passed = dv * sig
                    dxb[r, c] = passed
                    draw = (passed * base - coef) * (1.0 - sig)
                    net = jnp.concatenate([passed, draw], axis=0).astype(BF16)
                    dn[r, c] = net
                    gain_acc[...] += net.astype(F32)
        grads = dstats[0:64, :]
        high = grads.astype(BF16)
        low = (grads - high.astype(F32)).astype(BF16)
        dprior[:, 0:64] += (
            dot(taps_hi[...], high, NT) + dot(taps_hi[...], low, NT) + dot(taps_lo[...], high, NT)
        )
        stack = jnp.concatenate([high, high, low], axis=0)
        dtaps[...] = dot(wpt[:, 0:192], stack)
        for w in range(half):
            lanes = pl.ds(w * count, count)
            for ty in range(3):
                for tx in range(3):
                    for dy in range(2):
                        for dx in range(2):
                            k = (ty * 3 + tx) * 32 + dy * 16 + dx * 8
                            dxa[2 * r2 + 2 * ty + dy, 2 * w + 2 * tx + dx] += dtaps[pl.ds(k, 8), lanes]
        return carry

    lax.fori_loop(0, rows // 2, per_row, 0)

    total[...] = jnp.zeros_like(total)
    for er in range(rows + 4):
        field = xt[er, 1 : width + 1].reshape(width * 16, count)
        part_a = dxa[er, 2 : width + 2].reshape(width * 8, count)
        if 2 <= er < rows + 2:
            part_b = dxb[er - 2].reshape(width * 8, count)
            part = jnp.concatenate([part_a, part_b], axis=0)
        else:
            part = part_a
        size = part.shape[0]
        high = part.astype(BF16)
        low = (part - high.astype(F32)).astype(BF16)
        total[0:size, :] += dot(high, field, NT) + dot(low, field, NT)
    row, col = iota((256, 256), 0), iota((256, 256), 1)
    masked = jnp.where(((row & 127) >> 3) == (col >> 4), total[...], 0.0)
    gather = as_f32((iota((16, 256), 0) == ((iota((16, 256), 1) & 7) + 8 * (iota((16, 256), 1) >> 7))))
    fold = as_f32((iota((256, 128), 0) & 15) == iota((256, 128), 1))
    small[...] = jnp.zeros_like(small)
    small[:, 128:256] = dot(dot(gather, masked, NN, HIGH), fold, NN, HIGH)
    small[:, 0:128] = dot(hot, table_acc[...], NT, HIGH)
    lone = jnp.ones((8, count), F32)
    gain_row = dot(dot(lone, gain_acc[...], NT, HIGH), half_map(), NN, HIGH)
    small[0:8, 256:384] = gain_row
    value = jnp.sum(jnp.sum(loss_acc[...], axis=0, keepdims=True) * coef[0:1], axis=1, keepdims=True)
    small[8:16, 256:384] = jnp.broadcast_to(-value, (8, 128))


def backward_kernel(cols, sub, act1, sg1, act2, sg2, place, dn, dn_top, dn_bottom, xa2, xt, mixth, woutt, wt,
                    dprior, small, keep, send, packed, dnp, taps, gtaps, bias_acc, wfield, gout, gin):
    step = pl.program_id(0)
    rows, width, _, count = dn.shape
    groups = width // cols

    @pl.when(step == 0)
    def _():
        packed[...] = jnp.zeros_like(packed)
        gout[...] = jnp.zeros_like(gout)
        gin[...] = jnp.zeros_like(gin)
        bias_acc[...] = jnp.zeros_like(bias_acc)
        wfield[...] = jnp.zeros_like(wfield)
        dnp[...] = jnp.zeros_like(dnp)
        dnp[0, 1 : width + 1] = dn_top[...]
        dnp[1 : rows + 1, 1 : width + 1] = dn[...]
        dnp[rows + 1, 1 : width + 1] = dn_bottom[...]
        taps[240:256, :] = jnp.zeros_like(taps[240:256, :])
        gtaps[144:256, :] = jnp.zeros_like(gtaps[144:256, :])

    row = step // groups
    start = (step % groups) * cols
    for i in range(cols):
        lanes = pl.ds(i * count, count)
        for dy in range(3):
            for j in range(2):
                taps[pl.ds((dy * 2 + j) * 16, 16), lanes] = xa2[row + 1 + dy, start + i + 2 * j]
            for dx in range(3):
                tap = dy * 3 + dx
                taps[pl.ds(96 + tap * 16, 16), lanes] = xt[row + 1 + dy, start + i + dx]
                gtaps[pl.ds(tap * 16, 16), lanes] = dnp[row + 2 - dy, start + i + 2 - dx]
    size = sub * count
    for s in range(cols // sub):
        lanes = pl.ds(s * size, size)
        grad2 = (dot(woutt[...], gtaps[:, lanes]) * sg2[0, :, lanes].astype(F32)).astype(BF16)
        grad1 = (dot(mixth[...], grad2) * sg1[0, :, lanes].astype(F32)).astype(BF16)
        wide = grad2.astype(F32)
        bias = wide[:, 0:128]
        for k in range(1, size // 128):
            bias = bias + wide[:, k * 128 : (k + 1) * 128]
        bias_acc[...] += bias
        gout[...] += dot(gtaps[0:144, lanes], act2[0, :, lanes], NT)
        packed[ROW_MIX:ROW_OUT, :] += dot(grad2, act1[0, :, lanes], NT)
        gathered = dot(taps[0:240, lanes], grad1, NT)
        gin[...] += gathered[0:96]
        wfield[...] += gathered[96:240]

    @pl.when(step == rows * groups - 1)
    def _():
        for tap in range(9):
            at = ROW_OUT + 12 * tap
            packed[at : at + 6, :] = gout[16 * tap : 16 * tap + 6, :]
            packed[at + 6 : at + 12, :] = gout[16 * tap + 8 : 16 * tap + 14, :]
            at = ROW_IN + 6 * tap
            from_row = (tap // 3) * 32 + (tap % 3) * 8
            packed[at : at + 6, :] = gin[from_row : from_row + 6, :]
        packed[ROW_BIAS : ROW_BIAS + 1, :] = gin[46:47, :]
        lone = jnp.ones((8, 128), F32)
        packed[ROW_BIAS + 1 : ROW_BIAS + 2, :] = dot(lone, bias_acc[...], NT, HIGH)[0:1]
        for k in range(4):
            packed[ROW_PRIOR:ROW_SMALL, 128 * k : 128 * k + 128] = dprior[72 * k : 72 * k + 72, :]
        packed[ROW_SMALL:ROWS, :] = small[...]
        cross = dot(wt[0:96, :], wfield[...], NT, HIGH)
        row, col = iota((96, 144), 0), iota((96, 144), 1)
        slot = (row >> 3) & 3
        same = (slot < 3) & ((row >> 5) * 3 + slot == col >> 4) & ((row & 7) < 6)
        gather = as_f32(iota((8, 96), 0) == (iota((8, 96), 1) & 7))
        fold = as_f32((iota((144, 128), 0) & 15) == iota((144, 128), 1))
        field_terms = dot(dot(gather, jnp.where(same, cross, 0.0), NN, HIGH), fold, NN, HIGH)
        packed[ROW_SMALL : ROW_SMALL + 8, 128:256] += 2.0 * field_terms
        chunks, each = keep.shape[:2]
        core = place[0]
        for k in range(2 * chunks):
            block = packed[k * each : (k + 1) * each, :]
            mine = core == k // chunks

            @pl.when(mine)
            def _():
                keep[k % chunks] = block

            @pl.when(jnp.logical_not(mine))
            def _():
                send[k % chunks] = block


def halve_kernel(place, keep, got, mine, *sends):
    count = len(sends) + 1
    bands = keep.shape[0] // count
    here = place[1]
    for m in range(count):
        target = mine if m == 0 else sends[m - 1]
        at = pl.ds((here ^ m) * bands, bands)
        target[...] = keep[at] + got[at]


def spread_kernel(place, bands, first, *refs):
    gots, mine, sends = refs[: -bands], refs[-bands], refs[1 - bands :]
    here = place[2]
    for k in range(bands):
        target = mine if k == 0 else sends[k - 1]
        at = lax.rem(here + k, bands)
        value = first[at]
        for got in gots:
            value = value + got[at]
        target[...] = value


def sum_kernel(*refs):
    value = refs[0][...]
    for ref in refs[1:-1]:
        value = value + ref[...]
    refs[-1][...] = value


def gather_kernel(place, which, xor, mine, *refs):
    out = refs[-1]
    here = place[which]
    count = len(refs)
    for k in range(count):
        at = (here ^ k) if xor else lax.rem(here - k + count, count)
        out[at] = (mine if k == 0 else refs[k - 1])[...]


def adamw(weight, first, second, grad, out, out_first, out_second, at=Ellipsis):
    first_new = BETA_ONE * first[at] + (1.0 - BETA_ONE) * grad
    second_new = BETA_TWO * second[at] + (1.0 - BETA_TWO) * grad * grad
    first_hat = first_new / (1.0 - BETA_ONE**STEP)
    second_hat = second_new / (1.0 - BETA_TWO**STEP)
    out[at] = weight[at] - RATE * (
        first_hat / (jnp.sqrt(second_hat) + EPSILON) + DECAY * weight[at]
    )
    out_first[at] = first_new
    out_second[at] = second_new


def update_kernel(area, dims, *refs):
    place, own, other, counts = refs[:4]
    refs = refs[4:]
    params, firsts, seconds = refs[:8], refs[8:16], refs[16:24]
    loss, norm = refs[24:26]
    news, new_firsts, new_seconds = refs[26:34], refs[34:42], refs[42:50]
    square, strip, gin, gout, flat, grads = refs[50:]
    chunks, each = own.shape[:2]
    for k in range(2 * chunks):
        mine = place[0] == k // chunks
        grads[k * each : (k + 1) * each, :] = jnp.where(mine, own[k % chunks], other[k % chunks])
    bias, gains_ref, lu_ref = params[4:7]
    hidden = grads.shape[1]
    square[...] = jnp.zeros_like(square)
    square[0:12, 0:12] = lu_ref[...]
    strip[...] = jnp.zeros_like(strip)
    strip[0:3, 0:12] = gains_ref[...]
    gains = strip[...]
    lower, upper, eye = lu_factors(square[...])
    weight = spread_weight(square[...], gains)
    field = grads[ROW_SMALL:ROWS, 128:256]
    lane = iota((16, 128), 1)
    level = jnp.sum(jnp.where(lane == 12, field, 0.0), axis=1, keepdims=True)
    real = iota((16, 128), 0) & 7
    moved = jnp.where((lane < 12) & (real < 6), field + level * gains[0:1], 0.0)
    level = jnp.where(real < 6, level, 0.0)
    present = counts[...] / jnp.maximum(counts[...], 1.0)
    share = jnp.sum(present[:, 0:1], axis=0, keepdims=True)
    coef = share * (1.0 / (10.0 * dims * LOG_TWO)) * area
    weight = jnp.where(lane < 12, weight, 0.0)
    d_shift = jnp.sum(weight * level, axis=0, keepdims=True)
    d_scale = jnp.sum(weight * moved, axis=0, keepdims=True) - coef
    d_product = dot(channel_map(), moved * jnp.exp(gains[1:2]), TN, HIGH)
    d_lower = dot(d_product, upper, NT, HIGH)
    d_upper = dot(lower, d_product, TN, HIGH)
    row, col = iota((128, 128), 0), iota((128, 128), 1)
    d_lu = jnp.where(row > col, d_lower, 0.0) + jnp.where(row < col, d_upper, 0.0)
    d_lu = d_lu + jnp.where(eye, d_upper * jnp.exp(square[...]) - coef, 0.0)
    d_lu = jnp.where((row < 12) & (col < 12), d_lu, 0.0)
    diag = jnp.sum(jnp.sum(jnp.where(eye, square[...], 0.0), axis=0, keepdims=True), axis=1, keepdims=True)
    logs = jnp.sum(jnp.where(lane[0:1] < 12, gains[1:2], 0.0), axis=1, keepdims=True)
    d_bias_out = grads[ROW_SMALL : ROW_SMALL + 1, 256:384]
    row8 = iota((8, 128), 0)
    d_gains = jnp.where(row8 == 0, d_shift, jnp.where(row8 == 1, d_scale, jnp.where(row8 == 2, d_bias_out, 0.0)))
    d_gains = jnp.where(iota((8, 128), 1) < 12, d_gains, 0.0)
    for tap in range(9):
        gin[tap] = grads[ROW_IN + 6 * tap : ROW_IN + 6 * tap + 6, :]
        gout[tap] = grads[ROW_OUT + 12 * tap : ROW_OUT + 12 * tap + 12, :]
    for k in range(4):
        flat[72 * k : 72 * k + 72, :] = grads[ROW_PRIOR:ROW_SMALL, 128 * k : 128 * k + 128]
    out_map = prior_out_map()
    d_prior = dot(dot(prior_in_map(), flat[...], TN, HIGH)[:, 0:64], out_map, NT, HIGH)
    d_table = grads[ROW_SMALL:ROWS, 0:128]
    d_table = [dot(d_table[:, 0:64], out_map, NT, HIGH), dot(d_table[:, 64:128], out_map, NT, HIGH)]
    d_table = [part[0:10] for part in d_table]
    d_bias = [grads[ROW_BIAS : ROW_BIAS + 1, :], grads[ROW_BIAS + 1 : ROW_BIAS + 2, :]]
    d_mix = grads[0:ROW_OUT, :]

    def squares(value):
        value = value * value
        if value.ndim == 3:
            value = jnp.sum(value, axis=0)
        return jnp.sum(jnp.sum(value, axis=0, keepdims=True), axis=1, keepdims=True)

    squared = squares(d_mix) + squares(gin[...]) + squares(gout[...]) + squares(d_prior)
    squared = squared + squares(d_bias[0]) + squares(d_bias[1]) + squares(d_gains) + squares(d_lu)
    squared = squared + squares(d_table[0]) + squares(d_table[1])
    total_norm = jnp.sqrt(squared)
    factor = jnp.minimum(1.0, CLIP_NORM / (total_norm + 1e-06))
    norm[...] = total_norm
    loss[...] = (
        grads[ROW_SMALL + 8 : ROW_SMALL + 9, 256:257] - coef * (logs + diag) + BITS * share / 10.0
    )

    def put(k, grad, at=Ellipsis):
        adamw(params[k], firsts[k], seconds[k], grad, news[k], new_firsts[k], new_seconds[k], at)

    put(0, factor * gin[...])
    put(1, factor * d_mix)
    put(2, factor * gout[...])
    put(3, (factor * d_prior).reshape(9, 24, 48))
    put(4, factor * d_bias[0], (slice(0, 1), slice(None)))
    put(4, factor * d_bias[1], (slice(1, 2), slice(None)))
    put(5, (factor * d_gains)[0:3, 0:12])
    put(6, (factor * d_lu)[0:12, 0:12])
    put(7, factor * d_table[0], (slice(None), slice(0, 48)))
    put(7, factor * d_table[1], (slice(None), slice(48, 96)))


def shape(dims, dtype=F32):
    return jax.ShapeDtypeStruct(dims, dtype)


def near(dims, dtype=F32):
    return pltpu.HBM(dims, dtype)


def far(array):
    return pltpu.with_memory_space_constraint(array, pltpu.HBM)


def params_of(limit):
    return pltpu.CompilerParams(vmem_limit_bytes=limit * MIB)


def exchange_rows(up, down):
    count = lax.axis_size("band")
    before = lax.ppermute(down, "band", [(i, i + 1) for i in range(count - 1)])
    after = lax.ppermute(up, "band", [(i + 1, i) for i in range(count - 1)])
    return before, after


def body(images, noise, labels, *rest):
    params, firsts, seconds = (list(rest[8 * k : 8 * k + 8]) for k in range(3))
    for group in (params, firsts, seconds):
        group[0] = group[0].transpose(0, 2, 1)
        group[3] = group[3].transpose(0, 2, 1)
    chans, rows, width, count = images.shape
    hidden = params[1].shape[0]
    band = lax.axis_index("band")
    bands = lax.axis_size("band")
    whole = pl.BlockSpec(memory_space=pltpu.VMEM)

    top, bottom = exchange_rows(
        images[:, :2] + noise[:, :2], images[:, rows - 2 :] + noise[:, rows - 2 :]
    )
    flags = jnp.stack([band > 0, band < bands - 1]).astype(F32)
    dp = lax.axis_index("dp")
    place = jnp.stack([dp & 1, dp >> 1, band]).astype(jnp.int32)
    smem = pl.BlockSpec(memory_space=pltpu.SMEM)
    hits = (labels[None, :] == jnp.arange(16, dtype=jnp.int32)[:, None]).astype(F32)
    groups = lax.axis_size("dp")
    counts = jnp.broadcast_to(jnp.sum(hits, axis=1)[None, :, None], (groups, 16, 128))
    counts = jnp.sum(lax.all_to_all(counts, "dp", 0, 0, tiled=True), axis=0)

    win, wt, mixh, mixth, bias2, wout, woutt, weff, wpt, wp, tablep = pl.pallas_call(
        weights_kernel,
        out_shape=(
            near((hidden, 128), BF16),
            near((128, hidden)),
            near((hidden, hidden), BF16),
            near((hidden, hidden), BF16),
            near((hidden, 128)),
            near((144, hidden), BF16),
            near((hidden, 256), BF16),
            near((16, 128)),
            near((288, 256), BF16),
            near((128, 384), BF16),
            near((16, 128)),
        ),
        in_specs=[whole] * 8,
        out_specs=(whole,) * 11,
        scratch_shapes=[
            pltpu.VMEM((512, hidden), F32),
            pltpu.VMEM((128, 128), F32),
            pltpu.VMEM((8, 128), F32),
        ],
        compiler_params=params_of(26),
        name="weights",
    )(*[far(p) for p in params])

    cols, sub = 4, 4
    groups = width // cols
    steps = rows * groups
    size = cols * count
    chunk = pl.BlockSpec((1, hidden, size), lambda i: (i, 0, 0))
    ext = (rows + 4, width + 2, 16, count)
    exta = (rows + 4, width + 4, 8, count)
    act1, sg1, act2, sg2, xa2, xt, xaf, xbf, nn, edge_top, edge_bottom = pl.pallas_call(
        functools.partial(forward_kernel, cols, sub),
        grid=(steps,),
        out_shape=(pltpu.HBM((steps, hidden, size), BF16),) * 4
        + (
            near(ext, BF16),
            near(ext, BF16),
            near(exta),
            near((rows, width, 8, count)),
            near((rows, width, 16, count)),
            near((width, 16, count), BF16),
            near((width, 16, count), BF16),
        ),
        in_specs=[whole] * 4 + [smem] + [whole] * 5,
        out_specs=(chunk,) * 4 + (whole,) * 7,
        scratch_shapes=[
            pltpu.VMEM((chans, rows + 4, width, count), F32),
            pltpu.VMEM((128, size), BF16),
            pltpu.VMEM((rows + 2, width + 2, 16, count), F32),
        ],
        compiler_params=params_of(26),
        name="forward",
    )(*map(far, (images, noise, top, bottom)), flags, *map(far, (weff, win, mixh, bias2, wout)))

    edge_top, edge_bottom = exchange_rows(edge_top, edge_bottom)
    gain3 = params[5][2]
    zero = jnp.zeros((2,), F32)
    net_bias = jnp.concatenate([gain3[:6], zero, gain3[6:] + 2.0, zero])[:, None]
    pixels = (width // 2) * count
    dn, dprior, small = pl.pallas_call(
        coupling_kernel,
        out_shape=(
            near((rows, width, 16, count), BF16),
            near((288, 128)),
            near((16, 512)),
        ),
        in_specs=[whole] * 12,
        out_specs=(whole,) * 3,
        scratch_shapes=[
            pltpu.VMEM((288, pixels), BF16),
            pltpu.VMEM((288, pixels), BF16),
            pltpu.VMEM((64, pixels), F32),
            pltpu.VMEM((64, pixels), F32),
            pltpu.VMEM((288, pixels), F32),
            pltpu.VMEM(exta, F32),
            pltpu.VMEM((rows, width, 8, count), F32),
            pltpu.VMEM((256, 256), F32),
            pltpu.VMEM((8, count), F32),
            pltpu.VMEM((16, count), F32),
            pltpu.VMEM((128, count), F32),
        ],
        compiler_params=params_of(26),
        name="coupling",
    )(*map(far, (nn, edge_top, edge_bottom, xaf, xbf, xt, labels[None, :], counts, wp, wpt, tablep, net_bias)))

    dn_top, dn_bottom = exchange_rows(dn[0], dn[rows - 1])
    both = ("dp", "band")
    devices = lax.axis_size(both)
    each = -(-ROWS // devices)
    half_shape = (devices // 2, each, hidden)
    keep, send = pl.pallas_call(
        functools.partial(backward_kernel, cols, sub),
        grid=(steps,),
        out_shape=(near(half_shape),) * 2,
        in_specs=[chunk] * 4 + [smem] + [whole] * 10,
        out_specs=(whole,) * 2,
        scratch_shapes=[
            pltpu.VMEM((devices * each, hidden), F32),
            pltpu.VMEM((rows + 2, width + 2, 16, count), BF16),
            pltpu.VMEM((256, size), BF16),
            pltpu.VMEM((256, size), BF16),
            pltpu.VMEM((hidden, 128), F32),
            pltpu.VMEM((144, hidden), F32),
            pltpu.VMEM((144, hidden), F32),
            pltpu.VMEM((96, hidden), F32),
        ],
        compiler_params=params_of(26),
        name="backward",
    )(*map(far, (act1, sg1, act2, sg2)), place, *map(far, (dn, dn_top, dn_bottom, xa2, xt, mixth, woutt, wt, dprior, small)))

    def call(kernel, name, outs, *inputs):
        return pl.pallas_call(
            kernel,
            out_shape=outs,
            in_specs=[smem if a is place else whole for a in inputs],
            out_specs=jax.tree.map(lambda _: whole, outs),
            compiler_params=params_of(26),
            name=name,
        )(*inputs)

    def swap(array, mask):
        pairs = [(i, i ^ mask) for i in range(groups_dp)]
        return lax.ppermute(array, "dp", pairs)

    def turn(array, k):
        return lax.ppermute(array, "band", [(i, (i + k) % bands) for i in range(bands)])

    groups_dp = lax.axis_size("dp")
    chips = groups_dp // 2
    got = swap(send, 1)
    block = shape((bands, each, hidden))
    tile = shape((each, hidden))
    mine, *sends = call(halve_kernel, "halve", (block,) * chips, place, keep, got)
    gots = [swap(a, 2 * (m + 1)) for m, a in enumerate(sends)]
    mine, *sends = call(
        lambda p, *refs: spread_kernel(p, bands, *refs), "spread", (tile,) * bands, place, mine, *gots
    )
    gots = [turn(a, k + 1) for k, a in enumerate(sends)]
    mine = call(sum_kernel, "total", tile, mine, *gots)
    gots = [turn(mine, k + 1) for k in range(bands - 1)]
    mine = call(
        lambda p, *refs: gather_kernel(p, 2, False, *refs), "gather_band", block, place, mine, *gots
    )
    gots = [swap(mine, 2 * (m + 1)) for m in range(chips - 1)]
    mine = call(
        lambda p, *refs: gather_kernel(p, 1, True, *refs),
        "gather_chips",
        shape((chips,) + block.shape),
        place,
        mine,
        *gots,
    )
    mine = mine.reshape(half_shape)
    other = swap(mine, 1)

    area = float(width * width)
    results = pl.pallas_call(
        functools.partial(update_kernel, area, 12.0 * width * width),
        out_shape=(shape((1, 1)), shape((1, 1))) + tuple(shape(p.shape) for p in params) * 3,
        in_specs=[smem] + [whole] * 27,
        out_specs=(whole,) * 26,
        scratch_shapes=[
            pltpu.VMEM((128, 128), F32),
            pltpu.VMEM((8, 128), F32),
            pltpu.VMEM((9, 6, hidden), F32),
            pltpu.VMEM((9, 12, hidden), F32),
            pltpu.VMEM((288, 128), F32),
            pltpu.VMEM((devices * each, hidden), F32),
        ],
        compiler_params=params_of(26),
        name="update",
    )(place, mine, other, counts, *params, *firsts, *seconds)
    outs = [results[0][0, 0], results[1][0, 0]]
    for k in range(3):
        group = list(results[2 + 8 * k : 10 + 8 * k])
        group[0] = group[0].transpose(0, 2, 1)
        group[3] = group[3].transpose(0, 2, 1)
        outs += group
    return tuple(outs)


def solution(mesh):
    field = P(None, "band", None, "dp")
    return jax.shard_map(
        body,
        mesh=mesh,
        in_specs=(field, field, P("dp")) + (P(),) * 24,
        out_specs=(P(),) * 26,
        check_vma=False,
    )
```

```python
import functools
import math

import jax
import jax.numpy as jnp
from jax import lax
from jax.experimental import pallas as pl
from jax.experimental.pallas import tpu as pltpu
from jax.sharding import PartitionSpec as P

STEP = 10
HIGH = lax.Precision.HIGHEST
LOG_TWO = math.log(2.0)
LOG_TWO_PI = math.log(2.0 * math.pi)
CLIP_NORM = 0.01
RATE = 0.05
BETA_ONE = 0.9
BETA_TWO = 0.999
EPSILON = 1e-08
DECAY = 0.01
BITS = 5.0
F32 = jnp.float32
BF16 = jnp.bfloat16
MIB = 1024 * 1024
VMEM_MIB = 30
NN = (((1,), (0,)), ((), ()))
NT = (((1,), (1,)), ((), ()))
TN = (((0,), (0,)), ((), ()))

ROW_MIX = 0
ROW_OUT = 512
ROW_IN = ROW_OUT + 108
ROW_BIAS = ROW_IN + 54
ROW_PRIOR = ROW_BIAS + 6
ROW_SMALL = ROW_PRIOR + 72
ROWS = ROW_SMALL + 16


def dot(left, right, dims=NN, precision=None):
    return lax.dot_general(left, right, dims, precision=precision, preferred_element_type=F32)


def iota(shape, dim):
    return lax.broadcasted_iota(jnp.int32, shape, dim)


def as_f32(mask):
    return jnp.where(mask, 1.0, 0.0).astype(F32)


def prior_out_map():
    row, col = iota((48, 64), 0), iota((48, 64), 1)
    kind, d, c = col >> 5, (col >> 3) & 3, col & 7
    return as_f32((c < 6) & (row == kind * 24 + 4 * c + d))


def prior_in_map():
    row, col = iota((288, 216), 0), iota((288, 216), 1)
    tap, d, c = row >> 5, (row >> 3) & 3, row & 7
    return as_f32((c < 6) & (col == tap * 24 + 4 * c + d))


def channel_map():
    row, col = iota((16, 128), 0), iota((16, 128), 1)
    return as_f32(((row < 6) & (col == 11 - row)) | ((row >= 8) & (row < 14) & (col == 13 - row)))


def half_map():
    row, col = iota((16, 128), 0), iota((16, 128), 1)
    return as_f32(((row < 6) & (col == row)) | ((row >= 8) & (row < 14) & (col == row - 2)))


def lu_factors(lu):
    row, col = iota((128, 128), 0), iota((128, 128), 1)
    eye = (row == col) & (row < 12)
    lower = jnp.where(row > col, lu, 0.0) + as_f32(eye)
    upper = jnp.where(row < col, lu, 0.0) + jnp.where(eye, jnp.exp(lu), 0.0)
    return lower, upper, eye


def spread_weight(lu, gains):
    lower, upper, _ = lu_factors(lu)
    weight = dot(channel_map(), dot(lower, upper, NN, HIGH), NN, HIGH)
    scaled = weight * jnp.exp(gains[1:2])
    shift = jnp.sum(scaled * gains[0:1], axis=1, keepdims=True)
    return jnp.where(iota((16, 128), 1) == 12, shift, scaled)


def weights_kernel(cin, mix, cout, prior, bias, gains, lu, table,
                   win, wt, mixh, mixth, bias2, wout, woutt, weff, wpt, wp, tablep, net_bias,
                   big, square, strip):
    hidden = mix.shape[0]
    wt[...] = jnp.zeros_like(wt)
    for dy in range(3):
        for dx in range(3):
            wt[pl.ds(dy * 32 + dx * 8, 6), :] = (
                0.5 * cin[dy * 3 + dx]
            ).astype(BF16).astype(F32)
    half = 0.5 * bias[0:1, :]
    first = half.astype(BF16).astype(F32)
    rest = half - first
    second = rest.astype(BF16).astype(F32)
    wt[46:47, :] = first
    wt[38:39, :] = second
    wt[54:55, :] = rest - second
    win[...] = wt[...].T.astype(BF16)
    mixh[...] = (0.5 * mix[...]).astype(BF16)
    mixth[...] = (0.5 * mix[...]).T.astype(BF16)
    bias2[...] = jnp.broadcast_to(0.5 * bias[1:2, :], (128, hidden)).T
    big[...] = jnp.zeros_like(big)
    for tap in range(9):
        big[pl.ds(tap * 16, 6), :] = cout[tap, 0:6, :]
        big[pl.ds(tap * 16 + 8, 6), :] = cout[tap, 6:12, :]
    wout[...] = big[0:144, :].astype(BF16)
    woutt[...] = (0.5 * big[0:256, :]).T.astype(BF16)
    square[...] = jnp.zeros_like(square)
    square[0:12, 0:12] = lu[...]
    strip[...] = jnp.zeros_like(strip)
    strip[0:3, 0:12] = gains[...]
    weff[...] = spread_weight(square[...], strip[0:8, :])
    added = dot(half_map(), strip[...], NT, HIGH)[:, 2:3] + as_f32(iota((16, 1), 0) >= 8) * 2.0
    net_bias[...] = jnp.broadcast_to(added, (16, 128))
    out_map = prior_out_map()
    flat = dot(prior_in_map(), dot(prior[...].reshape(216, 48), out_map, NN, HIGH), NN, HIGH)
    flat_hi = flat.astype(BF16)
    flat_lo = (flat - flat_hi.astype(F32)).astype(BF16)
    wpt[...] = jnp.zeros_like(wpt)
    wpt[:, 0:64] = flat_hi
    wpt[:, 64:128] = flat_lo
    wpt[:, 128:192] = flat_hi
    big[...] = jnp.zeros_like(big)
    big[0:288, 0:64] = flat_hi.astype(F32)
    big[0:288, 64:128] = flat_lo.astype(F32)
    wp[...] = big[0:384, 0:128].T.astype(BF16)
    tablep[...] = jnp.zeros_like(tablep)
    tablep[0:10, 0:64] = dot(table[:, 0:48], out_map, NN, HIGH)
    tablep[0:10, 64:128] = dot(table[:, 48:96], out_map, NN, HIGH)


def hidden_unit(u):
    wide = 1.0 + jnp.tanh(u)
    act = (u * wide).astype(BF16)
    wide = wide.astype(BF16)
    return act, wide + act * (2.0 - wide)


def fill_windows(xaf, r2, half, count, taps_hi, taps_lo=None):
    for w in range(half):
        lanes = pl.ds(w * count, count)
        for ty in range(3):
            for tx in range(3):
                for dy in range(2):
                    er, ec = 2 * r2 + 2 * ty + dy, 2 * w + 2 * tx
                    pair = jnp.concatenate([xaf[er, ec], xaf[er, ec + 1]], axis=0)
                    high = pair.astype(BF16)
                    at = pl.ds((ty * 3 + tx) * 32 + dy * 16, 16)
                    taps_hi[at, lanes] = high
                    if taps_lo is not None:
                        taps_lo[at, lanes] = (pair - high.astype(F32)).astype(BF16)


def forward_kernel(cols, sub, images, noise, top, bottom, flags, weff, win, mixh, bias2, wout, wp, labels,
                   act1, sg1, act2, sg2, xa2, xt, xaf, xbf, nn, edge_top, edge_bottom, stats,
                   xs, taps, acc, taps_hi, taps_lo):
    step = pl.program_id(0)
    rows, width, count = images.shape[1:]
    groups = width // cols

    @pl.when(step == 0)
    def _():
        xs[:, 0:2] = top[...].astype(F32)
        xs[:, 2 : rows + 2] = images[...] + noise[...]
        xs[:, rows + 2 : rows + 4] = bottom[...].astype(F32)
        xaf[...] = jnp.zeros_like(xaf)
        xt[...] = jnp.zeros_like(xt)
        acc[...] = jnp.zeros_like(acc)
        row8 = iota((8, count), 0)
        ones = jnp.where((iota((16, count), 0) & 7) == 6, 1.0, 0.0)
        col_a = [jnp.broadcast_to(weff[0:8, c : c + 1], (8, count)) for c in range(13)]
        col_b = [jnp.broadcast_to(weff[8:16, c : c + 1], (8, count)) for c in range(13)]

        def per_row(er, carry):
            own = (er >= 2) & (er < rows + 2)
            valid = jnp.where(er < 2, flags[0], jnp.where(er >= rows + 2, flags[1], 1.0))
            inner = jnp.clip(er - 2, 0, rows - 1)
            before = jnp.zeros((8, count), F32)
            for c in range(width):
                a, b = col_a[12], col_b[12]
                t0 = jnp.zeros((8, count), F32)
                t1 = jnp.where(row8 == 4, valid, 0.0)
                for ch in range(12):
                    x = jnp.broadcast_to(xs[ch, er, c : c + 1, :], (8, count))
                    a = a + col_a[ch] * x
                    b = b + col_b[ch] * x
                    if ch < 8:
                        t0 = jnp.where(row8 == ch, x, t0)
                    else:
                        t1 = jnp.where(row8 == ch - 8, x, t1)
                a = a * valid
                xaf[er, c + 2] = a
                xa2[er, c] = (jnp.concatenate([before, a], axis=0) + ones).astype(BF16)
                before = a
                xt[er, c + 1] = jnp.concatenate([t0, t1], axis=0).astype(BF16)

                @pl.when(own)
                def _():
                    xbf[inner, c] = b

            last = jnp.concatenate([before, jnp.zeros((8, count), F32)], axis=0)
            xa2[er, width] = (last + ones).astype(BF16)
            xa2[er, width + 1] = ones.astype(BF16)
            return carry

        lax.fori_loop(0, rows + 4, per_row, 0)

        def per_pair(r2, carry):
            fill_windows(xaf, r2, width // 2, count, taps_hi, taps_lo)
            main = dot(wp[:, 0:288], taps_hi[...])
            stats[r2] = main[0:64] + main[64:128] + dot(wp[0:64, 0:288], taps_lo[...])
            return carry

        lax.fori_loop(0, rows // 2, per_pair, 0)

    row = step // groups
    start = (step % groups) * cols
    for i in range(cols):
        lanes = pl.ds(i * count, count)
        for dy in range(3):
            for j in range(2):
                taps[pl.ds((dy * 2 + j) * 16, 16), lanes] = xa2[row + 1 + dy, start + i + 2 * j]
        taps[96:112, lanes] = xt[row + 2, start + i + 1]
        taps[112:128, lanes] = xt[row + 2, start + i + 1]
    size = sub * count
    for s in range(cols // sub):
        lanes = pl.ds(s * size, size)
        one, slope1 = hidden_unit(dot(win[...], taps[:, lanes]))
        act1[0, :, lanes] = one
        sg1[0, :, lanes] = slope1
        bias = jnp.concatenate([bias2[...]] * (size // 128), axis=1)
        two, slope2 = hidden_unit(dot(mixh[...], one) + bias)
        act2[0, :, lanes] = two
        sg2[0, :, lanes] = slope2
        out = dot(wout[...], two)
        for dy in range(3):
            for k in range(sub + 2):
                value = None
                for dx in range(3):
                    i = k + dx - 2
                    if 0 <= i < sub:
                        at = 16 * (dy * 3 + dx)
                        part = out[at : at + 16, i * count : (i + 1) * count]
                        value = part if value is None else value + part
                acc[row + 2 - dy, start + s * sub + k] += value

    @pl.when(step == rows * groups - 1)
    def _():
        nn[...] = acc[1 : rows + 1, 1 : width + 1]
        edge_top[...] = acc[0, 1 : width + 1].astype(BF16)
        edge_bottom[...] = acc[rows + 1, 1 : width + 1].astype(BF16)


def coupling_kernel(dims, nn, edge_top, edge_bottom, xbf, stats, labels, everyone, tablep, net_bias,
                    dn, dn_first, dn_last, dstats, dxb, loss_acc, per_image, counts):
    rows, width, _, count = nn.shape
    half = width // 2
    hot = as_f32(iota((16, count), 0) == jnp.broadcast_to(labels[...], (16, count)))
    seen = jnp.zeros((16, count), F32)
    for k in range(everyone.shape[0]):
        same = iota((16, count), 0) == jnp.broadcast_to(everyone[k : k + 1, :], (16, count))
        seen = seen + as_f32(same)
    number = jnp.broadcast_to(jnp.sum(seen, axis=1, keepdims=True), (16, 128))
    counts[...] = number
    scale16 = 1.0 / (10.0 * jnp.maximum(number, 1.0) * (dims * LOG_TWO))
    coef = jnp.sum(hot * scale16[:, 0:1], axis=0, keepdims=True)
    coef = jnp.broadcast_to(coef, (8, count))
    cls = dot(tablep[...], hot, TN, HIGH)
    per_image[0:128, :] = cls
    per_image[128:136, :] = coef
    per_image[136:152, :] = hot
    bias_a = jnp.broadcast_to(net_bias[0:8, 0:1], (8, count))
    bias_b = jnp.broadcast_to(net_bias[8:16, 0:1], (8, count))
    loss = jnp.zeros((8, count), F32)
    for r2 in range(rows // 2):
        for w in range(half):
            lanes = pl.ds(w * count, count)
            for dy in range(2):
                pair = []
                for dx in range(2):
                    d = 2 * dy + dx
                    r, c = 2 * r2 + dy, 2 * w + dx
                    tile = nn[r, c]
                    if r == 0:
                        tile = tile + edge_top[c].astype(F32)
                    if r == rows - 1:
                        tile = tile + edge_bottom[c].astype(F32)
                    raw = tile[8:16] + bias_b
                    sig = jax.nn.sigmoid(raw)
                    log_sig = jnp.minimum(raw, 0.0) - jnp.log(1.0 + jnp.exp(-jnp.abs(raw)))
                    base = xbf[r, c] + tile[0:8] + bias_a
                    logs = stats[r2, pl.ds(32 + 8 * d, 8), lanes] + cls[32 + 8 * d : 40 + 8 * d]
                    diff = base * sig - (stats[r2, pl.ds(8 * d, 8), lanes] + cls[8 * d : 8 * d + 8])
                    weighted = diff * jnp.exp(-2.0 * logs)
                    quad = diff * weighted
                    loss = loss + (log_sig - 0.5 * (LOG_TWO_PI + 2.0 * logs + quad))
                    dv = coef * weighted
                    dstats[r2, pl.ds(8 * d, 8), lanes] = -dv
                    dstats[r2, pl.ds(32 + 8 * d, 8), lanes] = coef - coef * quad
                    passed = dv * sig
                    pair.append(passed)
                    draw = (passed * base - coef) * (1.0 - sig)
                    dn[r, c] = jnp.concatenate([passed, draw], axis=0).astype(BF16)
                dxb[2 * r2 + dy, w] = jnp.concatenate(pair, axis=0).astype(BF16)
    loss_acc[...] = loss
    dn_first[...] = dn[0]
    dn_last[...] = dn[rows - 1]


def prior_kernel(dn, dstats, dxb, loss_part, xaf, xt, per_image, wpt,
                 dprior, small, taps_hi, dtaps, dxa, table_acc):
    rows, width, _, count = dn.shape
    half = width // 2
    cls = per_image[0:128, :]
    coef = per_image[128:136, :]
    hot = per_image[136:152, :]
    weight_grad = None
    for r2 in range(rows // 2):
        fill_windows(xaf, r2, half, count, taps_hi)
        grads = dstats[r2]
        high = grads.astype(BF16)
        low = (grads - high.astype(F32)).astype(BF16)
        part = dot(taps_hi[...], high, NT)
        weight_grad = part if weight_grad is None else weight_grad + part
        dtaps[r2] = dot(wpt[:, 0:192], jnp.concatenate([high, high, low], axis=0))
    dprior[...] = jnp.zeros_like(dprior)
    dprior[:, 0:64] = weight_grad
    for k in range(8):
        rows8 = pl.ds(8 * k, 8)
        value = jnp.zeros((8, count), F32)
        for r2 in range(rows // 2):
            for w in range(half):
                value = value + dstats[r2, rows8, pl.ds(w * count, count)]
        table_acc[rows8, :] = value
    gain = jnp.zeros((16, count), F32)
    loss = loss_part[...]
    means = [jnp.zeros((8, count), F32)] * 4
    scales = [jnp.zeros((8, count), F32)] * 4
    for er in range(rows + 4):
        for pair in range(half):
            both = []
            for dx in range(2):
                c = 2 * pair + dx
                value = None
                for r2 in range(rows // 2):
                    ey = er - 2 * r2
                    for w in range(half):
                        ex = c + 2 - 2 * w
                        if 0 <= ey < 6 and 0 <= ex < 6:
                            at = ((ey // 2) * 3 + ex // 2) * 32 + (ey % 2) * 16 + (ex % 2) * 8
                            part = dtaps[r2, pl.ds(at, 8), pl.ds(w * count, count)]
                            value = part if value is None else value + part
                r = er - 2
                if 0 <= r < rows:
                    d = 2 * (r % 2) + dx
                    gain = gain + dn[r, c].astype(F32)
                    logs = cls[96 + 8 * d : 104 + 8 * d]
                    diff = xaf[er, c + 2] - cls[64 + 8 * d : 72 + 8 * d]
                    weighted = diff * jnp.exp(-2.0 * logs)
                    quad = diff * weighted
                    loss = loss - 0.5 * (LOG_TWO_PI + 2.0 * logs + quad)
                    dv = coef * weighted
                    means[d] = means[d] - dv
                    scales[d] = scales[d] + (coef - coef * quad)
                    value = value + dv
                both.append(value)
            dxa[er, pair] = jnp.concatenate(both, axis=0).astype(BF16)
    for d in range(4):
        table_acc[pl.ds(64 + 8 * d, 8), :] = means[d]
        table_acc[pl.ds(96 + 8 * d, 8), :] = scales[d]
    outer = jnp.zeros((width * 8, width * 16), F32)
    inner = jnp.zeros((width * 8, width * 16), F32)
    for er in range(rows + 4):
        field = xt[er, 1 : width + 1].reshape(width * 16, count)
        outer = outer + dot(dxa[er].reshape(width * 8, count), field, NT)
        if 2 <= er < rows + 2:
            inner = inner + dot(dxb[er - 2].reshape(width * 8, count), field, NT)
    total = jnp.concatenate([outer, inner], axis=0)
    row, col = iota((256, 256), 0), iota((256, 256), 1)
    masked = jnp.where(((row & 127) >> 3) == (col >> 4), total, 0.0)
    wide = iota((16, 256), 1)
    gather = as_f32(iota((16, 256), 0) == (wide & 7) + 8 * (wide >> 7))
    fold = as_f32((iota((256, 128), 0) & 15) == iota((256, 128), 1))
    small[...] = jnp.zeros_like(small)
    small[:, 128:256] = dot(dot(gather, masked, NN, HIGH), fold, NN, HIGH)
    small[:, 0:128] = dot(hot, table_acc[...], NT, HIGH)
    lone = jnp.ones((8, count), F32)
    small[0:8, 256:384] = dot(dot(lone, gain, NT, HIGH), half_map(), NN, HIGH)
    value = jnp.where(iota((8, count), 0) < 6, loss * coef, 0.0)
    value = jnp.sum(jnp.sum(value, axis=0, keepdims=True), axis=1, keepdims=True)
    small[8:16, 256:384] = jnp.broadcast_to(-value, (8, 128))


def backward_kernel(cols, sub, act1, sg1, act2, sg2, place, dn, dn_top, dn_bottom, xa2, xt, mixth, woutt, wt,
                    dprior, small, keep, send, packed, dnp, taps, gtaps, bias_acc, wfield, gout, gin):
    step = pl.program_id(0)
    rows, width, _, count = dn.shape
    groups = width // cols

    @pl.when(step == 0)
    def _():
        packed[...] = jnp.zeros_like(packed)
        gout[...] = jnp.zeros_like(gout)
        gin[...] = jnp.zeros_like(gin)
        bias_acc[...] = jnp.zeros_like(bias_acc)
        wfield[...] = jnp.zeros_like(wfield)
        dnp[...] = jnp.zeros_like(dnp)
        dnp[0, 1 : width + 1] = dn_top[...]
        dnp[1 : rows + 1, 1 : width + 1] = dn[...]
        dnp[rows + 1, 1 : width + 1] = dn_bottom[...]
        taps[240:256, :] = jnp.zeros_like(taps[240:256, :])
        gtaps[144:256, :] = jnp.zeros_like(gtaps[144:256, :])

    row = step // groups
    start = (step % groups) * cols
    for i in range(cols):
        lanes = pl.ds(i * count, count)
        for dy in range(3):
            for j in range(2):
                taps[pl.ds((dy * 2 + j) * 16, 16), lanes] = xa2[row + 1 + dy, start + i + 2 * j]
            for dx in range(3):
                tap = dy * 3 + dx
                taps[pl.ds(96 + tap * 16, 16), lanes] = xt[row + 1 + dy, start + i + dx]
                gtaps[pl.ds(tap * 16, 16), lanes] = dnp[row + 2 - dy, start + i + 2 - dx]
    size = sub * count
    for s in range(cols // sub):
        lanes = pl.ds(s * size, size)
        grad2 = (dot(woutt[...], gtaps[:, lanes]) * sg2[0, :, lanes].astype(F32)).astype(BF16)
        grad1 = (dot(mixth[...], grad2) * sg1[0, :, lanes].astype(F32)).astype(BF16)
        wide = grad2.astype(F32)
        bias = wide[:, 0:128]
        for k in range(1, size // 128):
            bias = bias + wide[:, k * 128 : (k + 1) * 128]
        bias_acc[...] += bias
        gout[...] += dot(gtaps[0:144, lanes], act2[0, :, lanes], NT)
        packed[ROW_MIX:ROW_OUT, :] += dot(grad2, act1[0, :, lanes], NT)
        gathered = dot(taps[0:240, lanes], grad1, NT)
        gin[...] += gathered[0:96]
        wfield[...] += gathered[96:240]

    @pl.when(step == rows * groups - 1)
    def _():
        for tap in range(9):
            at = ROW_OUT + 12 * tap
            packed[at : at + 6, :] = gout[16 * tap : 16 * tap + 6, :]
            packed[at + 6 : at + 12, :] = gout[16 * tap + 8 : 16 * tap + 14, :]
            at = ROW_IN + 6 * tap
            from_row = (tap // 3) * 32 + (tap % 3) * 8
            packed[at : at + 6, :] = gin[from_row : from_row + 6, :]
        packed[ROW_BIAS : ROW_BIAS + 1, :] = gin[46:47, :]
        lone = jnp.ones((8, 128), F32)
        packed[ROW_BIAS + 1 : ROW_BIAS + 2, :] = dot(lone, bias_acc[...], NT, HIGH)[0:1]
        for k in range(4):
            packed[ROW_PRIOR:ROW_SMALL, 128 * k : 128 * k + 128] = dprior[72 * k : 72 * k + 72, :]
        packed[ROW_SMALL:ROWS, :] = small[...]
        cross = dot(wt[0:96, :], wfield[...], NT, HIGH)
        row, col = iota((96, 144), 0), iota((96, 144), 1)
        slot = (row >> 3) & 3
        same = (slot < 3) & ((row >> 5) * 3 + slot == col >> 4) & ((row & 7) < 6)
        gather = as_f32(iota((8, 96), 0) == (iota((8, 96), 1) & 7))
        fold = as_f32((iota((144, 128), 0) & 15) == iota((144, 128), 1))
        field_terms = dot(dot(gather, jnp.where(same, cross, 0.0), NN, HIGH), fold, NN, HIGH)
        packed[ROW_SMALL : ROW_SMALL + 8, 128:256] += 2.0 * field_terms
        chunks, each = keep.shape[:2]
        core = place[0]
        for k in range(2 * chunks):
            block = chunk_of(packed, k, each)
            mine = core == k // chunks

            @pl.when(mine)
            def _():
                keep[k % chunks] = block

            @pl.when(jnp.logical_not(mine))
            def _():
                send[k % chunks] = to_wire(block)


def chunk_of(packed, k, each):
    plain, fine = 2 * each // 3, each // 3
    return jnp.concatenate(
        [
            packed[k * plain : (k + 1) * plain, :],
            packed[ROW_OUT + k * fine : ROW_OUT + (k + 1) * fine, :],
        ],
        axis=0,
    )


def to_wire(block):
    axis = block.ndim - 2
    each = block.shape[axis]
    plain = lax.slice_in_dim(block, 0, 2 * each // 3, axis=axis)
    fine = lax.slice_in_dim(block, 2 * each // 3, each, axis=axis)
    high = fine.astype(BF16).astype(F32)
    return jnp.concatenate([plain, high, fine - high], axis=axis).astype(BF16)


def from_wire(wire):
    axis = wire.ndim - 2
    part = wire.shape[axis] // 4
    wide = wire.astype(F32)
    fine = lax.slice_in_dim(wide, 2 * part, 3 * part, axis=axis)
    fine = fine + lax.slice_in_dim(wide, 3 * part, 4 * part, axis=axis)
    return jnp.concatenate([lax.slice_in_dim(wide, 0, 2 * part, axis=axis), fine], axis=axis)


def halve_kernel(place, keep, got, mine, *sends):
    count = len(sends) + 1
    bands = keep.shape[0] // count
    here = place[1]
    for m in range(count):
        for b in range(bands):
            at = (here ^ m) * bands + b
            value = keep[at] + from_wire(got[at])
            if m == 0:
                mine[b] = value
            else:
                sends[m - 1][b] = to_wire(value)


def spread_kernel(place, bands, first, *refs):
    gots, mine, sends = refs[:-bands], refs[-bands], refs[1 - bands :]
    here = place[2]
    for k in range(bands):
        at = lax.rem(here + k, bands)
        value = first[at]
        for got in gots:
            value = value + from_wire(got[at])
        if k == 0:
            mine[...] = value
        else:
            sends[k - 1][...] = to_wire(value)


def sum_kernel(mine, *refs):
    value = mine[...]
    for ref in refs[:-1]:
        value = value + from_wire(ref[...])
    refs[-1][...] = to_wire(value)


def gather_kernel(place, which, xor, mine, *refs):
    out = refs[-1]
    here = place[which]
    count = len(refs)
    for k in range(count):
        at = (here ^ k) if xor else lax.rem(here - k + count, count)
        out[at] = (mine if k == 0 else refs[k - 1])[...]


def adamw(weight, first, second, grad, out, out_first, out_second, at=Ellipsis):
    first_new = BETA_ONE * first[at] + (1.0 - BETA_ONE) * grad
    second_new = BETA_TWO * second[at] + (1.0 - BETA_TWO) * grad * grad
    first_hat = first_new / (1.0 - BETA_ONE**STEP)
    second_hat = second_new / (1.0 - BETA_TWO**STEP)
    out[at] = weight[at] - RATE * (
        first_hat / (jnp.sqrt(second_hat) + EPSILON) + DECAY * weight[at]
    )
    out_first[at] = first_new
    out_second[at] = second_new


def update_kernel(area, dims, *refs):
    place, own, other, counts = refs[:4]
    refs = refs[4:]
    params, firsts, seconds = refs[:8], refs[8:16], refs[16:24]
    loss, norm = refs[24:26]
    news, new_firsts, new_seconds = refs[26:34], refs[34:42], refs[42:50]
    square, strip, gin, gout, flat, grads = refs[50:]
    chunks = own.shape[0]
    fine = own.shape[1] // 4
    for k in range(2 * chunks):
        mine = place[0] == k // chunks
        block = from_wire(jnp.where(mine, own[k % chunks], other[k % chunks]))
        grads[2 * k * fine : 2 * (k + 1) * fine, :] = block[0 : 2 * fine]
        grads[ROW_OUT + k * fine : ROW_OUT + (k + 1) * fine, :] = block[2 * fine :]
    bias, gains_ref, lu_ref = params[4:7]
    hidden = grads.shape[1]
    square[...] = jnp.zeros_like(square)
    square[0:12, 0:12] = lu_ref[...]
    strip[...] = jnp.zeros_like(strip)
    strip[0:3, 0:12] = gains_ref[...]
    gains = strip[...]
    lower, upper, eye = lu_factors(square[...])
    weight = spread_weight(square[...], gains)
    field = grads[ROW_SMALL:ROWS, 128:256]
    lane = iota((16, 128), 1)
    level = jnp.sum(jnp.where(lane == 12, field, 0.0), axis=1, keepdims=True)
    real = iota((16, 128), 0) & 7
    moved = jnp.where((lane < 12) & (real < 6), field + level * gains[0:1], 0.0)
    level = jnp.where(real < 6, level, 0.0)
    number = counts[...]
    present = number / jnp.maximum(number, 1.0)
    share = jnp.sum(present[:, 0:1], axis=0, keepdims=True)
    coef = share * (1.0 / (10.0 * dims * LOG_TWO)) * area
    weight = jnp.where(lane < 12, weight, 0.0)
    d_shift = jnp.sum(weight * level, axis=0, keepdims=True)
    d_scale = jnp.sum(weight * moved, axis=0, keepdims=True) - coef
    d_product = dot(channel_map(), moved * jnp.exp(gains[1:2]), TN, HIGH)
    d_lower = dot(d_product, upper, NT, HIGH)
    d_upper = dot(lower, d_product, TN, HIGH)
    row, col = iota((128, 128), 0), iota((128, 128), 1)
    d_lu = jnp.where(row > col, d_lower, 0.0) + jnp.where(row < col, d_upper, 0.0)
    d_lu = d_lu + jnp.where(eye, d_upper * jnp.exp(square[...]) - coef, 0.0)
    d_lu = jnp.where((row < 12) & (col < 12), d_lu, 0.0)
    diag = jnp.sum(jnp.sum(jnp.where(eye, square[...], 0.0), axis=0, keepdims=True), axis=1, keepdims=True)
    logs = jnp.sum(jnp.where(lane[0:1] < 12, gains[1:2], 0.0), axis=1, keepdims=True)
    d_bias_out = grads[ROW_SMALL : ROW_SMALL + 1, 256:384]
    row8 = iota((8, 128), 0)
    d_gains = jnp.where(row8 == 0, d_shift, jnp.where(row8 == 1, d_scale, jnp.where(row8 == 2, d_bias_out, 0.0)))
    d_gains = jnp.where(iota((8, 128), 1) < 12, d_gains, 0.0)
    for tap in range(9):
        gin[tap] = grads[ROW_IN + 6 * tap : ROW_IN + 6 * tap + 6, :]
        gout[tap] = grads[ROW_OUT + 12 * tap : ROW_OUT + 12 * tap + 12, :]
    for k in range(4):
        flat[72 * k : 72 * k + 72, :] = grads[ROW_PRIOR:ROW_SMALL, 128 * k : 128 * k + 128]
    out_map = prior_out_map()
    d_prior = dot(dot(prior_in_map(), flat[...], TN, HIGH)[:, 0:64], out_map, NT, HIGH)
    d_table = grads[ROW_SMALL:ROWS, 0:128]
    d_table = [dot(d_table[:, 0:64], out_map, NT, HIGH), dot(d_table[:, 64:128], out_map, NT, HIGH)]
    d_table = [part[0:10] for part in d_table]
    d_bias = [grads[ROW_BIAS : ROW_BIAS + 1, :], grads[ROW_BIAS + 1 : ROW_BIAS + 2, :]]
    d_mix = grads[0:ROW_OUT, :]

    def squares(value):
        value = value * value
        if value.ndim == 3:
            value = jnp.sum(value, axis=0)
        return jnp.sum(jnp.sum(value, axis=0, keepdims=True), axis=1, keepdims=True)

    squared = squares(d_mix) + squares(gin[...]) + squares(gout[...]) + squares(d_prior)
    squared = squared + squares(d_bias[0]) + squares(d_bias[1]) + squares(d_gains) + squares(d_lu)
    squared = squared + squares(d_table[0]) + squares(d_table[1])
    total_norm = jnp.sqrt(squared)
    factor = jnp.minimum(1.0, CLIP_NORM / (total_norm + 1e-06))
    norm[...] = total_norm
    loss[...] = (
        grads[ROW_SMALL + 8 : ROW_SMALL + 9, 256:257] - coef * (logs + diag) + BITS * share / 10.0
    )

    def put(k, grad, at=Ellipsis):
        adamw(params[k], firsts[k], seconds[k], grad, news[k], new_firsts[k], new_seconds[k], at)

    put(0, factor * gin[...])
    put(1, factor * d_mix)
    put(2, factor * gout[...])
    put(3, (factor * d_prior).reshape(9, 24, 48))
    put(4, factor * d_bias[0], (slice(0, 1), slice(None)))
    put(4, factor * d_bias[1], (slice(1, 2), slice(None)))
    put(5, (factor * d_gains)[0:3, 0:12])
    put(6, (factor * d_lu)[0:12, 0:12])
    put(7, factor * d_table[0], (slice(None), slice(0, 48)))
    put(7, factor * d_table[1], (slice(None), slice(48, 96)))


def shape(dims, dtype=F32):
    return jax.ShapeDtypeStruct(dims, dtype)


def near(dims, dtype=F32):
    return pltpu.HBM(dims, dtype)


def far(array):
    return pltpu.with_memory_space_constraint(array, pltpu.HBM)


def params_of(limit):
    return pltpu.CompilerParams(vmem_limit_bytes=limit * MIB)


def exchange_rows(up, down):
    count = lax.axis_size("band")
    before = lax.ppermute(down, "band", [(i, i + 1) for i in range(count - 1)])
    after = lax.ppermute(up, "band", [(i + 1, i) for i in range(count - 1)])
    return before, after


def body(images, noise, labels, *rest):
    params, firsts, seconds = (list(rest[8 * k : 8 * k + 8]) for k in range(3))
    for group in (params, firsts, seconds):
        group[0] = group[0].transpose(0, 2, 1)
        group[3] = group[3].transpose(0, 2, 1)
    chans, rows, width, count = images.shape
    hidden = params[1].shape[0]
    band = lax.axis_index("band")
    bands = lax.axis_size("band")
    whole = pl.BlockSpec(memory_space=pltpu.VMEM)

    top, bottom = exchange_rows(
        (images[:, :2] + noise[:, :2]).astype(BF16),
        (images[:, rows - 2 :] + noise[:, rows - 2 :]).astype(BF16),
    )
    everyone = jnp.broadcast_to(labels[None, :], (lax.axis_size("dp"), count))
    everyone = lax.all_to_all(everyone, "dp", 0, 0, tiled=True)
    flags = jnp.stack([band > 0, band < bands - 1]).astype(F32)
    dp = lax.axis_index("dp")
    place = jnp.stack([dp & 1, dp >> 1, band]).astype(jnp.int32)
    smem = pl.BlockSpec(memory_space=pltpu.SMEM)
    win, wt, mixh, mixth, bias2, wout, woutt, weff, wpt, wp, tablep, net_bias = pl.pallas_call(
        weights_kernel,
        out_shape=(
            near((hidden, 128), BF16),
            near((128, hidden)),
            near((hidden, hidden), BF16),
            near((hidden, hidden), BF16),
            near((hidden, 128)),
            near((144, hidden), BF16),
            near((hidden, 256), BF16),
            near((16, 128)),
            near((288, 256), BF16),
            near((128, 384), BF16),
            near((16, 128)),
            near((16, 128)),
        ),
        in_specs=[whole] * 8,
        out_specs=(whole,) * 12,
        scratch_shapes=[
            pltpu.VMEM((512, hidden), F32),
            pltpu.VMEM((128, 128), F32),
            pltpu.VMEM((8, 128), F32),
        ],
        compiler_params=params_of(VMEM_MIB),
        name="weights",
    )(*[far(p) for p in params])

    cols, sub = 4, 4
    pixels = (width // 2) * count
    groups = width // cols
    steps = rows * groups
    size = cols * count
    chunk = pl.BlockSpec((1, hidden, size), lambda i: (i, 0, 0))
    ext = (rows + 4, width + 2, 16, count)
    exta = (rows + 4, width + 4, 8, count)
    act1, sg1, act2, sg2, xa2, xt, xaf, xbf, nn, edge_top, edge_bottom, stats = pl.pallas_call(
        functools.partial(forward_kernel, cols, sub),
        grid=(steps,),
        out_shape=(pltpu.HBM((steps, hidden, size), BF16),) * 4
        + (
            near(ext, BF16),
            near(ext, BF16),
            near(exta),
            near((rows, width, 8, count)),
            near((rows, width, 16, count)),
            near((width, 16, count), BF16),
            near((width, 16, count), BF16),
            near((rows // 2, 64, pixels)),
        ),
        in_specs=[whole] * 4 + [smem] + [whole] * 7,
        out_specs=(chunk,) * 4 + (whole,) * 8,
        scratch_shapes=[
            pltpu.VMEM((chans, rows + 4, width, count), F32),
            pltpu.VMEM((128, size), BF16),
            pltpu.VMEM((rows + 2, width + 2, 16, count), F32),
            pltpu.VMEM((288, pixels), BF16),
            pltpu.VMEM((288, pixels), BF16),
        ],
        compiler_params=params_of(VMEM_MIB),
        cost_estimate=pl.CostEstimate(
            flops=2 * rows * width * count * hidden * (hidden + 272),
            transcendentals=2 * rows * width * count * hidden,
            bytes_accessed=8 * rows * width * count * hidden,
        ),
        name="forward",
    )(far(images), far(noise), top, bottom, flags, *map(far, (weff, win, mixh, bias2, wout, wp)), everyone)

    got_top, got_bottom = exchange_rows(edge_top, edge_bottom)
    def local(kernel, name, outs, scratch, *inputs):
        return pl.pallas_call(
            kernel,
            out_shape=outs,
            in_specs=[whole for _ in inputs],
            out_specs=tuple(whole for _ in outs),
            scratch_shapes=scratch,
            compiler_params=params_of(VMEM_MIB),
            name=name,
        )(*[a if a is got_top or a is got_bottom else far(a) for a in inputs])

    dn, dn_first, dn_last, dstats, dxb, loss_part, per_image, counts = local(
        functools.partial(coupling_kernel, 12.0 * width * width),
        "coupling",
        (
            near((rows, width, 16, count), BF16),
            near((width, 16, count), BF16),
            near((width, 16, count), BF16),
            near((rows // 2, 64, pixels)),
            near((rows, width // 2, 16, count), BF16),
            near((8, count)),
            near((152, count)),
            near((16, 128)),
        ),
        [],
        nn,
        got_top,
        got_bottom,
        xbf,
        stats,
        labels[None, :],
        everyone,
        tablep,
        net_bias,
    )
    dprior, small = local(
        prior_kernel,
        "prior_grads",
        (near((288, 128)), near((16, 512))),
        [
            pltpu.VMEM((288, pixels), BF16),
            pltpu.VMEM((rows // 2, 288, pixels), F32),
            pltpu.VMEM((rows + 4, width // 2, 16, count), BF16),
            pltpu.VMEM((128, count), F32),
        ],
        dn,
        dstats,
        dxb,
        loss_part,
        xaf,
        xt,
        per_image,
        wpt,
    )

    dn_top, dn_bottom = exchange_rows(dn_first, dn_last)
    both = ("dp", "band")
    devices = lax.axis_size(both)
    each = ROWS // devices
    wires = each + each // 3
    half_shape = (devices // 2, each, hidden)
    keep, send = pl.pallas_call(
        functools.partial(backward_kernel, cols, sub),
        grid=(steps,),
        out_shape=(near(half_shape), near((devices // 2, wires, hidden), BF16)),
        in_specs=[chunk] * 4 + [smem] + [whole] * 10,
        out_specs=(whole,) * 2,
        scratch_shapes=[
            pltpu.VMEM((devices * each, hidden), F32),
            pltpu.VMEM((rows + 2, width + 2, 16, count), BF16),
            pltpu.VMEM((256, size), BF16),
            pltpu.VMEM((256, size), BF16),
            pltpu.VMEM((hidden, 128), F32),
            pltpu.VMEM((144, hidden), F32),
            pltpu.VMEM((144, hidden), F32),
            pltpu.VMEM((96, hidden), F32),
        ],
        compiler_params=params_of(VMEM_MIB),
        name="backward",
    )(*map(far, (act1, sg1, act2, sg2)), place, far(dn), dn_top, dn_bottom, *map(far, (xa2, xt, mixth, woutt, wt, dprior, small)))

    def call(kernel, name, outs, *inputs):
        return pl.pallas_call(
            kernel,
            out_shape=outs,
            in_specs=[smem if a is place else whole for a in inputs],
            out_specs=jax.tree.map(lambda _: whole, outs),
            compiler_params=params_of(VMEM_MIB),
            name=name,
        )(*inputs)

    def swap(array, mask):
        pairs = [(i, i ^ mask) for i in range(groups_dp)]
        return lax.ppermute(array, "dp", pairs)

    def turn(array, k):
        return lax.ppermute(array, "band", [(i, (i + k) % bands) for i in range(bands)])

    groups_dp = lax.axis_size("dp")
    chips = groups_dp // 2
    got = swap(send, 1)
    block = shape((bands, wires, hidden), BF16)
    tile = shape((wires, hidden), BF16)
    mine, *sends = call(
        halve_kernel, "halve", (shape((bands, each, hidden)),) + (block,) * (chips - 1), place, far(keep), got
    )
    gots = [swap(a, 2 * (m + 1)) for m, a in enumerate(sends)]
    mine, *sends = call(
        lambda p, *refs: spread_kernel(p, bands, *refs),
        "spread",
        (shape((each, hidden)),) + (tile,) * (bands - 1),
        place,
        mine,
        *gots,
    )
    gots = [turn(a, k + 1) for k, a in enumerate(sends)]
    mine = call(sum_kernel, "total", tile, mine, *gots)
    gots = [turn(mine, k + 1) for k in range(bands - 1)]
    mine = call(
        lambda p, *refs: gather_kernel(p, 2, False, *refs), "gather_band", block, place, mine, *gots
    )
    gots = [swap(mine, 2 * (m + 1)) for m in range(chips - 1)]
    mine = call(
        lambda p, *refs: gather_kernel(p, 1, True, *refs),
        "gather_chips",
        shape((chips,) + block.shape, BF16),
        place,
        mine,
        *gots,
    )
    mine = mine.reshape((devices // 2, wires, hidden))
    other = swap(mine, 1)

    area = float(width * width)
    results = pl.pallas_call(
        functools.partial(update_kernel, area, 12.0 * width * width),
        out_shape=(shape((1, 1)), shape((1, 1))) + tuple(shape(p.shape) for p in params) * 3,
        in_specs=[smem] + [whole] * 27,
        out_specs=(whole,) * 26,
        scratch_shapes=[
            pltpu.VMEM((128, 128), F32),
            pltpu.VMEM((8, 128), F32),
            pltpu.VMEM((9, 6, hidden), F32),
            pltpu.VMEM((9, 12, hidden), F32),
            pltpu.VMEM((288, 128), F32),
            pltpu.VMEM((devices * each, hidden), F32),
        ],
        compiler_params=params_of(VMEM_MIB),
        name="update",
    )(place, mine, other, counts, *params, *firsts, *seconds)
    outs = [results[0][0, 0], results[1][0, 0]]
    for k in range(3):
        group = list(results[2 + 8 * k : 10 + 8 * k])
        group[0] = group[0].transpose(0, 2, 1)
        group[3] = group[3].transpose(0, 2, 1)
        outs += group
    return tuple(outs)


def solution(mesh):
    field = P(None, "band", None, "dp")
    return jax.shard_map(
        body,
        mesh=mesh,
        in_specs=(field, field, P("dp")) + (P(),) * 24,
        out_specs=(P(),) * 26,
        check_vma=False,
    )
```

```python
import functools
import math

import jax
import jax.numpy as jnp
from jax import lax
from jax.experimental import pallas as pl
from jax.experimental.pallas import tpu as pltpu
from jax.sharding import PartitionSpec as P

STEP = 10
HIGH = lax.Precision.HIGHEST
LOG_TWO = math.log(2.0)
LOG_TWO_PI = math.log(2.0 * math.pi)
CLIP_NORM = 0.01
RATE = 0.05
BETA_ONE = 0.9
BETA_TWO = 0.999
EPSILON = 1e-08
DECAY = 0.01
BITS = 5.0
F32 = jnp.float32
BF16 = jnp.bfloat16
MIB = 1024 * 1024
VMEM_MIB = 46
NN = (((1,), (0,)), ((), ()))
NT = (((1,), (1,)), ((), ()))
TN = (((0,), (0,)), ((), ()))

ROW_MIX = 0
ROW_OUT = 512
ROW_IN = ROW_OUT + 108
ROW_BIAS = ROW_IN + 54
ROW_PRIOR = ROW_BIAS + 6
ROW_SMALL = ROW_PRIOR + 72
ROWS = ROW_SMALL + 16


def dot(left, right, dims=NN, precision=None):
    return lax.dot_general(left, right, dims, precision=precision, preferred_element_type=F32)


def thirds(value):
    high = value.astype(BF16)
    rest = value - high.astype(F32)
    middle = rest.astype(BF16)
    return high, middle, (rest - middle.astype(F32)).astype(BF16)


def select(left, right, dims=NN):
    left = left.astype(BF16)
    high, middle, low = (dot(left, part, dims) for part in thirds(right))
    return high + (middle + low)


def selected(left, right, dims=NN):
    right = right.astype(BF16)
    high, middle, low = (dot(part, right, dims) for part in thirds(left))
    return high + (middle + low)


def iota(shape, dim):
    return lax.broadcasted_iota(jnp.int32, shape, dim)


def as_f32(mask):
    return jnp.where(mask, 1.0, 0.0).astype(F32)


def prior_out_map():
    row, col = iota((48, 64), 0), iota((48, 64), 1)
    kind, d, c = col >> 5, (col >> 3) & 3, col & 7
    return as_f32((c < 6) & (row == kind * 24 + 4 * c + d))


def prior_in_map():
    row, col = iota((288, 216), 0), iota((288, 216), 1)
    tap, d, c = row >> 5, (row >> 3) & 3, row & 7
    return as_f32((c < 6) & (col == tap * 24 + 4 * c + d))


def channel_map():
    row, col = iota((16, 128), 0), iota((16, 128), 1)
    return as_f32(((row < 6) & (col == 11 - row)) | ((row >= 8) & (row < 14) & (col == 13 - row)))


def half_map():
    row, col = iota((16, 128), 0), iota((16, 128), 1)
    return as_f32(((row < 6) & (col == row)) | ((row >= 8) & (row < 14) & (col == row - 2)))


def lu_factors(lu):
    row, col = iota((128, 128), 0), iota((128, 128), 1)
    eye = (row == col) & (row < 12)
    lower = jnp.where(row > col, lu, 0.0) + as_f32(eye)
    upper = jnp.where(row < col, lu, 0.0) + jnp.where(eye, jnp.exp(lu), 0.0)
    return lower, upper, eye


def spread_weight(lu, gains):
    lower, upper, _ = lu_factors(lu)
    weight = select(channel_map(), dot(lower, upper, NN, HIGH))
    scaled = weight * jnp.exp(gains[1:2])
    shift = jnp.sum(scaled * gains[0:1], axis=1, keepdims=True)
    return jnp.where(iota((16, 128), 1) == 12, shift, scaled)


def weights_kernel(cin, mix, cout, prior, bias, gains, lu, table,
                   win, wt, mixh, mixth, bias2, wout, woutt, weff, wpt, wp, tablep, net_bias,
                   big, square, strip):
    hidden = mix.shape[0]
    wt[...] = jnp.zeros_like(wt)
    for dy in range(3):
        for dx in range(3):
            wt[pl.ds(dy * 32 + dx * 8, 6), :] = (
                0.5 * cin[dy * 3 + dx]
            ).astype(BF16).astype(F32)
    half = 0.5 * bias[0:1, :]
    first = half.astype(BF16).astype(F32)
    rest = half - first
    second = rest.astype(BF16).astype(F32)
    wt[46:47, :] = first
    wt[38:39, :] = second
    wt[54:55, :] = rest - second
    win[...] = wt[...].T.astype(BF16)
    mixh[...] = (0.5 * mix[...]).astype(BF16)
    mixth[...] = (0.5 * mix[...]).T.astype(BF16)
    bias2[...] = jnp.broadcast_to(0.5 * bias[1:2, :], (128, hidden)).T
    big[...] = jnp.zeros_like(big)
    for tap in range(9):
        big[pl.ds(tap * 16, 6), :] = cout[tap, 0:6, :]
        big[pl.ds(tap * 16 + 8, 6), :] = cout[tap, 6:12, :]
    wout[...] = big[0:144, :].astype(BF16)
    woutt[...] = (0.5 * big[0:256, :]).T.astype(BF16)
    square[...] = jnp.zeros_like(square)
    square[0:12, 0:12] = lu[...]
    strip[...] = jnp.zeros_like(strip)
    strip[0:3, 0:12] = gains[...]
    weff[...] = spread_weight(square[...], strip[0:8, :])
    added = select(half_map(), strip[...], NT)[:, 2:3] + as_f32(iota((16, 1), 0) >= 8) * 2.0
    net_bias[...] = jnp.broadcast_to(added, (16, 128))
    out_map = prior_out_map()
    flat = select(prior_in_map(), selected(prior[...].reshape(216, 48), out_map))
    flat_hi = flat.astype(BF16)
    flat_lo = (flat - flat_hi.astype(F32)).astype(BF16)
    wpt[...] = jnp.zeros_like(wpt)
    wpt[:, 0:64] = flat_hi
    wpt[:, 64:128] = flat_lo
    wpt[:, 128:192] = flat_hi
    big[...] = jnp.zeros_like(big)
    big[0:288, 0:64] = flat_hi.astype(F32)
    big[0:288, 64:128] = flat_lo.astype(F32)
    wp[...] = big[0:384, 0:128].T.astype(BF16)
    tablep[...] = jnp.zeros_like(tablep)
    tablep[0:10, 0:64] = selected(table[:, 0:48], out_map)
    tablep[0:10, 64:128] = selected(table[:, 48:96], out_map)


def hidden_unit(u):
    wide = 1.0 + jnp.tanh(u)
    act = (u * wide).astype(BF16)
    wide = wide.astype(BF16)
    return act, wide + act * (2.0 - wide)


def fill_windows(xaf, r2, half, count, taps_hi, taps_lo=None):
    for w in range(half):
        lanes = pl.ds(w * count, count)
        for ty in range(3):
            for tx in range(3):
                for dy in range(2):
                    er, ec = 2 * r2 + 2 * ty + dy, 2 * w + 2 * tx
                    pair = jnp.concatenate([xaf[er, ec], xaf[er, ec + 1]], axis=0)
                    high = pair.astype(BF16)
                    at = pl.ds((ty * 3 + tx) * 32 + dy * 16, 16)
                    taps_hi[at, lanes] = high
                    if taps_lo is not None:
                        taps_lo[at, lanes] = (pair - high.astype(F32)).astype(BF16)


def forward_kernel(cols, sub, images, noise, top, bottom, flags, weff, win, mixh, bias2, wout, wp, labels, others,
                   act1, sg1, act2, sg2, xa2, xt, xaf, xbf, nn, edge_top, edge_bottom, stats, hits,
                   xs, taps, acc, taps_hi, taps_lo):
    step = pl.program_id(0)
    rows, width, count = images.shape[1:]
    groups = width // cols

    @pl.when(step == 0)
    def _():
        seen = iota((16, count), 0) == jnp.broadcast_to(labels[...], (16, count))
        same = iota((16, count), 0) == jnp.broadcast_to(others[...], (16, count))
        seen = jnp.sum(as_f32(seen) + as_f32(same), axis=1, keepdims=True)
        hits[...] = jnp.broadcast_to(seen, (16, 128))
        xs[:, 0:2] = top[...].astype(F32)
        xs[:, 2 : rows + 2] = images[...] + noise[...]
        xs[:, rows + 2 : rows + 4] = bottom[...].astype(F32)
        xaf[...] = jnp.zeros_like(xaf)
        xt[...] = jnp.zeros_like(xt)
        acc[...] = jnp.zeros_like(acc)
        row8 = iota((8, count), 0)
        ones = jnp.where((iota((16, count), 0) & 7) == 6, 1.0, 0.0)
        col_a = [jnp.broadcast_to(weff[0:8, c : c + 1], (8, count)) for c in range(13)]
        col_b = [jnp.broadcast_to(weff[8:16, c : c + 1], (8, count)) for c in range(13)]

        def per_row(own, er):
            valid = jnp.where(er < 2, flags[0], jnp.where(er >= rows + 2, flags[1], 1.0))
            before = jnp.zeros((8, count), F32)
            for c in range(width):
                a, b = col_a[12], col_b[12]
                t0 = jnp.zeros((8, count), F32)
                t1 = jnp.where(row8 == 4, valid, 0.0)
                for ch in range(12):
                    x = jnp.broadcast_to(xs[ch, er, c : c + 1, :], (8, count))
                    a = a + col_a[ch] * x
                    if own:
                        b = b + col_b[ch] * x
                    if ch < 8:
                        t0 = jnp.where(row8 == ch, x, t0)
                    else:
                        t1 = jnp.where(row8 == ch - 8, x, t1)
                a = a * valid
                xaf[er, c + 2] = a
                xa2[er, c] = (jnp.concatenate([before, a], axis=0) + ones).astype(BF16)
                before = a
                xt[er, c + 1] = jnp.concatenate([t0, t1], axis=0).astype(BF16)

                if own:
                    xbf[er - 2, c] = b

            last = jnp.concatenate([before, jnp.zeros((8, count), F32)], axis=0)
            xa2[er, width] = (last + ones).astype(BF16)
            xa2[er, width + 1] = ones.astype(BF16)

        def own_row(i, carry):
            per_row(True, i + 2)
            return carry

        def other_row(i, carry):
            per_row(False, jnp.where(i < 2, i, i + rows))
            return carry

        lax.fori_loop(0, rows, own_row, 0)
        lax.fori_loop(0, 4, other_row, 0)

        def per_pair(r2, carry):
            fill_windows(xaf, r2, width // 2, count, taps_hi, taps_lo)
            main = dot(wp[:, 0:288], taps_hi[...])
            stats[r2] = main[0:64] + main[64:128] + dot(wp[0:64, 0:288], taps_lo[...])
            return carry

        lax.fori_loop(0, rows // 2, per_pair, 0)

    row = step // groups
    start = (step % groups) * cols
    for i in range(cols):
        lanes = pl.ds(i * count, count)
        for dy in range(3):
            for j in range(2):
                taps[pl.ds((dy * 2 + j) * 16, 16), lanes] = xa2[row + 1 + dy, start + i + 2 * j]
        taps[96:112, lanes] = xt[row + 2, start + i + 1]
        taps[112:128, lanes] = xt[row + 2, start + i + 1]
    size = sub * count
    for s in range(cols // sub):
        lanes = pl.ds(s * size, size)
        one, slope1 = hidden_unit(dot(win[...], taps[:, lanes]))
        act1[0, :, lanes] = one
        sg1[0, :, lanes] = slope1
        bias = jnp.concatenate([bias2[...]] * (size // 128), axis=1)
        two, slope2 = hidden_unit(dot(mixh[...], one) + bias)
        act2[0, :, lanes] = two
        sg2[0, :, lanes] = slope2
        out = dot(wout[...], two)
        for dy in range(3):
            for k in range(sub + 2):
                value = None
                for dx in range(3):
                    i = k + dx - 2
                    if 0 <= i < sub:
                        at = 16 * (dy * 3 + dx)
                        part = out[at : at + 16, i * count : (i + 1) * count]
                        value = part if value is None else value + part
                acc[row + 2 - dy, start + s * sub + k] += value

    @pl.when(step == rows * groups - 1)
    def _():
        nn[...] = acc[1 : rows + 1, 1 : width + 1]
        edge_top[...] = acc[0, 1 : width + 1].astype(BF16)
        edge_bottom[...] = acc[rows + 1, 1 : width + 1].astype(BF16)


def coupling_kernel(dims, nn, edge_top, edge_bottom, xbf, stats, labels, tablep, net_bias, *refs):
    dn, dn_first, dn_last, dstats, dxb, loss_acc, per_image, counts = refs[-8:]
    rows, width, _, count = nn.shape
    half = width // 2
    hot = as_f32(iota((16, count), 0) == jnp.broadcast_to(labels[...], (16, count)))
    number = refs[0][...]
    for ref in refs[1:-8]:
        number = number + ref[...]
    counts[...] = number
    scale16 = 1.0 / (10.0 * jnp.maximum(number, 1.0) * (dims * LOG_TWO))
    coef = jnp.sum(hot * scale16[:, 0:1], axis=0, keepdims=True)
    coef = jnp.broadcast_to(coef, (8, count))
    cls = selected(tablep[...], hot, TN)
    per_image[0:128, :] = cls
    per_image[128:136, :] = coef
    per_image[136:152, :] = hot
    bias_a = jnp.broadcast_to(net_bias[0:8, 0:1], (8, count))
    bias_b = jnp.broadcast_to(net_bias[8:16, 0:1], (8, count))
    loss = jnp.zeros((8, count), F32)
    for r2 in range(rows // 2):
        for w in range(half):
            lanes = pl.ds(w * count, count)
            for dy in range(2):
                pair = []
                for dx in range(2):
                    d = 2 * dy + dx
                    r, c = 2 * r2 + dy, 2 * w + dx
                    tile = nn[r, c]
                    if r == 0:
                        tile = tile + edge_top[c].astype(F32)
                    if r == rows - 1:
                        tile = tile + edge_bottom[c].astype(F32)
                    raw = tile[8:16] + bias_b
                    sig = 0.5 + 0.5 * jnp.tanh(0.5 * raw)
                    log_sig = jnp.minimum(raw, 0.0) - jnp.log(1.0 + jnp.exp(-jnp.abs(raw)))
                    base = xbf[r, c] + tile[0:8] + bias_a
                    logs = stats[r2, pl.ds(32 + 8 * d, 8), lanes] + cls[32 + 8 * d : 40 + 8 * d]
                    diff = base * sig - (stats[r2, pl.ds(8 * d, 8), lanes] + cls[8 * d : 8 * d + 8])
                    weighted = diff * jnp.exp(-2.0 * logs)
                    quad = diff * weighted
                    loss = loss + (log_sig - 0.5 * (LOG_TWO_PI + 2.0 * logs + quad))
                    dv = coef * weighted
                    dstats[r2, pl.ds(8 * d, 8), lanes] = -dv
                    dstats[r2, pl.ds(32 + 8 * d, 8), lanes] = coef - coef * quad
                    passed = dv * sig
                    pair.append(passed)
                    draw = (passed * base - coef) * (1.0 - sig)
                    dn[r, c] = jnp.concatenate([passed, draw], axis=0).astype(BF16)
                dxb[2 * r2 + dy, w] = jnp.concatenate(pair, axis=0).astype(BF16)
    loss_acc[...] = loss
    dn_first[...] = dn[0]
    dn_last[...] = dn[rows - 1]


def prior_kernel(dn, dstats, dxb, loss_part, xaf, xt, per_image, wpt,
                 dprior, small, taps_hi, dtaps, dxa, table_acc):
    rows, width, _, count = dn.shape
    half = width // 2
    cls = per_image[0:128, :]
    coef = per_image[128:136, :]
    hot = per_image[136:152, :]
    weight_grad = None
    for r2 in range(rows // 2):
        fill_windows(xaf, r2, half, count, taps_hi)
        grads = dstats[r2]
        high = grads.astype(BF16)
        low = (grads - high.astype(F32)).astype(BF16)
        part = dot(taps_hi[...], high, NT)
        weight_grad = part if weight_grad is None else weight_grad + part
        dtaps[r2] = dot(wpt[:, 0:192], jnp.concatenate([high, high, low], axis=0))
    dprior[...] = jnp.zeros_like(dprior)
    dprior[:, 0:64] = weight_grad
    for k in range(8):
        rows8 = pl.ds(8 * k, 8)
        value = jnp.zeros((8, count), F32)
        for r2 in range(rows // 2):
            for w in range(half):
                value = value + dstats[r2, rows8, pl.ds(w * count, count)]
        table_acc[rows8, :] = value
    gain = jnp.zeros((16, count), F32)
    loss = loss_part[...]
    means = [jnp.zeros((8, count), F32)] * 4
    scales = [jnp.zeros((8, count), F32)] * 4
    for er in range(rows + 4):
        for pair in range(half):
            both = []
            for dx in range(2):
                c = 2 * pair + dx
                value = None
                for r2 in range(rows // 2):
                    ey = er - 2 * r2
                    for w in range(half):
                        ex = c + 2 - 2 * w
                        if 0 <= ey < 6 and 0 <= ex < 6:
                            at = ((ey // 2) * 3 + ex // 2) * 32 + (ey % 2) * 16 + (ex % 2) * 8
                            part = dtaps[r2, pl.ds(at, 8), pl.ds(w * count, count)]
                            value = part if value is None else value + part
                r = er - 2
                if 0 <= r < rows:
                    d = 2 * (r % 2) + dx
                    gain = gain + dn[r, c].astype(F32)
                    logs = cls[96 + 8 * d : 104 + 8 * d]
                    diff = xaf[er, c + 2] - cls[64 + 8 * d : 72 + 8 * d]
                    weighted = diff * jnp.exp(-2.0 * logs)
                    quad = diff * weighted
                    loss = loss - 0.5 * (LOG_TWO_PI + 2.0 * logs + quad)
                    dv = coef * weighted
                    means[d] = means[d] - dv
                    scales[d] = scales[d] + (coef - coef * quad)
                    value = value + dv
                both.append(value)
            dxa[er, pair] = jnp.concatenate(both, axis=0).astype(BF16)
    for d in range(4):
        table_acc[pl.ds(64 + 8 * d, 8), :] = means[d]
        table_acc[pl.ds(96 + 8 * d, 8), :] = scales[d]
    outer = jnp.zeros((width * 8, width * 16), F32)
    inner = jnp.zeros((width * 8, width * 16), F32)
    for er in range(rows + 4):
        field = xt[er, 1 : width + 1].reshape(width * 16, count)
        outer = outer + dot(dxa[er].reshape(width * 8, count), field, NT)
        if 2 <= er < rows + 2:
            inner = inner + dot(dxb[er - 2].reshape(width * 8, count), field, NT)
    total = jnp.concatenate([outer, inner], axis=0)
    row, col = iota((256, 256), 0), iota((256, 256), 1)
    masked = jnp.where(((row & 127) >> 3) == (col >> 4), total, 0.0)
    halves = []
    for h in range(2):
        value = masked[128 * h : 128 * h + 8]
        for k in range(1, 16):
            value = value + masked[128 * h + 8 * k : 128 * h + 8 * k + 8]
        halves.append(value)
    fold = as_f32((iota((256, 128), 0) & 15) == iota((256, 128), 1))
    small[...] = jnp.zeros_like(small)
    small[:, 128:256] = selected(jnp.concatenate(halves, axis=0), fold)
    small[:, 0:128] = select(hot, table_acc[...], NT)
    spread = half_map() * jnp.sum(gain, axis=1, keepdims=True)
    small[0:8, 256:384] = jnp.broadcast_to(jnp.sum(spread, axis=0, keepdims=True), (8, 128))
    value = jnp.where(iota((8, count), 0) < 6, loss * coef, 0.0)
    value = jnp.sum(jnp.sum(value, axis=0, keepdims=True), axis=1, keepdims=True)
    small[8:16, 256:384] = jnp.broadcast_to(-value, (8, 128))


def backward_kernel(cols, sub, act1, sg1, act2, sg2, place, dn, dn_top, dn_bottom, xa2, xt, mixth, woutt, wt,
                    dprior, small, keep, send, packed, dnp, taps, gtaps, bias_acc, wfield, gout, gin):
    step = pl.program_id(0)
    rows, width, _, count = dn.shape
    groups = width // cols

    @pl.when(step == 0)
    def _():
        packed[...] = jnp.zeros_like(packed)
        gout[...] = jnp.zeros_like(gout)
        gin[...] = jnp.zeros_like(gin)
        bias_acc[...] = jnp.zeros_like(bias_acc)
        wfield[...] = jnp.zeros_like(wfield)
        dnp[...] = jnp.zeros_like(dnp)
        dnp[0, 1 : width + 1] = dn_top[...]
        dnp[1 : rows + 1, 1 : width + 1] = dn[...]
        dnp[rows + 1, 1 : width + 1] = dn_bottom[...]
        taps[240:256, :] = jnp.zeros_like(taps[240:256, :])
        gtaps[144:256, :] = jnp.zeros_like(gtaps[144:256, :])

    row = step // groups
    start = (step % groups) * cols
    for i in range(cols):
        lanes = pl.ds(i * count, count)
        for dy in range(3):
            for j in range(2):
                taps[pl.ds((dy * 2 + j) * 16, 16), lanes] = xa2[row + 1 + dy, start + i + 2 * j]
            for dx in range(3):
                tap = dy * 3 + dx
                taps[pl.ds(96 + tap * 16, 16), lanes] = xt[row + 1 + dy, start + i + dx]
                gtaps[pl.ds(tap * 16, 16), lanes] = dnp[row + 2 - dy, start + i + 2 - dx]
    size = sub * count
    for s in range(cols // sub):
        lanes = pl.ds(s * size, size)
        grad2 = (dot(woutt[...], gtaps[:, lanes]) * sg2[0, :, lanes].astype(F32)).astype(BF16)
        grad1 = (dot(mixth[...], grad2) * sg1[0, :, lanes].astype(F32)).astype(BF16)
        wide = grad2.astype(F32)
        bias = wide[:, 0:128]
        for k in range(1, size // 128):
            bias = bias + wide[:, k * 128 : (k + 1) * 128]
        bias_acc[...] += bias
        gout[...] += dot(gtaps[0:144, lanes], act2[0, :, lanes], NT)
        packed[ROW_MIX:ROW_OUT, :] += dot(grad2, act1[0, :, lanes], NT)
        gathered = dot(taps[0:240, lanes], grad1, NT)
        gin[...] += gathered[0:96]
        wfield[...] += gathered[96:240]

    @pl.when(step == rows * groups - 1)
    def _():
        for tap in range(9):
            at = ROW_OUT + 12 * tap
            packed[at : at + 6, :] = gout[16 * tap : 16 * tap + 6, :]
            packed[at + 6 : at + 12, :] = gout[16 * tap + 8 : 16 * tap + 14, :]
            at = ROW_IN + 6 * tap
            from_row = (tap // 3) * 32 + (tap % 3) * 8
            packed[at : at + 6, :] = gin[from_row : from_row + 6, :]
        packed[ROW_BIAS : ROW_BIAS + 1, :] = gin[46:47, :]
        lone = jnp.ones((8, 128), F32)
        packed[ROW_BIAS + 1 : ROW_BIAS + 2, :] = select(lone, bias_acc[...], NT)[0:1]
        for k in range(4):
            packed[ROW_PRIOR:ROW_SMALL, 128 * k : 128 * k + 128] = dprior[72 * k : 72 * k + 72, :]
        packed[ROW_SMALL:ROWS, :] = small[...]
        cross = select(wt[0:96, :], wfield[...], NT)
        row, col = iota((96, 144), 0), iota((96, 144), 1)
        slot = (row >> 3) & 3
        same = (slot < 3) & ((row >> 5) * 3 + slot == col >> 4) & ((row & 7) < 6)
        fold = as_f32((iota((144, 128), 0) & 15) == iota((144, 128), 1))
        cross = jnp.where(same, cross, 0.0)
        value = cross[0:8]
        for k in range(1, 12):
            value = value + cross[8 * k : 8 * k + 8]
        field_terms = selected(value, fold)
        packed[ROW_SMALL : ROW_SMALL + 8, 128:256] += 2.0 * field_terms
        chunks, each = keep.shape[:2]
        core = place[0]
        for k in range(2 * chunks):
            block = chunk_of(packed, k, each)
            mine = core == k // chunks

            @pl.when(mine)
            def _():
                keep[k % chunks] = block

            @pl.when(jnp.logical_not(mine))
            def _():
                send[k % chunks] = to_wire(block)


def chunk_of(packed, k, each):
    plain, fine = 2 * each // 3, each // 3
    return jnp.concatenate(
        [
            packed[k * plain : (k + 1) * plain, :],
            packed[ROW_OUT + k * fine : ROW_OUT + (k + 1) * fine, :],
        ],
        axis=0,
    )


def to_wire(block):
    axis = block.ndim - 2
    each = block.shape[axis]
    plain = lax.slice_in_dim(block, 0, 2 * each // 3, axis=axis)
    fine = lax.slice_in_dim(block, 2 * each // 3, each, axis=axis)
    high = fine.astype(BF16).astype(F32)
    return jnp.concatenate([plain, high, fine - high], axis=axis).astype(BF16)


def from_wire(wire):
    axis = wire.ndim - 2
    part = wire.shape[axis] // 4
    wide = wire.astype(F32)
    fine = lax.slice_in_dim(wide, 2 * part, 3 * part, axis=axis)
    fine = fine + lax.slice_in_dim(wide, 3 * part, 4 * part, axis=axis)
    return jnp.concatenate([lax.slice_in_dim(wide, 0, 2 * part, axis=axis), fine], axis=axis)


def halve_kernel(place, keep, got, mine, *sends):
    count = len(sends) + 1
    bands = keep.shape[0] // count
    here = place[1]
    for m in range(count):
        for b in range(bands):
            at = (here ^ m) * bands + b
            value = keep[at] + from_wire(got[at])
            if m == 0:
                mine[b] = value
            else:
                sends[m - 1][b] = to_wire(value)


def spread_kernel(place, bands, first, *refs):
    gots, mine, sends = refs[:-bands], refs[-bands], refs[1 - bands :]
    here = place[2]
    for k in range(bands):
        at = lax.rem(here + k, bands)
        value = first[at]
        for got in gots:
            value = value + from_wire(got[at])
        if k == 0:
            mine[...] = value
        else:
            sends[k - 1][...] = to_wire(value)


def sum_kernel(mine, *refs):
    value = mine[...]
    for ref in refs[:-1]:
        value = value + from_wire(ref[...])
    refs[-1][...] = to_wire(value)


def gather_kernel(place, which, xor, mine, *refs):
    out = refs[-1]
    here = place[which]
    count = len(refs)
    for k in range(count):
        at = (here ^ k) if xor else lax.rem(here - k + count, count)
        out[at] = (mine if k == 0 else refs[k - 1])[...]


def adamw(weight, first, second, grad, out, out_first, out_second, at=Ellipsis):
    first_new = BETA_ONE * first[at] + (1.0 - BETA_ONE) * grad
    second_new = BETA_TWO * second[at] + (1.0 - BETA_TWO) * grad * grad
    first_hat = first_new * (1.0 / (1.0 - BETA_ONE**STEP))
    second_hat = second_new * (1.0 / (1.0 - BETA_TWO**STEP))
    out[at] = weight[at] - RATE * (
        first_hat / (jnp.sqrt(second_hat) + EPSILON) + DECAY * weight[at]
    )
    out_first[at] = first_new
    out_second[at] = second_new


def update_kernel(area, dims, *refs):
    place, own, other, counts = refs[:4]
    refs = refs[4:]
    params, firsts, seconds = refs[:8], refs[8:16], refs[16:24]
    loss, norm = refs[24:26]
    news, new_firsts, new_seconds = refs[26:34], refs[34:42], refs[42:50]
    square, strip, gin, gout, flat, kept, grads = refs[50:]
    chunks = own.shape[0]
    fine = own.shape[1] // 4
    for k in range(2 * chunks):
        mine = place[0] == k // chunks
        block = from_wire(jnp.where(mine, own[k % chunks], other[k % chunks]))
        grads[2 * k * fine : 2 * (k + 1) * fine, :] = block[0 : 2 * fine]
        grads[ROW_OUT + k * fine : ROW_OUT + (k + 1) * fine, :] = block[2 * fine :]
    bias, gains_ref, lu_ref = params[4:7]
    hidden = grads.shape[1]
    square[...] = jnp.zeros_like(square)
    square[0:12, 0:12] = lu_ref[...]
    strip[...] = jnp.zeros_like(strip)
    strip[0:3, 0:12] = gains_ref[...]
    gains = strip[...]
    lower, upper, eye = lu_factors(square[...])
    weight = spread_weight(square[...], gains)
    field = grads[ROW_SMALL:ROWS, 128:256]
    lane = iota((16, 128), 1)
    level = jnp.sum(jnp.where(lane == 12, field, 0.0), axis=1, keepdims=True)
    real = iota((16, 128), 0) & 7
    moved = jnp.where((lane < 12) & (real < 6), field + level * gains[0:1], 0.0)
    level = jnp.where(real < 6, level, 0.0)
    number = counts[...]
    present = number / jnp.maximum(number, 1.0)
    share = jnp.sum(present[:, 0:1], axis=0, keepdims=True)
    coef = share * (1.0 / (10.0 * dims * LOG_TWO)) * area
    weight = jnp.where(lane < 12, weight, 0.0)
    d_shift = jnp.sum(weight * level, axis=0, keepdims=True)
    d_scale = jnp.sum(weight * moved, axis=0, keepdims=True) - coef
    d_product = select(channel_map(), moved * jnp.exp(gains[1:2]), TN)
    d_lower = dot(d_product, upper, NT, HIGH)
    d_upper = dot(lower, d_product, TN, HIGH)
    row, col = iota((128, 128), 0), iota((128, 128), 1)
    d_lu = jnp.where(row > col, d_lower, 0.0) + jnp.where(row < col, d_upper, 0.0)
    d_lu = d_lu + jnp.where(eye, d_upper * jnp.exp(square[...]) - coef, 0.0)
    d_lu = jnp.where((row < 12) & (col < 12), d_lu, 0.0)
    diag = jnp.sum(jnp.sum(jnp.where(eye, square[...], 0.0), axis=0, keepdims=True), axis=1, keepdims=True)
    logs = jnp.sum(jnp.where(lane[0:1] < 12, gains[1:2], 0.0), axis=1, keepdims=True)
    d_bias_out = grads[ROW_SMALL : ROW_SMALL + 1, 256:384]
    row8 = iota((8, 128), 0)
    d_gains = jnp.where(row8 == 0, d_shift, jnp.where(row8 == 1, d_scale, jnp.where(row8 == 2, d_bias_out, 0.0)))
    d_gains = jnp.where(iota((8, 128), 1) < 12, d_gains, 0.0)
    for tap in range(9):
        gin[tap] = grads[ROW_IN + 6 * tap : ROW_IN + 6 * tap + 6, :]
        gout[tap] = grads[ROW_OUT + 12 * tap : ROW_OUT + 12 * tap + 12, :]
    for k in range(4):
        flat[72 * k : 72 * k + 72, :] = grads[ROW_PRIOR:ROW_SMALL, 128 * k : 128 * k + 128]
    out_map = prior_out_map()
    for k in range(36):
        kept[pl.ds((k >> 2) * 24 + (k & 3), 6, stride=4), :] = flat[8 * k : 8 * k + 6, :]
    d_prior = selected(kept[:, 0:64], out_map, NT)
    d_table = grads[ROW_SMALL:ROWS, 0:128]
    d_table = [selected(d_table[:, 0:64], out_map, NT), selected(d_table[:, 64:128], out_map, NT)]
    d_table = [part[0:10] for part in d_table]
    d_bias = [grads[ROW_BIAS : ROW_BIAS + 1, :], grads[ROW_BIAS + 1 : ROW_BIAS + 2, :]]
    d_mix = grads[0:ROW_OUT, :]

    def squares(value):
        value = value * value
        if value.ndim == 3:
            value = jnp.sum(value, axis=0)
        return jnp.sum(jnp.sum(value, axis=0, keepdims=True), axis=1, keepdims=True)

    squared = squares(d_mix) + squares(gin[...]) + squares(gout[...]) + squares(d_prior)
    squared = squared + squares(d_bias[0]) + squares(d_bias[1]) + squares(d_gains) + squares(d_lu)
    squared = squared + squares(d_table[0]) + squares(d_table[1])
    total_norm = jnp.sqrt(squared)
    factor = jnp.minimum(1.0, CLIP_NORM / (total_norm + 1e-06))
    norm[...] = total_norm
    loss[...] = (
        grads[ROW_SMALL + 8 : ROW_SMALL + 9, 256:257] - coef * (logs + diag) + BITS * share / 10.0
    )

    def put(k, grad, at=Ellipsis):
        adamw(params[k], firsts[k], seconds[k], grad, news[k], new_firsts[k], new_seconds[k], at)

    put(0, factor * gin[...])
    put(1, factor * d_mix)
    put(2, factor * gout[...])
    put(3, (factor * d_prior).reshape(9, 24, 48))
    put(4, factor * d_bias[0], (slice(0, 1), slice(None)))
    put(4, factor * d_bias[1], (slice(1, 2), slice(None)))
    put(5, (factor * d_gains)[0:3, 0:12])
    put(6, (factor * d_lu)[0:12, 0:12])
    put(7, factor * d_table[0], (slice(None), slice(0, 48)))
    put(7, factor * d_table[1], (slice(None), slice(48, 96)))


def shape(dims, dtype=F32):
    return jax.ShapeDtypeStruct(dims, dtype)


def near(dims, dtype=F32):
    return pltpu.HBM(dims, dtype)


def far(array):
    return pltpu.with_memory_space_constraint(array, pltpu.HBM)


def params_of(limit):
    return pltpu.CompilerParams(vmem_limit_bytes=limit * MIB)


def exchange_rows(up, down):
    count = lax.axis_size("band")
    before = lax.ppermute(down, "band", [(i, i + 1) for i in range(count - 1)])
    after = lax.ppermute(up, "band", [(i + 1, i) for i in range(count - 1)])
    return before, after


def body(images, noise, labels, *rest):
    params, firsts, seconds = (list(rest[8 * k : 8 * k + 8]) for k in range(3))
    for group in (params, firsts, seconds):
        group[0] = group[0].transpose(0, 2, 1)
        group[3] = group[3].transpose(0, 2, 1)
    chans, rows, width, count = images.shape
    hidden = params[1].shape[0]
    band = lax.axis_index("band")
    bands = lax.axis_size("band")
    whole = pl.BlockSpec(memory_space=pltpu.VMEM)

    top, bottom = exchange_rows(
        (images[:, :2] + noise[:, :2]).astype(BF16),
        (images[:, rows - 2 :] + noise[:, rows - 2 :]).astype(BF16),
    )
    groups_dp = lax.axis_size("dp")
    chips = groups_dp // 2

    def swap(array, mask):
        pairs = [(i, i ^ mask) for i in range(groups_dp)]
        return lax.ppermute(array, "dp", pairs)

    labels = labels[None, :]
    others = swap(labels, 1)
    flags = jnp.stack([band > 0, band < bands - 1]).astype(F32)
    dp = lax.axis_index("dp")
    place = jnp.stack([dp & 1, dp >> 1, band]).astype(jnp.int32)
    smem = pl.BlockSpec(memory_space=pltpu.SMEM)
    win, wt, mixh, mixth, bias2, wout, woutt, weff, wpt, wp, tablep, net_bias = pl.pallas_call(
        weights_kernel,
        out_shape=(
            near((hidden, 128), BF16),
            near((128, hidden)),
            near((hidden, hidden), BF16),
            near((hidden, hidden), BF16),
            near((hidden, 128)),
            near((144, hidden), BF16),
            near((hidden, 256), BF16),
            near((16, 128)),
            near((288, 256), BF16),
            near((128, 384), BF16),
            near((16, 128)),
            near((16, 128)),
        ),
        in_specs=[whole] * 8,
        out_specs=(whole,) * 12,
        scratch_shapes=[
            pltpu.VMEM((512, hidden), F32),
            pltpu.VMEM((128, 128), F32),
            pltpu.VMEM((8, 128), F32),
        ],
        compiler_params=params_of(VMEM_MIB),
        name="weights",
    )(*[far(p) for p in params])

    cols, sub = 8, 4
    pixels = (width // 2) * count
    groups = width // cols
    steps = rows * groups
    size = cols * count
    chunk = pl.BlockSpec((1, hidden, size), lambda i: (i, 0, 0))
    ext = (rows + 4, width + 2, 16, count)
    exta = (rows + 4, width + 4, 8, count)
    act1, sg1, act2, sg2, xa2, xt, xaf, xbf, nn, edge_top, edge_bottom, stats, hits = pl.pallas_call(
        functools.partial(forward_kernel, cols, sub),
        grid=(steps,),
        out_shape=(pltpu.HBM((steps, hidden, size), BF16),) * 4
        + (
            near(ext, BF16),
            near(ext, BF16),
            near(exta),
            near((rows, width, 8, count)),
            near((rows, width, 16, count)),
            near((width, 16, count), BF16),
            near((width, 16, count), BF16),
            near((rows // 2, 64, pixels)),
            shape((16, 128)),
        ),
        in_specs=[whole] * 4 + [smem] + [whole] * 8,
        out_specs=(chunk,) * 4 + (whole,) * 9,
        scratch_shapes=[
            pltpu.VMEM((chans, rows + 4, width, count), F32),
            pltpu.VMEM((128, size), BF16),
            pltpu.VMEM((rows + 2, width + 2, 16, count), F32),
            pltpu.VMEM((288, pixels), BF16),
            pltpu.VMEM((288, pixels), BF16),
        ],
        compiler_params=params_of(VMEM_MIB),
        cost_estimate=pl.CostEstimate(
            flops=2 * rows * width * count * hidden * (hidden + 272),
            transcendentals=2 * rows * width * count * hidden,
            bytes_accessed=8 * rows * width * count * hidden,
        ),
        name="forward",
    )(far(images), far(noise), top, bottom, flags, *map(far, (weff, win, mixh, bias2, wout, wp, labels)), others)

    got_top, got_bottom = exchange_rows(edge_top, edge_bottom)
    plain = (got_top.shape, hits.shape)

    def local(kernel, name, outs, scratch, *inputs):
        return pl.pallas_call(
            kernel,
            out_shape=outs,
            in_specs=[whole for _ in inputs],
            out_specs=tuple(whole for _ in outs),
            scratch_shapes=scratch,
            compiler_params=params_of(VMEM_MIB),
            name=name,
        )(*[a if a.shape in plain else far(a) for a in inputs])

    dn, dn_first, dn_last, dstats, dxb, loss_part, per_image, counts = local(
        functools.partial(coupling_kernel, 12.0 * width * width),
        "coupling",
        (
            near((rows, width, 16, count), BF16),
            near((width, 16, count), BF16),
            near((width, 16, count), BF16),
            near((rows // 2, 64, pixels)),
            near((rows, width // 2, 16, count), BF16),
            near((8, count)),
            near((152, count)),
            near((16, 128)),
        ),
        [],
        nn,
        got_top,
        got_bottom,
        xbf,
        stats,
        labels,
        tablep,
        net_bias,
        hits,
        *[swap(hits, 2 * m) for m in range(1, chips)],
    )
    dprior, small = local(
        prior_kernel,
        "prior_grads",
        (near((288, 128)), near((16, 512))),
        [
            pltpu.VMEM((288, pixels), BF16),
            pltpu.VMEM((rows // 2, 288, pixels), F32),
            pltpu.VMEM((rows + 4, width // 2, 16, count), BF16),
            pltpu.VMEM((128, count), F32),
        ],
        dn,
        dstats,
        dxb,
        loss_part,
        xaf,
        xt,
        per_image,
        wpt,
    )

    dn_top, dn_bottom = exchange_rows(dn_first, dn_last)
    both = ("dp", "band")
    devices = lax.axis_size(both)
    each = ROWS // devices
    wires = each + each // 3
    half_shape = (devices // 2, each, hidden)
    keep, send = pl.pallas_call(
        functools.partial(backward_kernel, cols, sub),
        grid=(steps,),
        out_shape=(near(half_shape), near((devices // 2, wires, hidden), BF16)),
        in_specs=[chunk] * 4 + [smem] + [whole] * 10,
        out_specs=(whole,) * 2,
        scratch_shapes=[
            pltpu.VMEM((devices * each, hidden), F32),
            pltpu.VMEM((rows + 2, width + 2, 16, count), BF16),
            pltpu.VMEM((256, size), BF16),
            pltpu.VMEM((256, size), BF16),
            pltpu.VMEM((hidden, 128), F32),
            pltpu.VMEM((144, hidden), F32),
            pltpu.VMEM((144, hidden), F32),
            pltpu.VMEM((96, hidden), F32),
        ],
        compiler_params=params_of(VMEM_MIB),
        name="backward",
    )(*map(far, (act1, sg1, act2, sg2)), place, far(dn), dn_top, dn_bottom, *map(far, (xa2, xt, mixth, woutt, wt, dprior, small)))

    def call(kernel, name, outs, *inputs):
        return pl.pallas_call(
            kernel,
            out_shape=outs,
            in_specs=[smem if a is place else whole for a in inputs],
            out_specs=jax.tree.map(lambda _: whole, outs),
            compiler_params=params_of(VMEM_MIB),
            name=name,
        )(*inputs)

    def turn(array, k):
        return lax.ppermute(array, "band", [(i, (i + k) % bands) for i in range(bands)])

    got = swap(send, 1)
    block = shape((bands, wires, hidden), BF16)
    tile = shape((wires, hidden), BF16)
    mine, *sends = call(
        halve_kernel, "halve", (shape((bands, each, hidden)),) + (block,) * (chips - 1), place, far(keep), got
    )
    gots = [swap(a, 2 * (m + 1)) for m, a in enumerate(sends)]
    mine, *sends = call(
        lambda p, *refs: spread_kernel(p, bands, *refs),
        "spread",
        (shape((each, hidden)),) + (tile,) * (bands - 1),
        place,
        mine,
        *gots,
    )
    gots = [turn(a, k + 1) for k, a in enumerate(sends)]
    mine = call(sum_kernel, "total", tile, mine, *gots)
    gots = [turn(mine, k + 1) for k in range(bands - 1)]
    mine = call(
        lambda p, *refs: gather_kernel(p, 2, False, *refs), "gather_band", block, place, mine, *gots
    )
    gots = [swap(mine, 2 * (m + 1)) for m in range(chips - 1)]
    mine = call(
        lambda p, *refs: gather_kernel(p, 1, True, *refs),
        "gather_chips",
        shape((chips,) + block.shape, BF16),
        place,
        mine,
        *gots,
    )
    mine = mine.reshape((devices // 2, wires, hidden))
    other = swap(mine, 1)

    area = float(width * width)
    results = pl.pallas_call(
        functools.partial(update_kernel, area, 12.0 * width * width),
        out_shape=(shape((1, 1)), shape((1, 1))) + tuple(shape(p.shape) for p in params) * 3,
        in_specs=[smem] + [whole] * 27,
        out_specs=(whole,) * 26,
        scratch_shapes=[
            pltpu.VMEM((128, 128), F32),
            pltpu.VMEM((8, 128), F32),
            pltpu.VMEM((9, 6, hidden), F32),
            pltpu.VMEM((9, 12, hidden), F32),
            pltpu.VMEM((288, 128), F32),
            pltpu.VMEM((216, 128), F32),
            pltpu.VMEM((devices * each, hidden), F32),
        ],
        compiler_params=params_of(VMEM_MIB),
        name="update",
    )(place, mine, other, counts, *params, *firsts, *seconds)
    outs = [results[0][0, 0], results[1][0, 0]]
    for k in range(3):
        group = list(results[2 + 8 * k : 10 + 8 * k])
        group[0] = group[0].transpose(0, 2, 1)
        group[3] = group[3].transpose(0, 2, 1)
        outs += group
    return tuple(outs)


def solution(mesh):
    field = P(None, "band", None, "dp")
    return jax.shard_map(
        body,
        mesh=mesh,
        in_specs=(field, field, P("dp")) + (P(),) * 24,
        out_specs=(P(),) * 26,
        check_vma=False,
    )
```

```python
import functools
import math

import jax
import jax.numpy as jnp
from jax import lax
from jax.experimental import pallas as pl
from jax.experimental.pallas import tpu as pltpu
from jax.sharding import PartitionSpec as P

STEP = 10
HIGH = lax.Precision.HIGHEST
LOG_TWO = math.log(2.0)
LOG_TWO_PI = math.log(2.0 * math.pi)
CLIP_NORM = 0.01
RATE = 0.05
BETA_ONE = 0.9
BETA_TWO = 0.999
EPSILON = 1e-08
DECAY = 0.01
BITS = 5.0
F32 = jnp.float32
BF16 = jnp.bfloat16
MIB = 1024 * 1024
VMEM_MIB = 46
NN = (((1,), (0,)), ((), ()))
NT = (((1,), (1,)), ((), ()))
TN = (((0,), (0,)), ((), ()))

ROW_MIX = 0
ROW_OUT = 512
ROW_IN = ROW_OUT + 108
ROW_BIAS = ROW_IN + 54
ROW_PRIOR = ROW_BIAS + 6
ROW_SMALL = ROW_PRIOR + 72
ROWS = ROW_SMALL + 16


def dot(left, right, dims=NN, precision=None):
    return lax.dot_general(left, right, dims, precision=precision, preferred_element_type=F32)


def thirds(value):
    high = value.astype(BF16)
    rest = value - high.astype(F32)
    middle = rest.astype(BF16)
    return high, middle, (rest - middle.astype(F32)).astype(BF16)


def select(left, right, dims=NN):
    left = left.astype(BF16)
    high, middle, low = (dot(left, part, dims) for part in thirds(right))
    return high + (middle + low)


def selected(left, right, dims=NN):
    right = right.astype(BF16)
    high, middle, low = (dot(part, right, dims) for part in thirds(left))
    return high + (middle + low)


def iota(shape, dim):
    return lax.broadcasted_iota(jnp.int32, shape, dim)


def as_f32(mask):
    return jnp.where(mask, 1.0, 0.0).astype(F32)


def prior_out_map():
    row, col = iota((48, 64), 0), iota((48, 64), 1)
    kind, d, c = col >> 5, (col >> 3) & 3, col & 7
    return as_f32((c < 6) & (row == kind * 24 + 4 * c + d))


def prior_in_map():
    row, col = iota((288, 216), 0), iota((288, 216), 1)
    tap, d, c = row >> 5, (row >> 3) & 3, row & 7
    return as_f32((c < 6) & (col == tap * 24 + 4 * c + d))


def channel_map():
    row, col = iota((16, 128), 0), iota((16, 128), 1)
    return as_f32(((row < 6) & (col == 11 - row)) | ((row >= 8) & (row < 14) & (col == 13 - row)))


def half_map():
    row, col = iota((16, 128), 0), iota((16, 128), 1)
    return as_f32(((row < 6) & (col == row)) | ((row >= 8) & (row < 14) & (col == row - 2)))


def lu_factors(lu):
    row, col = iota((128, 128), 0), iota((128, 128), 1)
    eye = (row == col) & (row < 12)
    lower = jnp.where(row > col, lu, 0.0) + as_f32(eye)
    upper = jnp.where(row < col, lu, 0.0) + jnp.where(eye, jnp.exp(lu), 0.0)
    return lower, upper, eye


def spread_weight(lu, gains):
    lower, upper, _ = lu_factors(lu)
    weight = select(channel_map(), dot(lower, upper, NN, HIGH))
    scaled = weight * jnp.exp(gains[1:2])
    shift = jnp.sum(scaled * gains[0:1], axis=1, keepdims=True)
    return jnp.where(iota((16, 128), 1) == 12, shift, scaled)


def weights_kernel(cin, mix, cout, prior, bias, gains, lu, table,
                   win, wt, mixh, mixth, bias2, wout, woutt, weff, wpt, wp, tablep, net_bias,
                   big, square, strip):
    hidden = mix.shape[0]
    wt[...] = jnp.zeros_like(wt)
    for dy in range(3):
        for dx in range(3):
            wt[pl.ds(dy * 32 + dx * 8, 6), :] = (
                0.5 * cin[dy * 3 + dx]
            ).astype(BF16).astype(F32)
    half = 0.5 * bias[0:1, :]
    first = half.astype(BF16).astype(F32)
    rest = half - first
    second = rest.astype(BF16).astype(F32)
    wt[46:47, :] = first
    wt[38:39, :] = second
    wt[54:55, :] = rest - second
    win[...] = wt[...].T.astype(BF16)
    mixh[...] = (0.5 * mix[...]).astype(BF16)
    mixth[...] = (0.5 * mix[...]).T.astype(BF16)
    bias2[...] = jnp.broadcast_to(0.5 * bias[1:2, :], (128, hidden)).T
    big[...] = jnp.zeros_like(big)
    for tap in range(9):
        big[pl.ds(tap * 16, 6), :] = cout[tap, 0:6, :]
        big[pl.ds(tap * 16 + 8, 6), :] = cout[tap, 6:12, :]
    wout[...] = big[0:144, :].astype(BF16)
    woutt[...] = (0.5 * big[0:256, :]).T.astype(BF16)
    square[...] = jnp.zeros_like(square)
    square[0:12, 0:12] = lu[...]
    strip[...] = jnp.zeros_like(strip)
    strip[0:3, 0:12] = gains[...]
    weff[...] = spread_weight(square[...], strip[0:8, :])
    added = select(half_map(), strip[...], NT)[:, 2:3] + as_f32(iota((16, 1), 0) >= 8) * 2.0
    net_bias[...] = jnp.broadcast_to(added, (16, 128))
    out_map = prior_out_map()
    flat = select(prior_in_map(), selected(prior[...].reshape(216, 48), out_map))
    flat_hi = flat.astype(BF16)
    flat_lo = (flat - flat_hi.astype(F32)).astype(BF16)
    wpt[...] = jnp.zeros_like(wpt)
    wpt[:, 0:64] = flat_hi
    wpt[:, 64:128] = flat_lo
    wpt[:, 128:192] = flat_hi
    big[...] = jnp.zeros_like(big)
    big[0:288, 0:64] = flat_hi.astype(F32)
    big[0:288, 64:128] = flat_lo.astype(F32)
    wp[...] = big[0:384, 0:128].T.astype(BF16)
    tablep[...] = jnp.zeros_like(tablep)
    tablep[0:10, 0:64] = selected(table[:, 0:48], out_map)
    tablep[0:10, 64:128] = selected(table[:, 48:96], out_map)


def hidden_unit(u):
    wide = 1.0 + jnp.tanh(u)
    act = (u * wide).astype(BF16)
    wide = wide.astype(BF16)
    return act, wide + act * (2.0 - wide)


def fill_windows(xaf, r2, half, count, taps_hi, taps_lo=None):
    for w in range(half):
        lanes = pl.ds(w * count, count)
        for ty in range(3):
            for tx in range(3):
                for dy in range(2):
                    er, ec = 2 * r2 + 2 * ty + dy, 2 * w + 2 * tx
                    pair = jnp.concatenate([xaf[er, ec], xaf[er, ec + 1]], axis=0)
                    high = pair.astype(BF16)
                    at = pl.ds((ty * 3 + tx) * 32 + dy * 16, 16)
                    taps_hi[at, lanes] = high
                    if taps_lo is not None:
                        taps_lo[at, lanes] = (pair - high.astype(F32)).astype(BF16)


def forward_kernel(cols, sub, images, noise, top, bottom, flags, weff, win, mixh, bias2, wout, wp, labels, others,
                   act1, sg1, act2, sg2, xa2, xt, xaf, xbf, nn, edge_top, edge_bottom, stats, hits,
                   xs, taps, acc, taps_hi, taps_lo):
    step = pl.program_id(0)
    rows, width, count = images.shape[1:]
    groups = width // cols

    @pl.when(step == 0)
    def _():
        seen = iota((16, count), 0) == jnp.broadcast_to(labels[...], (16, count))
        same = iota((16, count), 0) == jnp.broadcast_to(others[...], (16, count))
        seen = jnp.sum(as_f32(seen) + as_f32(same), axis=1, keepdims=True)
        hits[...] = jnp.broadcast_to(seen, (16, 128))
        xs[:, 0:2] = top[...].astype(F32)
        xs[:, 2 : rows + 2] = images[...] + noise[...]
        xs[:, rows + 2 : rows + 4] = bottom[...].astype(F32)
        xaf[...] = jnp.zeros_like(xaf)
        xt[...] = jnp.zeros_like(xt)
        acc[...] = jnp.zeros_like(acc)
        row8 = iota((8, count), 0)
        ones = jnp.where((iota((16, count), 0) & 7) == 6, 1.0, 0.0)
        col_a = [jnp.broadcast_to(weff[0:8, c : c + 1], (8, count)) for c in range(13)]
        col_b = [jnp.broadcast_to(weff[8:16, c : c + 1], (8, count)) for c in range(13)]

        def per_row(own, er):
            valid = jnp.where(er < 2, flags[0], jnp.where(er >= rows + 2, flags[1], 1.0))
            before = jnp.zeros((8, count), F32)
            for c in range(width):
                a, b = col_a[12], col_b[12]
                t0 = jnp.zeros((8, count), F32)
                t1 = jnp.where(row8 == 4, valid, 0.0)
                for ch in range(12):
                    x = jnp.broadcast_to(xs[ch, er, c : c + 1, :], (8, count))
                    a = a + col_a[ch] * x
                    if own:
                        b = b + col_b[ch] * x
                    if ch < 8:
                        t0 = jnp.where(row8 == ch, x, t0)
                    else:
                        t1 = jnp.where(row8 == ch - 8, x, t1)
                a = a * valid
                xaf[er, c + 2] = a
                xa2[er, c] = (jnp.concatenate([before, a], axis=0) + ones).astype(BF16)
                before = a
                xt[er, c + 1] = jnp.concatenate([t0, t1], axis=0).astype(BF16)

                if own:
                    xbf[er - 2, c] = b

            last = jnp.concatenate([before, jnp.zeros((8, count), F32)], axis=0)
            xa2[er, width] = (last + ones).astype(BF16)
            xa2[er, width + 1] = ones.astype(BF16)

        def own_row(i, carry):
            per_row(True, i + 2)
            return carry

        def other_row(i, carry):
            per_row(False, jnp.where(i < 2, i, i + rows))
            return carry

        lax.fori_loop(0, rows, own_row, 0)
        lax.fori_loop(0, 4, other_row, 0)

        def per_pair(r2, carry):
            fill_windows(xaf, r2, width // 2, count, taps_hi, taps_lo)
            main = dot(wp[:, 0:288], taps_hi[...])
            stats[r2] = main[0:64] + main[64:128] + dot(wp[0:64, 0:288], taps_lo[...])
            return carry

        lax.fori_loop(0, rows // 2, per_pair, 0)

    row = step // groups
    start = (step % groups) * cols
    for i in range(cols):
        lanes = pl.ds(i * count, count)
        for dy in range(3):
            for j in range(2):
                taps[pl.ds((dy * 2 + j) * 16, 16), lanes] = xa2[row + 1 + dy, start + i + 2 * j]
        taps[96:112, lanes] = xt[row + 2, start + i + 1]
        taps[112:128, lanes] = xt[row + 2, start + i + 1]
    size = sub * count
    for s in range(cols // sub):
        lanes = pl.ds(s * size, size)
        one, slope1 = hidden_unit(dot(win[...], taps[:, lanes]))
        act1[0, :, lanes] = one
        sg1[0, :, lanes] = slope1
        bias = jnp.concatenate([bias2[...]] * (size // 128), axis=1)
        two, slope2 = hidden_unit(dot(mixh[...], one) + bias)
        act2[0, :, lanes] = two
        sg2[0, :, lanes] = slope2
        out = dot(wout[...], two)
        for dy in range(3):
            for k in range(sub + 2):
                value = None
                for dx in range(3):
                    i = k + dx - 2
                    if 0 <= i < sub:
                        at = 16 * (dy * 3 + dx)
                        part = out[at : at + 16, i * count : (i + 1) * count]
                        value = part if value is None else value + part
                acc[row + 2 - dy, start + s * sub + k] += value

    @pl.when(step == rows * groups - 1)
    def _():
        nn[...] = acc[1 : rows + 1, 1 : width + 1]
        edge_top[...] = acc[0, 1 : width + 1].astype(BF16)
        edge_bottom[...] = acc[rows + 1, 1 : width + 1].astype(BF16)


def coupling_kernel(dims, nn, edge_top, edge_bottom, xbf, stats, labels, tablep, net_bias, *refs):
    dn, dn_first, dn_last, dstats, dxb, loss_acc, per_image, counts = refs[-8:]
    rows, width, _, count = nn.shape
    half = width // 2
    hot = as_f32(iota((16, count), 0) == jnp.broadcast_to(labels[...], (16, count)))
    number = refs[0][...]
    for ref in refs[1:-8]:
        number = number + ref[...]
    counts[...] = number
    scale16 = 1.0 / (10.0 * jnp.maximum(number, 1.0) * (dims * LOG_TWO))
    coef = jnp.sum(hot * scale16[:, 0:1], axis=0, keepdims=True)
    coef = jnp.broadcast_to(coef, (8, count))
    cls = selected(tablep[...], hot, TN)
    per_image[0:128, :] = cls
    per_image[128:136, :] = coef
    per_image[136:152, :] = hot
    bias_a = jnp.broadcast_to(net_bias[0:8, 0:1], (8, count))
    bias_b = jnp.broadcast_to(net_bias[8:16, 0:1], (8, count))
    loss = jnp.zeros((8, count), F32)
    for r2 in range(rows // 2):
        for w in range(half):
            lanes = pl.ds(w * count, count)
            for dy in range(2):
                pair = []
                for dx in range(2):
                    d = 2 * dy + dx
                    r, c = 2 * r2 + dy, 2 * w + dx
                    tile = nn[r, c]
                    if r == 0:
                        tile = tile + edge_top[c].astype(F32)
                    if r == rows - 1:
                        tile = tile + edge_bottom[c].astype(F32)
                    raw = tile[8:16] + bias_b
                    sig = 0.5 + 0.5 * jnp.tanh(0.5 * raw)
                    log_sig = jnp.minimum(raw, 0.0) - jnp.log(1.0 + jnp.exp(-jnp.abs(raw)))
                    base = xbf[r, c] + tile[0:8] + bias_a
                    logs = stats[r2, pl.ds(32 + 8 * d, 8), lanes] + cls[32 + 8 * d : 40 + 8 * d]
                    diff = base * sig - (stats[r2, pl.ds(8 * d, 8), lanes] + cls[8 * d : 8 * d + 8])
                    weighted = diff * jnp.exp(-2.0 * logs)
                    quad = diff * weighted
                    loss = loss + (log_sig - 0.5 * (LOG_TWO_PI + 2.0 * logs + quad))
                    dv = coef * weighted
                    dstats[r2, pl.ds(8 * d, 8), lanes] = -dv
                    dstats[r2, pl.ds(32 + 8 * d, 8), lanes] = coef - coef * quad
                    passed = dv * sig
                    pair.append(passed)
                    draw = (passed * base - coef) * (1.0 - sig)
                    dn[r, c] = jnp.concatenate([passed, draw], axis=0).astype(BF16)
                dxb[2 * r2 + dy, w] = jnp.concatenate(pair, axis=0).astype(BF16)
    loss_acc[...] = loss
    dn_first[...] = dn[0]
    dn_last[...] = dn[rows - 1]


def prior_kernel(dn, dstats, dxb, loss_part, xaf, xt, per_image, wpt,
                 dprior, small, taps_hi, dtaps, dxa, table_acc):
    rows, width, _, count = dn.shape
    half = width // 2
    cls = per_image[0:128, :]
    coef = per_image[128:136, :]
    hot = per_image[136:152, :]
    weight_grad = None
    for r2 in range(rows // 2):
        fill_windows(xaf, r2, half, count, taps_hi)
        grads = dstats[r2]
        high = grads.astype(BF16)
        low = (grads - high.astype(F32)).astype(BF16)
        part = dot(taps_hi[...], high, NT)
        weight_grad = part if weight_grad is None else weight_grad + part
        dtaps[r2] = dot(wpt[:, 0:192], jnp.concatenate([high, high, low], axis=0))
    dprior[...] = jnp.zeros_like(dprior)
    dprior[:, 0:64] = weight_grad
    for k in range(8):
        rows8 = pl.ds(8 * k, 8)
        value = jnp.zeros((8, count), F32)
        for r2 in range(rows // 2):
            for w in range(half):
                value = value + dstats[r2, rows8, pl.ds(w * count, count)]
        table_acc[rows8, :] = value
    gain = jnp.zeros((16, count), F32)
    loss = loss_part[...]
    means = [jnp.zeros((8, count), F32)] * 4
    scales = [jnp.zeros((8, count), F32)] * 4
    for er in range(rows + 4):
        for pair in range(half):
            both = []
            for dx in range(2):
                c = 2 * pair + dx
                value = None
                for r2 in range(rows // 2):
                    ey = er - 2 * r2
                    for w in range(half):
                        ex = c + 2 - 2 * w
                        if 0 <= ey < 6 and 0 <= ex < 6:
                            at = ((ey // 2) * 3 + ex // 2) * 32 + (ey % 2) * 16 + (ex % 2) * 8
                            part = dtaps[r2, pl.ds(at, 8), pl.ds(w * count, count)]
                            value = part if value is None else value + part
                r = er - 2
                if 0 <= r < rows:
                    d = 2 * (r % 2) + dx
                    gain = gain + dn[r, c].astype(F32)
                    logs = cls[96 + 8 * d : 104 + 8 * d]
                    diff = xaf[er, c + 2] - cls[64 + 8 * d : 72 + 8 * d]
                    weighted = diff * jnp.exp(-2.0 * logs)
                    quad = diff * weighted
                    loss = loss - 0.5 * (LOG_TWO_PI + 2.0 * logs + quad)
                    dv = coef * weighted
                    means[d] = means[d] - dv
                    scales[d] = scales[d] + (coef - coef * quad)
                    value = value + dv
                both.append(value)
            dxa[er, pair] = jnp.concatenate(both, axis=0).astype(BF16)
    for d in range(4):
        table_acc[pl.ds(64 + 8 * d, 8), :] = means[d]
        table_acc[pl.ds(96 + 8 * d, 8), :] = scales[d]
    outer = jnp.zeros((width * 8, width * 16), F32)
    inner = jnp.zeros((width * 8, width * 16), F32)
    for er in range(rows + 4):
        field = xt[er, 1 : width + 1].reshape(width * 16, count)
        outer = outer + dot(dxa[er].reshape(width * 8, count), field, NT)
        if 2 <= er < rows + 2:
            inner = inner + dot(dxb[er - 2].reshape(width * 8, count), field, NT)
    total = jnp.concatenate([outer, inner], axis=0)
    row, col = iota((256, 256), 0), iota((256, 256), 1)
    masked = jnp.where(((row & 127) >> 3) == (col >> 4), total, 0.0)
    halves = []
    for h in range(2):
        value = masked[128 * h : 128 * h + 8]
        for k in range(1, 16):
            value = value + masked[128 * h + 8 * k : 128 * h + 8 * k + 8]
        halves.append(value)
    fold = as_f32((iota((256, 128), 0) & 15) == iota((256, 128), 1))
    small[...] = jnp.zeros_like(small)
    small[:, 128:256] = selected(jnp.concatenate(halves, axis=0), fold)
    small[:, 0:128] = select(hot, table_acc[...], NT)
    spread = half_map() * jnp.sum(gain, axis=1, keepdims=True)
    small[0:8, 256:384] = jnp.broadcast_to(jnp.sum(spread, axis=0, keepdims=True), (8, 128))
    value = jnp.where(iota((8, count), 0) < 6, loss * coef, 0.0)
    value = jnp.sum(jnp.sum(value, axis=0, keepdims=True), axis=1, keepdims=True)
    small[8:16, 256:384] = jnp.broadcast_to(-value, (8, 128))


def backward_kernel(cols, sub, act1, sg1, act2, sg2, place, dn, dn_top, dn_bottom, xa2, xt, mixth, woutt, wt,
                    dprior, small, keep, send, packed, dnp, taps, gtaps, bias_acc, wfield, gout, gin, turned, turned2):
    step = pl.program_id(0)
    rows, width, _, count = dn.shape
    groups = width // cols
    hidden = mixth.shape[0]

    @pl.when(step == 0)
    def _():
        packed[...] = jnp.zeros_like(packed)
        turned2[...] = jnp.zeros_like(turned2)
        bias_acc[...] = jnp.zeros_like(bias_acc)
        turned[...] = jnp.zeros_like(turned)
        dnp[...] = jnp.zeros_like(dnp)
        dnp[0, 1 : width + 1] = dn_top[...]
        dnp[1 : rows + 1, 1 : width + 1] = dn[...]
        dnp[rows + 1, 1 : width + 1] = dn_bottom[...]
        taps[240:256, :] = jnp.zeros_like(taps[240:256, :])

    row = step // groups
    start = (step % groups) * cols
    for i in range(cols):
        lanes = pl.ds(i * count, count)
        for dy in range(3):
            for j in range(2):
                taps[pl.ds((dy * 2 + j) * 16, 16), lanes] = xa2[row + 1 + dy, start + i + 2 * j]
            for dx in range(3):
                tap = dy * 3 + dx
                taps[pl.ds(96 + tap * 16, 16), lanes] = xt[row + 1 + dy, start + i + dx]
                gtaps[pl.ds(tap * 16, 16), lanes] = dnp[row + 2 - dy, start + i + 2 - dx]
    size = sub * count
    for s in range(cols // sub):
        lanes = pl.ds(s * size, size)
        grad2 = (dot(woutt[:, 0:144], gtaps[0:144, lanes]) * sg2[0, :, lanes].astype(F32)).astype(BF16)
        grad1 = (dot(mixth[...], grad2) * sg1[0, :, lanes].astype(F32)).astype(BF16)
        wide = grad2.astype(F32)
        bias = wide[:, 0:128]
        for k in range(1, size // 128):
            bias = bias + wide[:, k * 128 : (k + 1) * 128]
        bias_acc[...] += bias
        turned2[...] += dot(act2[0, :, lanes], gtaps[0:144, lanes], NT)
        packed[ROW_MIX:ROW_OUT, :] += dot(grad2, act1[0, :, lanes], NT)
        turned[...] += dot(grad1, taps[:, lanes], NT)

    @pl.when(step == rows * groups - 1)
    def _():
        gathered = turned[...].T
        gin[...] = gathered[0:96]
        gout[...] = jnp.concatenate([turned2[...], jnp.zeros((hidden, 112), F32)], axis=1).T[0:144]
        wfield[...] = gathered[96:240]
        for tap in range(9):
            at = ROW_OUT + 12 * tap
            packed[at : at + 6, :] = gout[16 * tap : 16 * tap + 6, :]
            packed[at + 6 : at + 12, :] = gout[16 * tap + 8 : 16 * tap + 14, :]
            at = ROW_IN + 6 * tap
            from_row = (tap // 3) * 32 + (tap % 3) * 8
            packed[at : at + 6, :] = gin[from_row : from_row + 6, :]
        packed[ROW_BIAS : ROW_BIAS + 1, :] = gin[46:47, :]
        lone = jnp.ones((8, 128), F32)
        packed[ROW_BIAS + 1 : ROW_BIAS + 2, :] = select(lone, bias_acc[...], NT)[0:1]
        for k in range(4):
            packed[ROW_PRIOR:ROW_SMALL, 128 * k : 128 * k + 128] = dprior[72 * k : 72 * k + 72, :]
        packed[ROW_SMALL:ROWS, :] = small[...]
        cross = select(wt[0:96, :], wfield[...], NT)
        row, col = iota((96, 144), 0), iota((96, 144), 1)
        slot = (row >> 3) & 3
        same = (slot < 3) & ((row >> 5) * 3 + slot == col >> 4) & ((row & 7) < 6)
        fold = as_f32((iota((144, 128), 0) & 15) == iota((144, 128), 1))
        cross = jnp.where(same, cross, 0.0)
        value = cross[0:8]
        for k in range(1, 12):
            value = value + cross[8 * k : 8 * k + 8]
        field_terms = selected(value, fold)
        packed[ROW_SMALL : ROW_SMALL + 8, 128:256] += 2.0 * field_terms
        chunks, each = keep.shape[:2]
        core = place[0]
        for k in range(2 * chunks):
            block = chunk_of(packed, k, each)
            mine = core == k // chunks

            @pl.when(mine)
            def _():
                keep[k % chunks] = block

            @pl.when(jnp.logical_not(mine))
            def _():
                send[k % chunks] = to_wire(block)


def chunk_of(packed, k, each):
    plain, fine = 2 * each // 3, each // 3
    return jnp.concatenate(
        [
            packed[k * plain : (k + 1) * plain, :],
            packed[ROW_OUT + k * fine : ROW_OUT + (k + 1) * fine, :],
        ],
        axis=0,
    )


def to_wire(block):
    axis = block.ndim - 2
    each = block.shape[axis]
    plain = lax.slice_in_dim(block, 0, 2 * each // 3, axis=axis)
    fine = lax.slice_in_dim(block, 2 * each // 3, each, axis=axis)
    high = fine.astype(BF16).astype(F32)
    return jnp.concatenate([plain, high, fine - high], axis=axis).astype(BF16)


def from_wire(wire):
    axis = wire.ndim - 2
    part = wire.shape[axis] // 4
    wide = wire.astype(F32)
    fine = lax.slice_in_dim(wide, 2 * part, 3 * part, axis=axis)
    fine = fine + lax.slice_in_dim(wide, 3 * part, 4 * part, axis=axis)
    return jnp.concatenate([lax.slice_in_dim(wide, 0, 2 * part, axis=axis), fine], axis=axis)


def halve_kernel(place, keep, got, mine, *sends):
    count = len(sends) + 1
    bands = keep.shape[0] // count
    here = place[1]
    for m in range(count):
        for b in range(bands):
            at = (here ^ m) * bands + b
            value = keep[at] + from_wire(got[at])
            if m == 0:
                mine[b] = value
            else:
                sends[m - 1][b] = to_wire(value)


def spread_kernel(place, bands, first, *refs):
    gots, mine, sends = refs[:-bands], refs[-bands], refs[1 - bands :]
    here = place[2]
    for k in range(bands):
        at = lax.rem(here + k, bands)
        value = first[at]
        for got in gots:
            value = value + from_wire(got[at])
        if k == 0:
            mine[...] = value
        else:
            sends[k - 1][...] = to_wire(value)


def sum_kernel(mine, *refs):
    value = mine[...]
    for ref in refs[:-1]:
        value = value + from_wire(ref[...])
    refs[-1][...] = to_wire(value)


def gather_kernel(place, which, xor, mine, *refs):
    out = refs[-1]
    here = place[which]
    count = len(refs)
    for k in range(count):
        at = (here ^ k) if xor else lax.rem(here - k + count, count)
        out[at] = (mine if k == 0 else refs[k - 1])[...]


def adamw(weight, first, second, grad, out, out_first, out_second, at=Ellipsis):
    first_new = BETA_ONE * first[at] + (1.0 - BETA_ONE) * grad
    second_new = BETA_TWO * second[at] + (1.0 - BETA_TWO) * grad * grad
    first_hat = first_new * (1.0 / (1.0 - BETA_ONE**STEP))
    second_hat = second_new * (1.0 / (1.0 - BETA_TWO**STEP))
    out[at] = weight[at] - RATE * (
        first_hat / (jnp.sqrt(second_hat) + EPSILON) + DECAY * weight[at]
    )
    out_first[at] = first_new
    out_second[at] = second_new


def update_kernel(area, dims, *refs):
    place, own, other, counts = refs[:4]
    refs = refs[4:]
    params, firsts, seconds = refs[:8], refs[8:16], refs[16:24]
    loss, norm = refs[24:26]
    news, new_firsts, new_seconds = refs[26:34], refs[34:42], refs[42:50]
    square, strip, gin, gout, flat, kept, grads = refs[50:]
    chunks = own.shape[0]
    fine = own.shape[1] // 4
    for k in range(2 * chunks):
        mine = place[0] == k // chunks
        block = from_wire(jnp.where(mine, own[k % chunks], other[k % chunks]))
        grads[2 * k * fine : 2 * (k + 1) * fine, :] = block[0 : 2 * fine]
        grads[ROW_OUT + k * fine : ROW_OUT + (k + 1) * fine, :] = block[2 * fine :]
    bias, gains_ref, lu_ref = params[4:7]
    hidden = grads.shape[1]
    square[...] = jnp.zeros_like(square)
    square[0:12, 0:12] = lu_ref[...]
    strip[...] = jnp.zeros_like(strip)
    strip[0:3, 0:12] = gains_ref[...]
    gains = strip[...]
    lower, upper, eye = lu_factors(square[...])
    weight = spread_weight(square[...], gains)
    field = grads[ROW_SMALL:ROWS, 128:256]
    lane = iota((16, 128), 1)
    level = jnp.sum(jnp.where(lane == 12, field, 0.0), axis=1, keepdims=True)
    real = iota((16, 128), 0) & 7
    moved = jnp.where((lane < 12) & (real < 6), field + level * gains[0:1], 0.0)
    level = jnp.where(real < 6, level, 0.0)
    number = counts[...]
    present = number / jnp.maximum(number, 1.0)
    share = jnp.sum(present[:, 0:1], axis=0, keepdims=True)
    coef = share * (1.0 / (10.0 * dims * LOG_TWO)) * area
    weight = jnp.where(lane < 12, weight, 0.0)
    d_shift = jnp.sum(weight * level, axis=0, keepdims=True)
    d_scale = jnp.sum(weight * moved, axis=0, keepdims=True) - coef
    d_product = select(channel_map(), moved * jnp.exp(gains[1:2]), TN)
    d_lower = dot(d_product, upper, NT, HIGH)
    d_upper = dot(lower, d_product, TN, HIGH)
    row, col = iota((128, 128), 0), iota((128, 128), 1)
    d_lu = jnp.where(row > col, d_lower, 0.0) + jnp.where(row < col, d_upper, 0.0)
    d_lu = d_lu + jnp.where(eye, d_upper * jnp.exp(square[...]) - coef, 0.0)
    d_lu = jnp.where((row < 12) & (col < 12), d_lu, 0.0)
    diag = jnp.sum(jnp.sum(jnp.where(eye, square[...], 0.0), axis=0, keepdims=True), axis=1, keepdims=True)
    logs = jnp.sum(jnp.where(lane[0:1] < 12, gains[1:2], 0.0), axis=1, keepdims=True)
    d_bias_out = grads[ROW_SMALL : ROW_SMALL + 1, 256:384]
    row8 = iota((8, 128), 0)
    d_gains = jnp.where(row8 == 0, d_shift, jnp.where(row8 == 1, d_scale, jnp.where(row8 == 2, d_bias_out, 0.0)))
    d_gains = jnp.where(iota((8, 128), 1) < 12, d_gains, 0.0)
    for tap in range(9):
        gin[tap] = grads[ROW_IN + 6 * tap : ROW_IN + 6 * tap + 6, :]
        gout[tap] = grads[ROW_OUT + 12 * tap : ROW_OUT + 12 * tap + 12, :]
    for k in range(4):
        flat[72 * k : 72 * k + 72, :] = grads[ROW_PRIOR:ROW_SMALL, 128 * k : 128 * k + 128]
    out_map = prior_out_map()
    for k in range(36):
        kept[pl.ds((k >> 2) * 24 + (k & 3), 6, stride=4), :] = flat[8 * k : 8 * k + 6, :]
    d_prior = selected(kept[:, 0:64], out_map, NT)
    d_table = grads[ROW_SMALL:ROWS, 0:128]
    d_table = [selected(d_table[:, 0:64], out_map, NT), selected(d_table[:, 64:128], out_map, NT)]
    d_table = [part[0:10] for part in d_table]
    d_bias = [grads[ROW_BIAS : ROW_BIAS + 1, :], grads[ROW_BIAS + 1 : ROW_BIAS + 2, :]]
    d_mix = grads[0:ROW_OUT, :]

    def squares(value):
        value = value * value
        if value.ndim == 3:
            value = jnp.sum(value, axis=0)
        return jnp.sum(jnp.sum(value, axis=0, keepdims=True), axis=1, keepdims=True)

    squared = squares(d_mix) + squares(gin[...]) + squares(gout[...]) + squares(d_prior)
    squared = squared + squares(d_bias[0]) + squares(d_bias[1]) + squares(d_gains) + squares(d_lu)
    squared = squared + squares(d_table[0]) + squares(d_table[1])
    total_norm = jnp.sqrt(squared)
    factor = jnp.minimum(1.0, CLIP_NORM / (total_norm + 1e-06))
    norm[...] = total_norm
    loss[...] = (
        grads[ROW_SMALL + 8 : ROW_SMALL + 9, 256:257] - coef * (logs + diag) + BITS * share / 10.0
    )

    def put(k, grad, at=Ellipsis):
        adamw(params[k], firsts[k], seconds[k], grad, news[k], new_firsts[k], new_seconds[k], at)

    put(0, factor * gin[...])
    put(1, factor * d_mix)
    put(2, factor * gout[...])
    put(3, (factor * d_prior).reshape(9, 24, 48))
    put(4, factor * d_bias[0], (slice(0, 1), slice(None)))
    put(4, factor * d_bias[1], (slice(1, 2), slice(None)))
    put(5, (factor * d_gains)[0:3, 0:12])
    put(6, (factor * d_lu)[0:12, 0:12])
    put(7, factor * d_table[0], (slice(None), slice(0, 48)))
    put(7, factor * d_table[1], (slice(None), slice(48, 96)))


def shape(dims, dtype=F32):
    return jax.ShapeDtypeStruct(dims, dtype)


def near(dims, dtype=F32):
    return pltpu.HBM(dims, dtype)


def far(array):
    return pltpu.with_memory_space_constraint(array, pltpu.HBM)


def params_of(limit):
    return pltpu.CompilerParams(vmem_limit_bytes=limit * MIB)


def exchange_rows(up, down):
    count = lax.axis_size("band")
    before = lax.ppermute(down, "band", [(i, i + 1) for i in range(count - 1)])
    after = lax.ppermute(up, "band", [(i + 1, i) for i in range(count - 1)])
    return before, after


def body(images, noise, labels, *rest):
    params, firsts, seconds = (list(rest[8 * k : 8 * k + 8]) for k in range(3))
    for group in (params, firsts, seconds):
        group[0] = group[0].transpose(0, 2, 1)
        group[3] = group[3].transpose(0, 2, 1)
    chans, rows, width, count = images.shape
    hidden = params[1].shape[0]
    band = lax.axis_index("band")
    bands = lax.axis_size("band")
    whole = pl.BlockSpec(memory_space=pltpu.VMEM)

    top, bottom = exchange_rows(
        (images[:, :2] + noise[:, :2]).astype(BF16),
        (images[:, rows - 2 :] + noise[:, rows - 2 :]).astype(BF16),
    )
    groups_dp = lax.axis_size("dp")
    chips = groups_dp // 2

    def swap(array, mask):
        pairs = [(i, i ^ mask) for i in range(groups_dp)]
        return lax.ppermute(array, "dp", pairs)

    labels = labels[None, :]
    others = swap(labels, 1)
    flags = jnp.stack([band > 0, band < bands - 1]).astype(F32)
    dp = lax.axis_index("dp")
    place = jnp.stack([dp & 1, dp >> 1, band]).astype(jnp.int32)
    smem = pl.BlockSpec(memory_space=pltpu.SMEM)
    win, wt, mixh, mixth, bias2, wout, woutt, weff, wpt, wp, tablep, net_bias = pl.pallas_call(
        weights_kernel,
        out_shape=(
            near((hidden, 128), BF16),
            near((128, hidden)),
            near((hidden, hidden), BF16),
            near((hidden, hidden), BF16),
            near((hidden, 128)),
            near((144, hidden), BF16),
            near((hidden, 256), BF16),
            near((16, 128)),
            near((288, 256), BF16),
            near((128, 384), BF16),
            near((16, 128)),
            near((16, 128)),
        ),
        in_specs=[whole] * 8,
        out_specs=(whole,) * 12,
        scratch_shapes=[
            pltpu.VMEM((512, hidden), F32),
            pltpu.VMEM((128, 128), F32),
            pltpu.VMEM((8, 128), F32),
        ],
        compiler_params=params_of(VMEM_MIB),
        name="weights",
    )(*[far(p) for p in params])

    cols, sub = 8, 4
    pixels = (width // 2) * count
    groups = width // cols
    steps = rows * groups
    size = cols * count
    chunk = pl.BlockSpec((1, hidden, size), lambda i: (i, 0, 0))
    ext = (rows + 4, width + 2, 16, count)
    exta = (rows + 4, width + 4, 8, count)
    act1, sg1, act2, sg2, xa2, xt, xaf, xbf, nn, edge_top, edge_bottom, stats, hits = pl.pallas_call(
        functools.partial(forward_kernel, cols, sub),
        grid=(steps,),
        out_shape=(pltpu.HBM((steps, hidden, size), BF16),) * 4
        + (
            near(ext, BF16),
            near(ext, BF16),
            near(exta),
            near((rows, width, 8, count)),
            near((rows, width, 16, count)),
            near((width, 16, count), BF16),
            near((width, 16, count), BF16),
            near((rows // 2, 64, pixels)),
            shape((16, 128)),
        ),
        in_specs=[whole] * 4 + [smem] + [whole] * 8,
        out_specs=(chunk,) * 4 + (whole,) * 9,
        scratch_shapes=[
            pltpu.VMEM((chans, rows + 4, width, count), F32),
            pltpu.VMEM((128, size), BF16),
            pltpu.VMEM((rows + 2, width + 2, 16, count), F32),
            pltpu.VMEM((288, pixels), BF16),
            pltpu.VMEM((288, pixels), BF16),
        ],
        compiler_params=params_of(VMEM_MIB),
        cost_estimate=pl.CostEstimate(
            flops=2 * rows * width * count * hidden * (hidden + 272),
            transcendentals=2 * rows * width * count * hidden,
            bytes_accessed=8 * rows * width * count * hidden,
        ),
        name="forward",
    )(far(images), far(noise), top, bottom, flags, *map(far, (weff, win, mixh, bias2, wout, wp, labels)), others)

    got_top, got_bottom = exchange_rows(edge_top, edge_bottom)
    plain = (got_top.shape, hits.shape)

    def local(kernel, name, outs, scratch, *inputs):
        return pl.pallas_call(
            kernel,
            out_shape=outs,
            in_specs=[whole for _ in inputs],
            out_specs=tuple(whole for _ in outs),
            scratch_shapes=scratch,
            compiler_params=params_of(VMEM_MIB),
            name=name,
        )(*[a if a.shape in plain else far(a) for a in inputs])

    dn, dn_first, dn_last, dstats, dxb, loss_part, per_image, counts = local(
        functools.partial(coupling_kernel, 12.0 * width * width),
        "coupling",
        (
            near((rows, width, 16, count), BF16),
            near((width, 16, count), BF16),
            near((width, 16, count), BF16),
            near((rows // 2, 64, pixels)),
            near((rows, width // 2, 16, count), BF16),
            near((8, count)),
            near((152, count)),
            near((16, 128)),
        ),
        [],
        nn,
        got_top,
        got_bottom,
        xbf,
        stats,
        labels,
        tablep,
        net_bias,
        hits,
        *[swap(hits, 2 * m) for m in range(1, chips)],
    )
    dprior, small = local(
        prior_kernel,
        "prior_grads",
        (near((288, 128)), near((16, 512))),
        [
            pltpu.VMEM((288, pixels), BF16),
            pltpu.VMEM((rows // 2, 288, pixels), F32),
            pltpu.VMEM((rows + 4, width // 2, 16, count), BF16),
            pltpu.VMEM((128, count), F32),
        ],
        dn,
        dstats,
        dxb,
        loss_part,
        xaf,
        xt,
        per_image,
        wpt,
    )

    dn_top, dn_bottom = exchange_rows(dn_first, dn_last)
    both = ("dp", "band")
    devices = lax.axis_size(both)
    each = ROWS // devices
    wires = each + each // 3
    half_shape = (devices // 2, each, hidden)
    keep, send = pl.pallas_call(
        functools.partial(backward_kernel, cols, sub),
        grid=(steps,),
        out_shape=(near(half_shape), near((devices // 2, wires, hidden), BF16)),
        in_specs=[chunk] * 4 + [smem] + [whole] * 10,
        out_specs=(whole,) * 2,
        scratch_shapes=[
            pltpu.VMEM((devices * each, hidden), F32),
            pltpu.VMEM((rows + 2, width + 2, 16, count), BF16),
            pltpu.VMEM((256, size), BF16),
            pltpu.VMEM((144, size), BF16),
            pltpu.VMEM((hidden, 128), F32),
            pltpu.VMEM((144, hidden), F32),
            pltpu.VMEM((144, hidden), F32),
            pltpu.VMEM((96, hidden), F32),
            pltpu.VMEM((hidden, 256), F32),
            pltpu.VMEM((hidden, 144), F32),
        ],
        compiler_params=params_of(VMEM_MIB),
        name="backward",
    )(*map(far, (act1, sg1, act2, sg2)), place, far(dn), dn_top, dn_bottom, *map(far, (xa2, xt, mixth, woutt, wt, dprior, small)))

    def call(kernel, name, outs, *inputs):
        return pl.pallas_call(
            kernel,
            out_shape=outs,
            in_specs=[smem if a is place else whole for a in inputs],
            out_specs=jax.tree.map(lambda _: whole, outs),
            compiler_params=params_of(VMEM_MIB),
            name=name,
        )(*inputs)

    def turn(array, k):
        return lax.ppermute(array, "band", [(i, (i + k) % bands) for i in range(bands)])

    got = swap(send, 1)
    block = shape((bands, wires, hidden), BF16)
    tile = shape((wires, hidden), BF16)
    mine, *sends = call(
        halve_kernel, "halve", (shape((bands, each, hidden)),) + (block,) * (chips - 1), place, far(keep), got
    )
    gots = [swap(a, 2 * (m + 1)) for m, a in enumerate(sends)]
    mine, *sends = call(
        lambda p, *refs: spread_kernel(p, bands, *refs),
        "spread",
        (shape((each, hidden)),) + (tile,) * (bands - 1),
        place,
        mine,
        *gots,
    )
    gots = [turn(a, k + 1) for k, a in enumerate(sends)]
    mine = call(sum_kernel, "total", tile, mine, *gots)
    gots = [turn(mine, k + 1) for k in range(bands - 1)]
    mine = call(
        lambda p, *refs: gather_kernel(p, 2, False, *refs), "gather_band", block, place, mine, *gots
    )
    gots = [swap(mine, 2 * (m + 1)) for m in range(chips - 1)]
    mine = call(
        lambda p, *refs: gather_kernel(p, 1, True, *refs),
        "gather_chips",
        shape((chips,) + block.shape, BF16),
        place,
        mine,
        *gots,
    )
    mine = mine.reshape((devices // 2, wires, hidden))
    other = swap(mine, 1)

    area = float(width * width)
    results = pl.pallas_call(
        functools.partial(update_kernel, area, 12.0 * width * width),
        out_shape=(shape((1, 1)), shape((1, 1))) + tuple(shape(p.shape) for p in params) * 3,
        in_specs=[smem] + [whole] * 27,
        out_specs=(whole,) * 26,
        scratch_shapes=[
            pltpu.VMEM((128, 128), F32),
            pltpu.VMEM((8, 128), F32),
            pltpu.VMEM((9, 6, hidden), F32),
            pltpu.VMEM((9, 12, hidden), F32),
            pltpu.VMEM((288, 128), F32),
            pltpu.VMEM((216, 128), F32),
            pltpu.VMEM((devices * each, hidden), F32),
        ],
        compiler_params=params_of(VMEM_MIB),
        name="update",
    )(place, mine, other, counts, *params, *firsts, *seconds)
    outs = [results[0][0, 0], results[1][0, 0]]
    for k in range(3):
        group = list(results[2 + 8 * k : 10 + 8 * k])
        group[0] = group[0].transpose(0, 2, 1)
        group[3] = group[3].transpose(0, 2, 1)
        outs += group
    return tuple(outs)


def solution(mesh):
    field = P(None, "band", None, "dp")
    return jax.shard_map(
        body,
        mesh=mesh,
        in_specs=(field, field, P("dp")) + (P(),) * 24,
        out_specs=(P(),) * 26,
        check_vma=False,
    )
```

```python
import functools
import math

import jax
import jax.numpy as jnp
from jax import lax
from jax.experimental import pallas as pl
from jax.experimental.pallas import tpu as pltpu
from jax.sharding import PartitionSpec as P

STEP = 10
HIGH = lax.Precision.HIGHEST
LOG_TWO = math.log(2.0)
LOG_TWO_PI = math.log(2.0 * math.pi)
CLIP_NORM = 0.01
RATE = 0.05
BETA_ONE = 0.9
BETA_TWO = 0.999
EPSILON = 1e-08
DECAY = 0.01
BITS = 5.0
F32 = jnp.float32
BF16 = jnp.bfloat16
MIB = 1024 * 1024
VMEM_MIB = 46
NN = (((1,), (0,)), ((), ()))
NT = (((1,), (1,)), ((), ()))
TN = (((0,), (0,)), ((), ()))

ROW_MIX = 0
ROW_OUT = 512
ROW_IN = ROW_OUT + 108
ROW_BIAS = ROW_IN + 54
ROW_PRIOR = ROW_BIAS + 6
ROW_SMALL = ROW_PRIOR + 72
ROWS = ROW_SMALL + 16


def dot(left, right, dims=NN, precision=None):
    return lax.dot_general(left, right, dims, precision=precision, preferred_element_type=F32)


def thirds(value):
    high = value.astype(BF16)
    rest = value - high.astype(F32)
    middle = rest.astype(BF16)
    return high, middle, (rest - middle.astype(F32)).astype(BF16)


def select(left, right, dims=NN):
    left = left.astype(BF16)
    high, middle, low = (dot(left, part, dims) for part in thirds(right))
    return high + (middle + low)


def selected(left, right, dims=NN):
    right = right.astype(BF16)
    high, middle, low = (dot(part, right, dims) for part in thirds(left))
    return high + (middle + low)


def iota(shape, dim):
    return lax.broadcasted_iota(jnp.int32, shape, dim)


def as_f32(mask):
    return jnp.where(mask, 1.0, 0.0).astype(F32)


def prior_out_map():
    row, col = iota((48, 64), 0), iota((48, 64), 1)
    kind, d, c = col >> 5, (col >> 3) & 3, col & 7
    return as_f32((c < 6) & (row == kind * 24 + 4 * c + d))


def prior_in_map():
    row, col = iota((288, 216), 0), iota((288, 216), 1)
    tap, d, c = row >> 5, (row >> 3) & 3, row & 7
    return as_f32((c < 6) & (col == tap * 24 + 4 * c + d))


def channel_map():
    row, col = iota((16, 128), 0), iota((16, 128), 1)
    return as_f32(((row < 6) & (col == 11 - row)) | ((row >= 8) & (row < 14) & (col == 13 - row)))


def half_map():
    row, col = iota((16, 128), 0), iota((16, 128), 1)
    return as_f32(((row < 6) & (col == row)) | ((row >= 8) & (row < 14) & (col == row - 2)))


def lu_factors(lu):
    row, col = iota((128, 128), 0), iota((128, 128), 1)
    eye = (row == col) & (row < 12)
    lower = jnp.where(row > col, lu, 0.0) + as_f32(eye)
    upper = jnp.where(row < col, lu, 0.0) + jnp.where(eye, jnp.exp(lu), 0.0)
    return lower, upper, eye


def spread_weight(lu, gains):
    lower, upper, _ = lu_factors(lu)
    weight = select(channel_map(), dot(lower, upper, NN, HIGH))
    scaled = weight * jnp.exp(gains[1:2])
    shift = jnp.sum(scaled * gains[0:1], axis=1, keepdims=True)
    return jnp.where(iota((16, 128), 1) == 12, shift, scaled)


def weights_kernel(cin, mix, cout, prior, bias, gains, lu, table,
                   win, wt, mixh, mixth, bias2, wout, woutt, weff, wpt, wp, tablep, net_bias,
                   big, square, strip):
    hidden = mix.shape[0]
    wt[...] = jnp.zeros_like(wt)
    for dy in range(3):
        for dx in range(3):
            wt[pl.ds(dy * 32 + dx * 8, 6), :] = (
                0.5 * cin[dy * 3 + dx]
            ).astype(BF16).astype(F32)
    half = 0.5 * bias[0:1, :]
    first = half.astype(BF16).astype(F32)
    rest = half - first
    second = rest.astype(BF16).astype(F32)
    wt[46:47, :] = first
    wt[38:39, :] = second
    wt[54:55, :] = rest - second
    win[...] = wt[...].T.astype(BF16)
    mixh[...] = (0.5 * mix[...]).astype(BF16)
    mixth[...] = (0.5 * mix[...]).T.astype(BF16)
    bias2[...] = jnp.broadcast_to(0.5 * bias[1:2, :], (128, hidden)).T
    big[...] = jnp.zeros_like(big)
    for tap in range(9):
        big[pl.ds(tap * 16, 6), :] = cout[tap, 0:6, :]
        big[pl.ds(tap * 16 + 8, 6), :] = cout[tap, 6:12, :]
    wout[...] = big[0:144, :].astype(BF16)
    woutt[...] = (0.5 * big[0:256, :]).T.astype(BF16)
    square[...] = jnp.zeros_like(square)
    square[0:12, 0:12] = lu[...]
    strip[...] = jnp.zeros_like(strip)
    strip[0:3, 0:12] = gains[...]
    weff[...] = spread_weight(square[...], strip[0:8, :])
    added = select(half_map(), strip[...], NT)[:, 2:3] + as_f32(iota((16, 1), 0) >= 8) * 2.0
    net_bias[...] = jnp.broadcast_to(added, (16, 128))
    out_map = prior_out_map()
    flat = select(prior_in_map(), selected(prior[...].reshape(216, 48), out_map))
    flat_hi = flat.astype(BF16)
    flat_lo = (flat - flat_hi.astype(F32)).astype(BF16)
    wpt[...] = jnp.zeros_like(wpt)
    wpt[:, 0:64] = flat_hi
    wpt[:, 64:128] = flat_lo
    wpt[:, 128:192] = flat_hi
    big[...] = jnp.zeros_like(big)
    big[0:288, 0:64] = flat_hi.astype(F32)
    big[0:288, 64:128] = flat_lo.astype(F32)
    wp[...] = big[0:384, 0:128].T.astype(BF16)
    tablep[...] = jnp.zeros_like(tablep)
    tablep[0:10, 0:64] = selected(table[:, 0:48], out_map)
    tablep[0:10, 64:128] = selected(table[:, 48:96], out_map)


def hidden_unit(u):
    wide = 1.0 + jnp.tanh(u)
    act = (u * wide).astype(BF16)
    wide = wide.astype(BF16)
    return act, wide + act * (2.0 - wide)


def fill_windows(xaf, r2, half, count, taps_hi, taps_lo=None):
    for w in range(half):
        lanes = pl.ds(w * count, count)
        for ty in range(3):
            for tx in range(3):
                for dy in range(2):
                    er, ec = 2 * r2 + 2 * ty + dy, 2 * w + 2 * tx
                    pair = jnp.concatenate([xaf[er, ec], xaf[er, ec + 1]], axis=0)
                    high = pair.astype(BF16)
                    at = pl.ds((ty * 3 + tx) * 32 + dy * 16, 16)
                    taps_hi[at, lanes] = high
                    if taps_lo is not None:
                        taps_lo[at, lanes] = (pair - high.astype(F32)).astype(BF16)


def forward_kernel(cols, sub, images, noise, top, bottom, flags, weff, win, mixh, bias2, wout, wp, labels, others,
                   act1, sg1, act2, sg2, xa2, xt, xaf, xbf, nn, edge_top, edge_bottom, stats, hits,
                   xs, taps, acc, taps_hi, taps_lo):
    step = pl.program_id(0)
    rows, width, count = images.shape[1:]
    groups = width // cols

    @pl.when(step == 0)
    def _():
        seen = iota((16, count), 0) == jnp.broadcast_to(labels[...], (16, count))
        same = iota((16, count), 0) == jnp.broadcast_to(others[...], (16, count))
        seen = jnp.sum(as_f32(seen) + as_f32(same), axis=1, keepdims=True)
        hits[...] = jnp.broadcast_to(seen, (16, 128))
        xs[:, 0:2] = top[...].astype(F32)
        xs[:, 2 : rows + 2] = images[...] + noise[...]
        xs[:, rows + 2 : rows + 4] = bottom[...].astype(F32)
        xaf[...] = jnp.zeros_like(xaf)
        xt[...] = jnp.zeros_like(xt)
        acc[...] = jnp.zeros_like(acc)
        row8 = iota((8, count), 0)
        ones = jnp.where((iota((16, count), 0) & 7) == 6, 1.0, 0.0)
        col_a = [jnp.broadcast_to(weff[0:8, c : c + 1], (8, count)) for c in range(13)]
        col_b = [jnp.broadcast_to(weff[8:16, c : c + 1], (8, count)) for c in range(13)]

        def per_row(own, er):
            valid = jnp.where(er < 2, flags[0], jnp.where(er >= rows + 2, flags[1], 1.0))
            before = jnp.zeros((8, count), F32)
            for c in range(width):
                a, b = col_a[12], col_b[12]
                t0 = jnp.zeros((8, count), F32)
                t1 = jnp.where(row8 == 4, valid, 0.0)
                for ch in range(12):
                    x = jnp.broadcast_to(xs[ch, er, c : c + 1, :], (8, count))
                    a = a + col_a[ch] * x
                    if own:
                        b = b + col_b[ch] * x
                    if ch < 8:
                        t0 = jnp.where(row8 == ch, x, t0)
                    else:
                        t1 = jnp.where(row8 == ch - 8, x, t1)
                a = a * valid
                xaf[er, c + 2] = a
                xa2[er, c] = (jnp.concatenate([before, a], axis=0) + ones).astype(BF16)
                before = a
                xt[er, c + 1] = jnp.concatenate([t0, t1], axis=0).astype(BF16)

                if own:
                    xbf[er - 2, c] = b

            last = jnp.concatenate([before, jnp.zeros((8, count), F32)], axis=0)
            xa2[er, width] = (last + ones).astype(BF16)
            xa2[er, width + 1] = ones.astype(BF16)

        def own_row(i, carry):
            per_row(True, i + 2)
            return carry

        def other_row(i, carry):
            per_row(False, jnp.where(i < 2, i, i + rows))
            return carry

        lax.fori_loop(0, rows, own_row, 0)
        lax.fori_loop(0, 4, other_row, 0)

        def per_pair(r2, carry):
            fill_windows(xaf, r2, width // 2, count, taps_hi, taps_lo)
            main = dot(wp[:, 0:288], taps_hi[...])
            stats[r2] = main[0:64] + main[64:128] + dot(wp[0:64, 0:288], taps_lo[...])
            return carry

        lax.fori_loop(0, rows // 2, per_pair, 0)

    row = step // groups
    start = (step % groups) * cols
    for i in range(cols):
        lanes = pl.ds(i * count, count)
        for dy in range(3):
            for j in range(2):
                taps[pl.ds((dy * 2 + j) * 16, 16), lanes] = xa2[row + 1 + dy, start + i + 2 * j]
        taps[96:112, lanes] = xt[row + 2, start + i + 1]
        taps[112:128, lanes] = xt[row + 2, start + i + 1]
    size = sub * count
    for s in range(cols // sub):
        lanes = pl.ds(s * size, size)
        one, slope1 = hidden_unit(dot(win[...], taps[:, lanes]))
        act1[0, :, lanes] = one
        sg1[0, :, lanes] = slope1
        bias = jnp.concatenate([bias2[...]] * (size // 128), axis=1)
        two, slope2 = hidden_unit(dot(mixh[...], one) + bias)
        act2[0, :, lanes] = two
        sg2[0, :, lanes] = slope2
        out = dot(wout[...], two)
        for dy in range(3):
            for k in range(sub + 2):
                value = None
                for dx in range(3):
                    i = k + dx - 2
                    if 0 <= i < sub:
                        at = 16 * (dy * 3 + dx)
                        part = out[at : at + 16, i * count : (i + 1) * count]
                        value = part if value is None else value + part
                acc[row + 2 - dy, start + s * sub + k] += value

    @pl.when(step == rows * groups - 1)
    def _():
        nn[...] = acc[1 : rows + 1, 1 : width + 1]
        edge_top[...] = acc[0, 1 : width + 1].astype(BF16)
        edge_bottom[...] = acc[rows + 1, 1 : width + 1].astype(BF16)


def coupling_kernel(dims, nn, edge_top, edge_bottom, xbf, stats, labels, tablep, net_bias, *refs):
    dn, dn_first, dn_last, dstats, dxb, loss_acc, per_image, counts = refs[-8:]
    rows, width, _, count = nn.shape
    half = width // 2
    hot = as_f32(iota((16, count), 0) == jnp.broadcast_to(labels[...], (16, count)))
    number = refs[0][...]
    for ref in refs[1:-8]:
        number = number + ref[...]
    counts[...] = number
    scale16 = 1.0 / (10.0 * jnp.maximum(number, 1.0) * (dims * LOG_TWO))
    coef = jnp.sum(hot * scale16[:, 0:1], axis=0, keepdims=True)
    coef = jnp.broadcast_to(coef, (8, count))
    cls = selected(tablep[...], hot, TN)
    per_image[0:128, :] = cls
    per_image[128:136, :] = coef
    per_image[136:152, :] = hot
    bias_a = jnp.broadcast_to(net_bias[0:8, 0:1], (8, count))
    bias_b = jnp.broadcast_to(net_bias[8:16, 0:1], (8, count))
    loss = jnp.zeros((8, count), F32)
    for r2 in range(rows // 2):
        for w in range(half):
            lanes = pl.ds(w * count, count)
            for dy in range(2):
                pair = []
                for dx in range(2):
                    d = 2 * dy + dx
                    r, c = 2 * r2 + dy, 2 * w + dx
                    tile = nn[r, c]
                    if r == 0:
                        tile = tile + edge_top[c].astype(F32)
                    if r == rows - 1:
                        tile = tile + edge_bottom[c].astype(F32)
                    raw = tile[8:16] + bias_b
                    sig = 0.5 + 0.5 * jnp.tanh(0.5 * raw)
                    log_sig = jnp.minimum(raw, 0.0) - jnp.log(1.0 + jnp.exp(-jnp.abs(raw)))
                    base = xbf[r, c] + tile[0:8] + bias_a
                    logs = stats[r2, pl.ds(32 + 8 * d, 8), lanes] + cls[32 + 8 * d : 40 + 8 * d]
                    diff = base * sig - (stats[r2, pl.ds(8 * d, 8), lanes] + cls[8 * d : 8 * d + 8])
                    weighted = diff * jnp.exp(-2.0 * logs)
                    quad = diff * weighted
                    loss = loss + (log_sig - 0.5 * (LOG_TWO_PI + 2.0 * logs + quad))
                    dv = coef * weighted
                    dstats[r2, pl.ds(8 * d, 8), lanes] = -dv
                    dstats[r2, pl.ds(32 + 8 * d, 8), lanes] = coef - coef * quad
                    passed = dv * sig
                    pair.append(passed)
                    draw = (passed * base - coef) * (1.0 - sig)
                    dn[r, c] = jnp.concatenate([passed, draw], axis=0).astype(BF16)
                dxb[2 * r2 + dy, w] = jnp.concatenate(pair, axis=0).astype(BF16)
    loss_acc[...] = loss
    dn_first[...] = dn[0]
    dn_last[...] = dn[rows - 1]


def prior_kernel(dn, dstats, dxb, loss_part, xaf, xt, per_image, wpt,
                 dprior, small, taps_hi, dtaps, dxa, table_acc):
    rows, width, _, count = dn.shape
    half = width // 2
    cls = per_image[0:128, :]
    coef = per_image[128:136, :]
    hot = per_image[136:152, :]
    weight_grad = None
    for r2 in range(rows // 2):
        fill_windows(xaf, r2, half, count, taps_hi)
        grads = dstats[r2]
        high = grads.astype(BF16)
        low = (grads - high.astype(F32)).astype(BF16)
        part = dot(taps_hi[...], high, NT)
        weight_grad = part if weight_grad is None else weight_grad + part
        dtaps[r2] = dot(wpt[:, 0:192], jnp.concatenate([high, high, low], axis=0))
    dprior[...] = jnp.zeros_like(dprior)
    dprior[:, 0:64] = weight_grad
    for k in range(8):
        rows8 = pl.ds(8 * k, 8)
        value = jnp.zeros((8, count), F32)
        for r2 in range(rows // 2):
            for w in range(half):
                value = value + dstats[r2, rows8, pl.ds(w * count, count)]
        table_acc[rows8, :] = value
    gain = jnp.zeros((16, count), F32)
    loss = loss_part[...]
    means = [jnp.zeros((8, count), F32)] * 4
    scales = [jnp.zeros((8, count), F32)] * 4
    for er in range(rows + 4):
        for pair in range(half):
            both = []
            for dx in range(2):
                c = 2 * pair + dx
                value = None
                for r2 in range(rows // 2):
                    ey = er - 2 * r2
                    for w in range(half):
                        ex = c + 2 - 2 * w
                        if 0 <= ey < 6 and 0 <= ex < 6:
                            at = ((ey // 2) * 3 + ex // 2) * 32 + (ey % 2) * 16 + (ex % 2) * 8
                            part = dtaps[r2, pl.ds(at, 8), pl.ds(w * count, count)]
                            value = part if value is None else value + part
                r = er - 2
                if 0 <= r < rows:
                    d = 2 * (r % 2) + dx
                    gain = gain + dn[r, c].astype(F32)
                    logs = cls[96 + 8 * d : 104 + 8 * d]
                    diff = xaf[er, c + 2] - cls[64 + 8 * d : 72 + 8 * d]
                    weighted = diff * jnp.exp(-2.0 * logs)
                    quad = diff * weighted
                    loss = loss - 0.5 * (LOG_TWO_PI + 2.0 * logs + quad)
                    dv = coef * weighted
                    means[d] = means[d] - dv
                    scales[d] = scales[d] + (coef - coef * quad)
                    value = value + dv
                both.append(value)
            dxa[er, pair] = jnp.concatenate(both, axis=0).astype(BF16)
    for d in range(4):
        table_acc[pl.ds(64 + 8 * d, 8), :] = means[d]
        table_acc[pl.ds(96 + 8 * d, 8), :] = scales[d]
    outer = jnp.zeros((width * 8, width * 16), F32)
    inner = jnp.zeros((width * 8, width * 16), F32)
    for er in range(rows + 4):
        field = xt[er, 1 : width + 1].reshape(width * 16, count)
        outer = outer + dot(dxa[er].reshape(width * 8, count), field, NT)
        if 2 <= er < rows + 2:
            inner = inner + dot(dxb[er - 2].reshape(width * 8, count), field, NT)
    total = jnp.concatenate([outer, inner], axis=0)
    row, col = iota((256, 256), 0), iota((256, 256), 1)
    masked = jnp.where(((row & 127) >> 3) == (col >> 4), total, 0.0)
    halves = []
    for h in range(2):
        value = masked[128 * h : 128 * h + 8]
        for k in range(1, 16):
            value = value + masked[128 * h + 8 * k : 128 * h + 8 * k + 8]
        halves.append(value)
    fold = as_f32((iota((256, 128), 0) & 15) == iota((256, 128), 1))
    small[...] = jnp.zeros_like(small)
    small[:, 128:256] = selected(jnp.concatenate(halves, axis=0), fold)
    small[:, 0:128] = select(hot, table_acc[...], NT)
    spread = half_map() * jnp.sum(gain, axis=1, keepdims=True)
    small[0:8, 256:384] = jnp.broadcast_to(jnp.sum(spread, axis=0, keepdims=True), (8, 128))
    value = jnp.where(iota((8, count), 0) < 6, loss * coef, 0.0)
    value = jnp.sum(jnp.sum(value, axis=0, keepdims=True), axis=1, keepdims=True)
    small[8:16, 256:384] = jnp.broadcast_to(-value, (8, 128))


def backward_kernel(cols, sub, act1, sg1, act2, sg2, place, dn, dn_top, dn_bottom, xa2, xt, mixth, woutt, wt,
                    dprior, small, keep, send, packed, dnp, taps, gtaps, bias_acc, wfield, gout, gin, turned, turned2):
    step = pl.program_id(0)
    rows, width, _, count = dn.shape
    groups = width // cols
    hidden = mixth.shape[0]

    @pl.when(step == 0)
    def _():
        packed[...] = jnp.zeros_like(packed)
        turned2[...] = jnp.zeros_like(turned2)
        bias_acc[...] = jnp.zeros_like(bias_acc)
        turned[...] = jnp.zeros_like(turned)
        dnp[...] = jnp.zeros_like(dnp)
        dnp[0, 1 : width + 1] = dn_top[...]
        dnp[1 : rows + 1, 1 : width + 1] = dn[...]
        dnp[rows + 1, 1 : width + 1] = dn_bottom[...]
        taps[240:256, :] = jnp.zeros_like(taps[240:256, :])

    row = step // groups
    start = (step % groups) * cols
    for i in range(cols):
        lanes = pl.ds(i * count, count)
        for dy in range(3):
            for j in range(2):
                taps[pl.ds((dy * 2 + j) * 16, 16), lanes] = xa2[row + 1 + dy, start + i + 2 * j]
            for dx in range(3):
                tap = dy * 3 + dx
                taps[pl.ds(96 + tap * 16, 16), lanes] = xt[row + 1 + dy, start + i + dx]
                gtaps[pl.ds(tap * 16, 16), lanes] = dnp[row + 2 - dy, start + i + 2 - dx]
    size = sub * count
    for s in range(cols // sub):
        lanes = pl.ds(s * size, size)
        grad2 = (dot(woutt[:, 0:144], gtaps[0:144, lanes]) * sg2[0, :, lanes].astype(F32)).astype(BF16)
        grad1 = (dot(mixth[...], grad2) * sg1[0, :, lanes].astype(F32)).astype(BF16)
        wide = grad2.astype(F32)
        bias = wide[:, 0:128]
        for k in range(1, size // 128):
            bias = bias + wide[:, k * 128 : (k + 1) * 128]
        bias_acc[...] += bias
        turned2[...] += dot(act2[0, :, lanes], gtaps[0:144, lanes], NT)
        packed[ROW_MIX:ROW_OUT, :] += dot(grad2, act1[0, :, lanes], NT)
        turned[...] += dot(grad1, taps[:, lanes], NT)

    @pl.when(step == rows * groups - 1)
    def _():
        gathered = turned[...].T
        gin[...] = gathered[0:96]
        gout[...] = jnp.concatenate([turned2[...], jnp.zeros((hidden, 112), F32)], axis=1).T[0:144]
        wfield[...] = gathered[96:240]
        for tap in range(9):
            at = ROW_OUT + 12 * tap
            packed[at : at + 6, :] = gout[16 * tap : 16 * tap + 6, :]
            packed[at + 6 : at + 12, :] = gout[16 * tap + 8 : 16 * tap + 14, :]
            at = ROW_IN + 6 * tap
            from_row = (tap // 3) * 32 + (tap % 3) * 8
            packed[at : at + 6, :] = gin[from_row : from_row + 6, :]
        packed[ROW_BIAS : ROW_BIAS + 1, :] = gin[46:47, :]
        lone = jnp.ones((8, 128), F32)
        packed[ROW_BIAS + 1 : ROW_BIAS + 2, :] = select(lone, bias_acc[...], NT)[0:1]
        for k in range(4):
            packed[ROW_PRIOR:ROW_SMALL, 128 * k : 128 * k + 128] = dprior[72 * k : 72 * k + 72, :]
        packed[ROW_SMALL:ROWS, :] = small[...]
        cross = select(wt[0:96, :], wfield[...], NT)
        row, col = iota((96, 144), 0), iota((96, 144), 1)
        slot = (row >> 3) & 3
        same = (slot < 3) & ((row >> 5) * 3 + slot == col >> 4) & ((row & 7) < 6)
        fold = as_f32((iota((144, 128), 0) & 15) == iota((144, 128), 1))
        cross = jnp.where(same, cross, 0.0)
        value = cross[0:8]
        for k in range(1, 12):
            value = value + cross[8 * k : 8 * k + 8]
        field_terms = selected(value, fold)
        packed[ROW_SMALL : ROW_SMALL + 8, 128:256] += 2.0 * field_terms
        chunks, each = keep.shape[:2]
        core = place[0]
        for k in range(2 * chunks):
            block = chunk_of(packed, k, each)
            mine = core == k // chunks

            @pl.when(mine)
            def _():
                keep[k % chunks] = block

            @pl.when(jnp.logical_not(mine))
            def _():
                send[k % chunks] = to_wire(block)


def chunk_of(packed, k, each):
    plain, fine = 2 * each // 3, each // 3
    return jnp.concatenate(
        [
            packed[k * plain : (k + 1) * plain, :],
            packed[ROW_OUT + k * fine : ROW_OUT + (k + 1) * fine, :],
        ],
        axis=0,
    )


def to_wire(block):
    axis = block.ndim - 2
    each = block.shape[axis]
    plain = lax.slice_in_dim(block, 0, 2 * each // 3, axis=axis)
    fine = lax.slice_in_dim(block, 2 * each // 3, each, axis=axis)
    high = fine.astype(BF16).astype(F32)
    return jnp.concatenate([plain, high, fine - high], axis=axis).astype(BF16)


def from_wire(wire):
    axis = wire.ndim - 2
    part = wire.shape[axis] // 4
    wide = wire.astype(F32)
    fine = lax.slice_in_dim(wide, 2 * part, 3 * part, axis=axis)
    fine = fine + lax.slice_in_dim(wide, 3 * part, 4 * part, axis=axis)
    return jnp.concatenate([lax.slice_in_dim(wide, 0, 2 * part, axis=axis), fine], axis=axis)


def halve_kernel(place, keep, got, mine, *sends):
    count = len(sends) + 1
    bands = keep.shape[0] // count
    here = place[1]
    for m in range(count):
        for b in range(bands):
            at = (here ^ m) * bands + b
            value = keep[at] + from_wire(got[at])
            if m == 0:
                mine[b] = value
            else:
                sends[m - 1][b] = to_wire(value)


def spread_kernel(place, bands, first, *refs):
    gots, mine, sends = refs[:-bands], refs[-bands], refs[1 - bands :]
    here = place[2]
    for k in range(bands):
        at = lax.rem(here + k, bands)
        value = first[at]
        for got in gots:
            value = value + from_wire(got[at])
        if k == 0:
            mine[...] = value
        else:
            sends[k - 1][...] = to_wire(value)


def sum_kernel(mine, *refs):
    value = mine[...]
    for ref in refs[:-1]:
        value = value + from_wire(ref[...])
    refs[-1][...] = to_wire(value)


def gather_kernel(place, which, xor, mine, *refs):
    out = refs[-1]
    here = place[which]
    count = len(refs)
    for k in range(count):
        at = (here ^ k) if xor else lax.rem(here - k + count, count)
        out[at] = (mine if k == 0 else refs[k - 1])[...]


def adamw(weight, first, second, grad, out, out_first, out_second, at=Ellipsis):
    first_new = BETA_ONE * first[at] + (1.0 - BETA_ONE) * grad
    second_new = BETA_TWO * second[at] + (1.0 - BETA_TWO) * grad * grad
    first_hat = first_new * (1.0 / (1.0 - BETA_ONE**STEP))
    second_hat = second_new * (1.0 / (1.0 - BETA_TWO**STEP))
    out[at] = weight[at] - RATE * (
        first_hat / (jnp.sqrt(second_hat) + EPSILON) + DECAY * weight[at]
    )
    out_first[at] = first_new
    out_second[at] = second_new


def update_kernel(area, dims, *refs):
    place, own, other, counts = refs[:4]
    refs = refs[4:]
    params, firsts, seconds = refs[:8], refs[8:16], refs[16:24]
    loss, norm = refs[24:26]
    news, new_firsts, new_seconds = refs[26:34], refs[34:42], refs[42:50]
    square, strip, gin, gout, flat, kept, grads = refs[50:]
    chunks = own.shape[0]
    fine = own.shape[1] // 4
    for k in range(2 * chunks):
        mine = place[0] == k // chunks
        block = from_wire(jnp.where(mine, own[k % chunks], other[k % chunks]))
        grads[2 * k * fine : 2 * (k + 1) * fine, :] = block[0 : 2 * fine]
        grads[ROW_OUT + k * fine : ROW_OUT + (k + 1) * fine, :] = block[2 * fine :]
    bias, gains_ref, lu_ref = params[4:7]
    hidden = grads.shape[1]
    square[...] = jnp.zeros_like(square)
    square[0:12, 0:12] = lu_ref[...]
    strip[...] = jnp.zeros_like(strip)
    strip[0:3, 0:12] = gains_ref[...]
    gains = strip[...]
    lower, upper, eye = lu_factors(square[...])
    weight = spread_weight(square[...], gains)
    field = grads[ROW_SMALL:ROWS, 128:256]
    lane = iota((16, 128), 1)
    level = jnp.sum(jnp.where(lane == 12, field, 0.0), axis=1, keepdims=True)
    real = iota((16, 128), 0) & 7
    moved = jnp.where((lane < 12) & (real < 6), field + level * gains[0:1], 0.0)
    level = jnp.where(real < 6, level, 0.0)
    number = counts[...]
    present = number / jnp.maximum(number, 1.0)
    share = jnp.sum(present[:, 0:1], axis=0, keepdims=True)
    coef = share * (1.0 / (10.0 * dims * LOG_TWO)) * area
    weight = jnp.where(lane < 12, weight, 0.0)
    d_shift = jnp.sum(weight * level, axis=0, keepdims=True)
    d_scale = jnp.sum(weight * moved, axis=0, keepdims=True) - coef
    d_product = select(channel_map(), moved * jnp.exp(gains[1:2]), TN)
    d_lower = dot(d_product, upper, NT, HIGH)
    d_upper = dot(lower, d_product, TN, HIGH)
    row, col = iota((128, 128), 0), iota((128, 128), 1)
    d_lu = jnp.where(row > col, d_lower, 0.0) + jnp.where(row < col, d_upper, 0.0)
    d_lu = d_lu + jnp.where(eye, d_upper * jnp.exp(square[...]) - coef, 0.0)
    d_lu = jnp.where((row < 12) & (col < 12), d_lu, 0.0)
    diag = jnp.sum(jnp.sum(jnp.where(eye, square[...], 0.0), axis=0, keepdims=True), axis=1, keepdims=True)
    logs = jnp.sum(jnp.where(lane[0:1] < 12, gains[1:2], 0.0), axis=1, keepdims=True)
    d_bias_out = grads[ROW_SMALL : ROW_SMALL + 1, 256:384]
    row8 = iota((8, 128), 0)
    d_gains = jnp.where(row8 == 0, d_shift, jnp.where(row8 == 1, d_scale, jnp.where(row8 == 2, d_bias_out, 0.0)))
    d_gains = jnp.where(iota((8, 128), 1) < 12, d_gains, 0.0)
    for tap in range(9):
        gin[tap] = grads[ROW_IN + 6 * tap : ROW_IN + 6 * tap + 6, :]
        gout[tap] = grads[ROW_OUT + 12 * tap : ROW_OUT + 12 * tap + 12, :]
    for k in range(4):
        flat[72 * k : 72 * k + 72, :] = grads[ROW_PRIOR:ROW_SMALL, 128 * k : 128 * k + 128]
    out_map = prior_out_map()
    for k in range(36):
        kept[pl.ds((k >> 2) * 24 + (k & 3), 6, stride=4), :] = flat[8 * k : 8 * k + 6, :]
    d_prior = selected(kept[:, 0:64], out_map, NT)
    d_table = grads[ROW_SMALL:ROWS, 0:128]
    d_table = [selected(d_table[:, 0:64], out_map, NT), selected(d_table[:, 64:128], out_map, NT)]
    d_table = [part[0:10] for part in d_table]
    d_bias = [grads[ROW_BIAS : ROW_BIAS + 1, :], grads[ROW_BIAS + 1 : ROW_BIAS + 2, :]]
    d_mix = grads[0:ROW_OUT, :]

    def squares(value):
        value = value * value
        if value.ndim == 3:
            value = jnp.sum(value, axis=0)
        return jnp.sum(jnp.sum(value, axis=0, keepdims=True), axis=1, keepdims=True)

    squared = squares(d_mix) + squares(gin[...]) + squares(gout[...]) + squares(d_prior)
    squared = squared + squares(d_bias[0]) + squares(d_bias[1]) + squares(d_gains) + squares(d_lu)
    squared = squared + squares(d_table[0]) + squares(d_table[1])
    total_norm = jnp.sqrt(squared)
    factor = jnp.minimum(1.0, CLIP_NORM / (total_norm + 1e-06))
    norm[...] = total_norm
    loss[...] = (
        grads[ROW_SMALL + 8 : ROW_SMALL + 9, 256:257] - coef * (logs + diag) + BITS * share / 10.0
    )

    def put(k, grad, at=Ellipsis):
        adamw(params[k], firsts[k], seconds[k], grad, news[k], new_firsts[k], new_seconds[k], at)

    put(0, factor * gin[...])
    put(1, factor * d_mix)
    put(2, factor * gout[...])
    put(3, (factor * d_prior).reshape(9, 24, 48))
    put(4, factor * d_bias[0], (slice(0, 1), slice(None)))
    put(4, factor * d_bias[1], (slice(1, 2), slice(None)))
    put(5, (factor * d_gains)[0:3, 0:12])
    put(6, (factor * d_lu)[0:12, 0:12])
    put(7, factor * d_table[0], (slice(None), slice(0, 48)))
    put(7, factor * d_table[1], (slice(None), slice(48, 96)))


def shape(dims, dtype=F32):
    return jax.ShapeDtypeStruct(dims, dtype)


def near(dims, dtype=F32):
    return pltpu.HBM(dims, dtype)


def far(array):
    return pltpu.with_memory_space_constraint(array, pltpu.HBM)


def params_of(limit):
    return pltpu.CompilerParams(vmem_limit_bytes=limit * MIB)


def exchange_rows(up, down):
    count = lax.axis_size("band")
    before = lax.ppermute(down, "band", [(i, i + 1) for i in range(count - 1)])
    after = lax.ppermute(up, "band", [(i + 1, i) for i in range(count - 1)])
    return before, after


def body(images, noise, labels, *rest):
    params, firsts, seconds = (list(rest[8 * k : 8 * k + 8]) for k in range(3))
    for group in (params, firsts, seconds):
        group[0] = group[0].transpose(0, 2, 1)
        group[3] = group[3].transpose(0, 2, 1)
    chans, rows, width, count = images.shape
    hidden = params[1].shape[0]
    band = lax.axis_index("band")
    bands = lax.axis_size("band")
    whole = pl.BlockSpec(memory_space=pltpu.VMEM)

    top, bottom = exchange_rows(
        (images[:, :2] + noise[:, :2]).astype(BF16),
        (images[:, rows - 2 :] + noise[:, rows - 2 :]).astype(BF16),
    )
    groups_dp = lax.axis_size("dp")
    chips = groups_dp // 2

    def swap(array, mask):
        pairs = [(i, i ^ mask) for i in range(groups_dp)]
        return lax.ppermute(array, "dp", pairs)

    labels = labels[None, :]
    others = swap(labels, 1)
    flags = jnp.stack([band > 0, band < bands - 1]).astype(F32)
    dp = lax.axis_index("dp")
    place = jnp.stack([dp & 1, dp >> 1, band]).astype(jnp.int32)
    smem = pl.BlockSpec(memory_space=pltpu.SMEM)
    win, wt, mixh, mixth, bias2, wout, woutt, weff, wpt, wp, tablep, net_bias = pl.pallas_call(
        weights_kernel,
        out_shape=(
            near((hidden, 128), BF16),
            near((128, hidden)),
            near((hidden, hidden), BF16),
            near((hidden, hidden), BF16),
            near((hidden, 128)),
            near((144, hidden), BF16),
            near((hidden, 256), BF16),
            near((16, 128)),
            near((288, 256), BF16),
            near((128, 384), BF16),
            near((16, 128)),
            near((16, 128)),
        ),
        in_specs=[whole] * 8,
        out_specs=(whole,) * 12,
        scratch_shapes=[
            pltpu.VMEM((512, hidden), F32),
            pltpu.VMEM((128, 128), F32),
            pltpu.VMEM((8, 128), F32),
        ],
        compiler_params=params_of(VMEM_MIB),
        name="weights",
    )(*[far(p) for p in params])

    cols, sub = 8, 4
    pixels = (width // 2) * count
    groups = width // cols
    steps = rows * groups
    size = cols * count
    chunk = pl.BlockSpec((1, hidden, size), lambda i: (i, 0, 0))
    ext = (rows + 4, width + 2, 16, count)
    exta = (rows + 4, width + 4, 8, count)
    act1, sg1, act2, sg2, xa2, xt, xaf, xbf, nn, edge_top, edge_bottom, stats, hits = pl.pallas_call(
        functools.partial(forward_kernel, cols, sub),
        grid=(steps,),
        out_shape=(pltpu.HBM((steps, hidden, size), BF16),) * 4
        + (
            near(ext, BF16),
            near(ext, BF16),
            near(exta),
            near((rows, width, 8, count)),
            near((rows, width, 16, count)),
            near((width, 16, count), BF16),
            near((width, 16, count), BF16),
            near((rows // 2, 64, pixels)),
            shape((16, 128)),
        ),
        in_specs=[whole] * 4 + [smem] + [whole] * 8,
        out_specs=(chunk,) * 4 + (whole,) * 9,
        scratch_shapes=[
            pltpu.VMEM((chans, rows + 4, width, count), F32),
            pltpu.VMEM((128, size), BF16),
            pltpu.VMEM((rows + 2, width + 2, 16, count), F32),
            pltpu.VMEM((288, pixels), BF16),
            pltpu.VMEM((288, pixels), BF16),
        ],
        compiler_params=params_of(VMEM_MIB),
        cost_estimate=pl.CostEstimate(
            flops=2 * rows * width * count * hidden * (hidden + 272),
            transcendentals=2 * rows * width * count * hidden,
            bytes_accessed=8 * rows * width * count * hidden,
        ),
        name="forward",
    )(far(images), far(noise), top, bottom, flags, *map(far, (weff, win, mixh, bias2, wout, wp, labels)), others)

    got_top, got_bottom = exchange_rows(edge_top, edge_bottom)
    plain = (got_top.shape, hits.shape)

    def local(kernel, name, outs, scratch, *inputs):
        return pl.pallas_call(
            kernel,
            out_shape=outs,
            in_specs=[whole for _ in inputs],
            out_specs=tuple(whole for _ in outs),
            scratch_shapes=scratch,
            compiler_params=params_of(VMEM_MIB),
            name=name,
        )(*[a if a.shape in plain else far(a) for a in inputs])

    dn, dn_first, dn_last, dstats, dxb, loss_part, per_image, counts = local(
        functools.partial(coupling_kernel, 12.0 * width * width),
        "coupling",
        (
            near((rows, width, 16, count), BF16),
            near((width, 16, count), BF16),
            near((width, 16, count), BF16),
            near((rows // 2, 64, pixels)),
            near((rows, width // 2, 16, count), BF16),
            near((8, count)),
            near((152, count)),
            near((16, 128)),
        ),
        [],
        nn,
        got_top,
        got_bottom,
        xbf,
        stats,
        labels,
        tablep,
        net_bias,
        hits,
        *[swap(hits, 2 * m) for m in range(1, chips)],
    )
    dprior, small = local(
        prior_kernel,
        "prior_grads",
        (near((288, 128)), near((16, 512))),
        [
            pltpu.VMEM((288, pixels), BF16),
            pltpu.VMEM((rows // 2, 288, pixels), F32),
            pltpu.VMEM((rows + 4, width // 2, 16, count), BF16),
            pltpu.VMEM((128, count), F32),
        ],
        dn,
        dstats,
        dxb,
        loss_part,
        xaf,
        xt,
        per_image,
        wpt,
    )

    dn_top, dn_bottom = exchange_rows(dn_first, dn_last)
    both = ("dp", "band")
    devices = lax.axis_size(both)
    each = ROWS // devices
    wires = each + each // 3
    half_shape = (devices // 2, each, hidden)
    keep, send = pl.pallas_call(
        functools.partial(backward_kernel, cols, sub),
        grid=(steps,),
        out_shape=(pltpu.VMEM(half_shape, F32), pltpu.VMEM((devices // 2, wires, hidden), BF16)),
        in_specs=[chunk] * 4 + [smem] + [whole] * 10,
        out_specs=(whole,) * 2,
        scratch_shapes=[
            pltpu.VMEM((devices * each, hidden), F32),
            pltpu.VMEM((rows + 2, width + 2, 16, count), BF16),
            pltpu.VMEM((256, size), BF16),
            pltpu.VMEM((144, size), BF16),
            pltpu.VMEM((hidden, 128), F32),
            pltpu.VMEM((144, hidden), F32),
            pltpu.VMEM((144, hidden), F32),
            pltpu.VMEM((96, hidden), F32),
            pltpu.VMEM((hidden, 256), F32),
            pltpu.VMEM((hidden, 144), F32),
        ],
        compiler_params=params_of(VMEM_MIB),
        name="backward",
    )(*map(far, (act1, sg1, act2, sg2)), place, far(dn), dn_top, dn_bottom, *map(far, (xa2, xt, mixth, woutt, wt, dprior, small)))

    def call(kernel, name, outs, *inputs):
        return pl.pallas_call(
            kernel,
            out_shape=outs,
            in_specs=[smem if a is place else whole for a in inputs],
            out_specs=jax.tree.map(lambda _: whole, outs),
            compiler_params=params_of(VMEM_MIB),
            name=name,
        )(*inputs)

    def turn(array, k):
        return lax.ppermute(array, "band", [(i, (i + k) % bands) for i in range(bands)])

    got = swap(send, 1)
    block = shape((bands, wires, hidden), BF16)
    tile = shape((wires, hidden), BF16)
    mine, *sends = call(
        halve_kernel, "halve", (shape((bands, each, hidden)),) + (block,) * (chips - 1), place, keep, got
    )
    gots = [swap(a, 2 * (m + 1)) for m, a in enumerate(sends)]
    mine, *sends = call(
        lambda p, *refs: spread_kernel(p, bands, *refs),
        "spread",
        (shape((each, hidden)),) + (tile,) * (bands - 1),
        place,
        mine,
        *gots,
    )
    gots = [turn(a, k + 1) for k, a in enumerate(sends)]
    mine = call(sum_kernel, "total", tile, mine, *gots)
    gots = [turn(mine, k + 1) for k in range(bands - 1)]
    mine = call(
        lambda p, *refs: gather_kernel(p, 2, False, *refs), "gather_band", block, place, mine, *gots
    )
    gots = [swap(mine, 2 * (m + 1)) for m in range(chips - 1)]
    mine = call(
        lambda p, *refs: gather_kernel(p, 1, True, *refs),
        "gather_chips",
        shape((chips,) + block.shape, BF16),
        place,
        mine,
        *gots,
    )
    mine = mine.reshape((devices // 2, wires, hidden))
    other = swap(mine, 1)

    area = float(width * width)
    results = pl.pallas_call(
        functools.partial(update_kernel, area, 12.0 * width * width),
        out_shape=(shape((1, 1)), shape((1, 1))) + tuple(shape(p.shape) for p in params) * 3,
        in_specs=[smem] + [whole] * 27,
        out_specs=(whole,) * 26,
        scratch_shapes=[
            pltpu.VMEM((128, 128), F32),
            pltpu.VMEM((8, 128), F32),
            pltpu.VMEM((9, 6, hidden), F32),
            pltpu.VMEM((9, 12, hidden), F32),
            pltpu.VMEM((288, 128), F32),
            pltpu.VMEM((216, 128), F32),
            pltpu.VMEM((devices * each, hidden), F32),
        ],
        compiler_params=params_of(VMEM_MIB),
        name="update",
    )(place, mine, other, counts, *params, *firsts, *seconds)
    outs = [results[0][0, 0], results[1][0, 0]]
    for k in range(3):
        group = list(results[2 + 8 * k : 10 + 8 * k])
        group[0] = group[0].transpose(0, 2, 1)
        group[3] = group[3].transpose(0, 2, 1)
        outs += group
    return tuple(outs)


def solution(mesh):
    field = P(None, "band", None, "dp")
    return jax.shard_map(
        body,
        mesh=mesh,
        in_specs=(field, field, P("dp")) + (P(),) * 24,
        out_specs=(P(),) * 26,
        check_vma=False,
    )
```
